128 devices in a mesh: grp: 2 (over y_hi), fsdp: 64 (over y_lo, z, x, core).
Axes of the slice: x: 4, y: 4 (y_hi: 2, y_lo: 2; y = y_hi * 2 + y_lo), z: 4, core: 2. Of those that a mesh axis runs over, the one named last changes fastest.
Arguments:
- tokens: bfloat16 [2, 2, 8192, 1024], P('grp', None, 'fsdp'), may hold values from -6 to 6
- cotangent: bfloat16 [2, 2, 8192, 1024], P('grp', None, 'fsdp'), may hold values from -6 to 6
- lengths: int32 [2, 4], P('grp'), may hold values from 1024 to 2048, as said below
- attn_weight: float32 [4, 1024, 1024], P(None, 'fsdp')
- up_weight: float32 [1024, 4096], P('fsdp'), may hold values from -0.1875 to 0.1875
- down_weight: float32 [4096, 1024], P('fsdp'), may hold values from -0.09375 to 0.09375
- state_param: float32 [3, 1024, 16], P(None, 'fsdp')
- norm_gain: float32 [2, 1024], P(None, 'fsdp')
- attn_first: float32 [4, 1024, 1024], P(None, 'fsdp'), may hold values from -0.0008544922 to 0.0008544922
- attn_second: float32 [4, 1024, 1024], P(None, 'fsdp'), may hold values from 1.9787699e-08 to 7.9150794e-08
- up_first: float32 [1024, 4096], P('fsdp'), may hold values from -0.0008544922 to 0.0008544922
- up_second: float32 [1024, 4096], P('fsdp'), may hold values from 1.9787699e-08 to 7.9150794e-08
- down_first: float32 [4096, 1024], P('fsdp'), may hold values from -0.0008544922 to 0.0008544922
- down_second: float32 [4096, 1024], P('fsdp'), may hold values from 1.9787699e-08 to 7.9150794e-08
- state_first: float32 [3, 1024, 16], P(None, 'fsdp'), may hold values from -0.0008544922 to 0.0008544922
- state_second: float32 [3, 1024, 16], P(None, 'fsdp'), may hold values from 1.9787699e-08 to 7.9150794e-08
- gain_first: float32 [2, 1024], P(None, 'fsdp'), may hold values from -0.0008544922 to 0.0008544922
- gain_second: float32 [2, 1024], P(None, 'fsdp'), may hold values from 1.9787699e-08 to 7.9150794e-08
Outputs:
- output: bfloat16 [2, 2, 8192, 1024], P('grp', None, 'fsdp')
- token_grad: bfloat16 [2, 2, 8192, 1024], P('grp', None, 'fsdp')
- grad_norm: float32 [], replicated
- attn_moment: float32 [4, 1024, 1024], P(None, 'fsdp')
- attn_square: float32 [4, 1024, 1024], P(None, 'fsdp')
- attn_master: float32 [4, 1024, 1024], P(None, 'fsdp')
- attn_copy: bfloat16 [4, 1024, 1024], P(None, 'fsdp')
- up_moment: float32 [1024, 4096], P('fsdp')
- up_square: float32 [1024, 4096], P('fsdp')
- up_master: float32 [1024, 4096], P('fsdp')
- up_copy: bfloat16 [1024, 4096], P('fsdp')
- down_moment: float32 [4096, 1024], P('fsdp')
- down_square: float32 [4096, 1024], P('fsdp')
- down_master: float32 [4096, 1024], P('fsdp')
- down_copy: bfloat16 [4096, 1024], P('fsdp')
- state_moment: float32 [3, 1024, 16], P(None, 'fsdp')
- state_square: float32 [3, 1024, 16], P(None, 'fsdp')
- state_master: float32 [3, 1024, 16], P(None, 'fsdp')
- state_copy: bfloat16 [3, 1024, 16], P(None, 'fsdp')
- gain_moment: float32 [2, 1024], P(None, 'fsdp')
- gain_square: float32 [2, 1024], P(None, 'fsdp')
- gain_master: float32 [2, 1024], P(None, 'fsdp')
- gain_copy: bfloat16 [2, 1024], P(None, 'fsdp')
The draws below stay inside these ranges and needn't reach their ends.
Inputs may be any that keep to these rules, and one draw needn't show every extreme that they name: Slot j of lane 1 holds lengths[g, j] valid positions from its start, the rest padding; in each group some sequence fills its slot.
All inputs are finite; a program needn't handle non-finite values.
Results may differ from the reference program's by a relative error of at most 0.03.
Values may be sent and summed in bfloat16 or wider, within the bound.
No kernel may reach another device: no remote copies, remote signals or barrier semaphores. Data moves between devices by JAX's collectives and lax.ppermute only.
A program may use at most 448 MiB of HBM per device.

```python
import jax
import jax.numpy as jnp
from jax import lax

D = 1024
HEADS = 8
HEAD_DIM = 128
FF = 4096
NSTATE = 16
BLOCK = 512
STEP = 5
LANE = 8192
SLOT = 2048
SLOTS = 4
PARAMS = 12634112
N_GRP = 2


def draw_lengths(key, part):
    key = jax.random.fold_in(key, 11)
    first, second = jax.random.split(key)
    drawn = jax.random.randint(first, (N_GRP, SLOTS), SLOT // 2, SLOT + 1)
    chosen = jax.random.randint(second, (N_GRP, 1), 0, SLOTS)
    places = jnp.arange(SLOTS, dtype=jnp.int32)[None, :]
    return jnp.where(places == chosen, SLOT, drawn).astype(jnp.int32)


def draw_attn_weight(key, part):
    key = jax.random.fold_in(key, 23)
    scales = jnp.array([2.0, 1.0, 1.0, 2.8], jnp.float32) / jnp.sqrt(jnp.float32(D))
    return jax.random.normal(key, (4, D, D), jnp.float32) * scales[:, None, None]


def draw_state_param(key, part):
    key = jax.random.fold_in(key, 37)
    pick, slow_key, fast_key, input_key, output_key = jax.random.split(key, 5)
    share = 0.5
    slow = jax.random.bernoulli(pick, share, (D, NSTATE))
    chain = jnp.float32(LANE)
    width = jnp.float32(BLOCK)
    slow_log = jax.random.uniform(slow_key, (D, NSTATE), jnp.float32, jnp.log(0.2 * width / chain), jnp.log(2.0 * width / chain))
    fast_log = jax.random.uniform(fast_key, (D, NSTATE), jnp.float32, jnp.log(width / 50.0), jnp.log(width / 20.0))
    log_rate = jnp.where(slow, slow_log, fast_log)
    input_coef = jax.random.normal(input_key, (D, NSTATE), jnp.float32)
    output_coef = jax.random.normal(output_key, (D, NSTATE), jnp.float32) / jnp.sqrt(jnp.float32(NSTATE))
    return jnp.stack([log_rate, input_coef, output_coef])


def draw_norm_gain(key, part):
    key = jax.random.fold_in(key, 41)
    low_end, high_end = (0.6, 1.8)
    ramp = low_end + (high_end - low_end) * jnp.arange(D, dtype=jnp.float32) / (D - 1)
    noise = 1.0 + 0.1 * jax.random.normal(key, (2, D), jnp.float32)
    return ramp[None, :] * noise


def levels(key, extent, cuts, low, top_value):
    def one(position, blocks):
        heights = jax.random.uniform(jax.random.fold_in(jax.random.fold_in(key, 6), position), (blocks,), jnp.float32, low / len(cuts), top_value / len(cuts))
        return jnp.repeat(jnp.exp(heights), extent[position] // blocks).reshape((-1,) + (1,) * (len(extent) - position - 1))

    level = one(*cuts[0])
    for cut in cuts[1:]:
        level = level * one(*cut)
    return level


def gaussian(own_key, dims, spread, reach, cuts=(), held_as=jnp.bfloat16):
    level = levels(own_key, dims, cuts, -0.22, 0.18) if cuts else 1.0
    values = jax.random.normal(own_key, dims, jnp.float32) * spread * level
    return jnp.minimum(jnp.maximum(values, -reach), reach).astype(held_as)


def setup_inputs(seed: int = 0) -> dict:
    splits = jax.random.split(jax.random.key(seed), 19)
    return {
        "tokens": gaussian(splits[0], (N_GRP, 2, LANE, D), 1.0, 6.0, ((0, 2), (2, 64))),
        "cotangent": gaussian(splits[1], (N_GRP, 2, LANE, D), 1.0, 6.0, ((0, 2), (2, 64))),
        "lengths": draw_lengths(jax.random.fold_in(splits[18], 71), 0),
        "attn_weight": draw_attn_weight(jax.random.fold_in(splits[18], 71), 0),
        "up_weight": gaussian(splits[4], (D, FF), D ** -0.5, 0.1875, ((0, 64),), jnp.float32),
        "down_weight": gaussian(splits[5], (FF, D), FF ** -0.5, 0.09375, ((0, 64),), jnp.float32),
        "state_param": draw_state_param(jax.random.fold_in(splits[18], 71), 0),
        "norm_gain": draw_norm_gain(jax.random.fold_in(splits[18], 71), 0),
        "attn_first": gaussian(splits[8], (4, D, D), (0.5 / PARAMS ** 0.5), 0.0008544922, ((1, 64),), jnp.float32),
        "attn_second": jnp.clip(1.978769859078966e-08 + 5.936309577236898e-08 * jax.random.uniform(splits[9], (4, D, D), jnp.float32) ** levels(splits[9], (4, D, D), ((1, 64),), -0.2, 0.2), 1.978769859078966e-08, 7.915079436315864e-08),
        "up_first": gaussian(splits[10], (D, FF), (0.5 / PARAMS ** 0.5), 0.0008544922, ((0, 64),), jnp.float32),
        "up_second": jnp.clip(1.978769859078966e-08 + 5.936309577236898e-08 * jax.random.uniform(splits[11], (D, FF), jnp.float32) ** levels(splits[11], (D, FF), ((0, 64),), -0.2, 0.2), 1.978769859078966e-08, 7.915079436315864e-08),
        "down_first": gaussian(splits[12], (FF, D), (0.5 / PARAMS ** 0.5), 0.0008544922, ((0, 64),), jnp.float32),
        "down_second": jnp.clip(1.978769859078966e-08 + 5.936309577236898e-08 * jax.random.uniform(splits[13], (FF, D), jnp.float32) ** levels(splits[13], (FF, D), ((0, 64),), -0.2, 0.2), 1.978769859078966e-08, 7.915079436315864e-08),
        "state_first": gaussian(splits[14], (3, D, NSTATE), (0.5 / PARAMS ** 0.5), 0.0008544922, ((1, 64),), jnp.float32),
        "state_second": jnp.clip(1.978769859078966e-08 + 5.936309577236898e-08 * jax.random.uniform(splits[15], (3, D, NSTATE), jnp.float32) ** levels(splits[15], (3, D, NSTATE), ((1, 64),), -0.2, 0.2), 1.978769859078966e-08, 7.915079436315864e-08),
        "gain_first": gaussian(splits[16], (2, D), (0.5 / PARAMS ** 0.5), 0.0008544922, ((1, 64),), jnp.float32),
        "gain_second": jnp.clip(1.978769859078966e-08 + 5.936309577236898e-08 * jax.random.uniform(splits[17], (2, D), jnp.float32) ** levels(splits[17], (2, D), ((1, 64),), -0.2, 0.2), 1.978769859078966e-08, 7.915079436315864e-08),
    }


EPS_NORM = 1e-05
BETA_ONE = 0.5
BETA_TWO = 0.5
ADAM_EPS = 1e-08
WEIGHT_DECAY = 0.1
CLIP_NORM = 0.5
RATE_MATRIX = 0.02
RATE_STATE = 1.0
RATE_GAIN = 0.6
HIGH = lax.Precision.HIGHEST
MASKED = -1e+30

@jax.custom_vjp
def low(v):
    return lax.optimization_barrier(v.astype(jnp.bfloat16)).astype(jnp.float32)

@jax.custom_vjp
def low_back(v):
    return v

def low_keep(v):
    return (low(v), None)

def low_pass(kept, grad):
    return (grad,)

def back_keep(v):
    return (v, None)

def back_low(kept, grad):
    return (low(grad),)
low.defvjp(low_keep, low_pass)
low_back.defvjp(back_keep, back_low)

def rms_norm(value, gain):
    return value * lax.rsqrt(lax.optimization_barrier(jnp.mean(value * value, axis=-1, keepdims=True)) + EPS_NORM) * gain

def state_block(state, inputs, keeps, decay, bvec, cvec):

    def advance(carry, item):
        row, keep_row = item
        carry = decay * keep_row * carry + bvec * row[:, None]
        return (carry, lax.optimization_barrier(jnp.sum(cvec * carry, axis=1)))
    return lax.scan(advance, state, (inputs, keeps))

def state_space(inputs, keeps, decay, bvec, cvec):
    blocked = jax.checkpoint(state_block)

    def outer(carry, item):
        return blocked(carry, item[0], item[1], decay, bvec, cvec)
    length = inputs.shape[0]
    start = jnp.zeros(decay.shape, jnp.float32)
    final, outputs = lax.scan(outer, start, (inputs.reshape(length // BLOCK, BLOCK, -1), keeps.reshape(length // BLOCK, BLOCK)))
    return outputs.reshape(length, -1)

def block_attention(query, key, value):
    size = query.shape[0]
    query_h = query.reshape(size, HEADS, HEAD_DIM)
    key_h = key.reshape(size, HEADS, HEAD_DIM)
    value_h = value.reshape(size, HEADS, HEAD_DIM)
    scores = low_back(jnp.einsum('qhd,khd->hqk', query_h, key_h, precision=HIGH) * HEAD_DIM ** (-0.5))
    rows_at = lax.broadcasted_iota(jnp.int32, (size, size), 0)
    cols_at = lax.broadcasted_iota(jnp.int32, (size, size), 1)
    scores = jnp.where(cols_at <= rows_at, scores, MASKED)
    top = lax.optimization_barrier(jnp.max(scores, axis=-1, keepdims=True))
    weights = jnp.exp(scores - top)
    probs = low(weights / lax.optimization_barrier(jnp.sum(weights, axis=-1, keepdims=True)))
    mixed = jnp.einsum('hqk,khd->qhd', probs, value_h, precision=HIGH)
    return mixed.reshape(size, HEADS * HEAD_DIM)

def sequence(row_in, mask_row, keep_row, attn_full, up_full, down_full, state_full, gain_full):
    normed = rms_norm(row_in, gain_full[0])
    rate = jnp.exp(state_full[0]) / BLOCK
    decay = jnp.exp(-rate)
    bvec = jnp.sqrt(-jnp.expm1(-2.0 * rate)) * state_full[1]
    context = low(state_space(normed, keep_row, decay, bvec, state_full[2]))
    query = low(low_back(jnp.dot(low(normed), attn_full[0], precision=HIGH)))
    key = low(low_back(jnp.dot(context, attn_full[1], precision=HIGH)))
    value = low(low_back(jnp.dot(context, attn_full[2], precision=HIGH)))
    length = row_in.shape[0]
    count = length // BLOCK
    attend = jax.checkpoint(block_attention)
    mixed = lax.map(lambda item: attend(item[0], item[1], item[2]), (query.reshape(count, BLOCK, -1), key.reshape(count, BLOCK, -1), value.reshape(count, BLOCK, -1)))
    mixed = low(low_back(mixed.reshape(length, -1)))
    branch = low_back(jnp.dot(mixed, attn_full[3], precision=HIGH))
    middle = row_in + mask_row[:, None] * branch
    normed_two = rms_norm(middle, gain_full[1])
    gate = low_back(jnp.dot(low(normed_two), up_full, precision=HIGH))
    hidden = low(jax.nn.gelu(gate))
    return middle + mask_row[:, None] * jnp.dot(hidden, down_full, precision=HIGH)

def forward(tokens_f, attn_weight, up_weight, down_weight, state_param, norm_gain, masks, keeps):
    sent = (low(attn_weight), low(up_weight), low(down_weight), low(state_param), low(norm_gain))
    run = jax.checkpoint(sequence)
    length = tokens_f.shape[2]
    flat = tokens_f.reshape(-1, length, tokens_f.shape[3])
    result = lax.map(lambda item: run(item[0], item[1], item[2], sent[0], sent[1], sent[2], sent[3], sent[4]), (flat, masks.reshape(-1, length), keeps.reshape(-1, length)))
    return result.reshape(tokens_f.shape)

def adam(weight, first, second, grad, factor, rate, decay):
    clipped = grad * factor
    first_new = BETA_ONE * first + (1.0 - BETA_ONE) * clipped
    second_new = BETA_TWO * second + (1.0 - BETA_TWO) * clipped * clipped
    fix_one = 1.0 - BETA_ONE ** STEP
    fix_two = 1.0 - BETA_TWO ** STEP
    direction = first_new / fix_one / (jnp.sqrt(second_new / fix_two) + ADAM_EPS)
    weight_new = weight - rate * (direction + decay * weight)
    return (first_new, second_new, weight_new, weight_new.astype(jnp.bfloat16))

def reference(tokens, cotangent, lengths, attn_weight, up_weight, down_weight, state_param, norm_gain, attn_first, attn_second, up_first, up_second, down_first, down_second, state_first, state_second, gain_first, gain_second):
    positions = jnp.arange(LANE, dtype=jnp.int32)
    offset = positions % SLOT
    live = (offset[None, :] < lengths[:, positions // SLOT]).astype(jnp.float32)
    masks = jnp.stack([jnp.ones_like(live), live], axis=1)
    first_keep = (positions > 0).astype(jnp.float32)
    second_keep = (offset > 0).astype(jnp.float32)
    keeps = jnp.broadcast_to(jnp.stack([first_keep, second_keep])[None], masks.shape)
    tokens_f = tokens.astype(jnp.float32)

    def wrapped(tokens_in, attn_in, up_in, down_in, state_in, gain_in):
        return forward(tokens_in, attn_in, up_in, down_in, state_in, gain_in, masks, keeps)
    result, pullback = jax.vjp(wrapped, tokens_f, attn_weight, up_weight, down_weight, state_param, norm_gain)
    grads = pullback(cotangent.astype(jnp.float32))
    squares = jnp.float32(0.0)
    for grad in grads[1:]:
        squares = squares + jnp.sum(grad * grad)
    grad_norm = jnp.sqrt(squares)
    factor = jnp.minimum(1.0, CLIP_NORM / grad_norm)
    attn_new = adam(attn_weight, attn_first, attn_second, grads[1], factor, RATE_MATRIX, WEIGHT_DECAY)
    up_new = adam(up_weight, up_first, up_second, grads[2], factor, RATE_MATRIX, WEIGHT_DECAY)
    down_new = adam(down_weight, down_first, down_second, grads[3], factor, RATE_MATRIX, WEIGHT_DECAY)
    state_new = adam(state_param, state_first, state_second, grads[4], factor, RATE_STATE, 0.0)
    gain_new = adam(norm_gain, gain_first, gain_second, grads[5], factor, RATE_GAIN, 0.0)
    return (result.astype(jnp.bfloat16), grads[0].astype(jnp.bfloat16), grad_norm, attn_new[0], attn_new[1], attn_new[2], attn_new[3], up_new[0], up_new[1], up_new[2], up_new[3], down_new[0], down_new[1], down_new[2], down_new[3], state_new[0], state_new[1], state_new[2], state_new[3], gain_new[0], gain_new[1], gain_new[2], gain_new[3])
```

```python
import jax
import jax.numpy as jnp
from jax import lax
from jax.experimental import pallas as pl
from jax.experimental.pallas import tpu as pltpu
from jax.sharding import Mesh
from jax.sharding import PartitionSpec as P

HEAD_DIM = 128
BLOCK = 512
STEP = 5
SLOT = 2048

EPS_NORM = 1e-05
BETA_ONE = 0.5
BETA_TWO = 0.5
ADAM_EPS = 1e-08
WEIGHT_DECAY = 0.1
CLIP_NORM = 0.5
RATE_MATRIX = 0.02
RATE_STATE = 1.0
RATE_GAIN = 0.6
MASKED = -1e30

AXES = ("grp", "y", "z", "x", "core")
CHIPS = ("y", "z", "x")
SHARD = ("y", "z", "x", "core")
BF = jnp.bfloat16
F32 = jnp.float32
NST = 16
ROWS = 256
HALF = 512


def flip(v, axis, kind="a"):
    if lax.axis_size(axis) == 2:
        pairs = [(0, 1), (1, 0)]
    elif kind == "a":
        pairs = [(0, 1), (1, 0), (2, 3), (3, 2)]
    else:
        pairs = [(0, 3), (3, 0), (1, 2), (2, 1)]
    return lax.ppermute(v, axis, pairs)


def swap(v):
    return flip(v, "core")


def ordered(bit, own, other, axis):
    first = jnp.where(bit == 0, own, other)
    second = jnp.where(bit == 0, other, own)
    return jnp.concatenate([first, second], axis=axis)


def rms_scale(value):
    return lax.rsqrt(jnp.mean(value * value, axis=-1, keepdims=True) + EPS_NORM)


def norm_back(grad, value, inverse, gain):
    unit = value * inverse
    scaled = grad * gain
    return inverse * (scaled - unit * jnp.mean(scaled * unit, axis=-1, keepdims=True))


def mm(left, right):
    return jnp.einsum("ltk,kn->ltn", left, right, preferred_element_type=F32)


def mm_back(left, right):
    return jnp.einsum("ltn,kn->ltk", left, right, preferred_element_type=F32)


def outer(left, right):
    return jnp.einsum("ltk,ltn->kn", left, right, preferred_element_type=F32)


def spread(src, dst):
    for lane in range(2):
        for g in range(4):
            k = lane * 4 + g
            dst[pl.ds(k * ROWS, ROWS), :] = src[lane, :, g * 128 : (g + 1) * 128].astype(F32)


def collect(src, dst):
    for lane in range(2):
        for g in range(4):
            k = lane * 4 + g
            dst[lane, :, g * 128 : (g + 1) * 128] = src[pl.ds(k * ROWS, ROWS), :].astype(dst.dtype)


def at(ref, t):
    return ref[pl.ds(t, 8, stride=ROWS), :]


def end_kernel(reverse, u_ref, a_ref, e_ref, us):
    spread(u_ref, us)
    a = [a_ref[n] for n in range(NST)]

    def step(i, h):
        t = ROWS - 1 - i if reverse else i
        u = at(us, t)
        return tuple(a[n] * h[n] + u for n in range(NST))

    h = lax.fori_loop(0, ROWS, step, tuple(jnp.zeros((8, 128), F32) for _ in range(NST)), unroll=4)
    for n in range(NST):
        e_ref[n] = h[n]


def run_kernel(u_ref, a_ref, cb_ref, h_ref, s_ref, us, ss):
    spread(u_ref, us)

    def step(t, h):
        u = at(us, t)
        h = tuple(a_ref[n] * h[n] + u for n in range(NST))
        terms = [cb_ref[n] * h[n] for n in range(NST)]
        while len(terms) > 1:
            terms = [terms[i] + terms[i + 1] for i in range(0, len(terms), 2)]
        ss[pl.ds(t, 8, stride=ROWS), :] = terms[0]
        return h

    lax.fori_loop(0, ROWS, step, tuple(h_ref[n] for n in range(NST)), unroll=4)
    collect(ss, s_ref)


def back_kernel(u_ref, d_ref, a_ref, cb_ref, h_ref, q_ref, du_ref, qu_ref, r_ref, us, ds, dus, hist):
    spread(u_ref, us)
    spread(d_ref, ds)
    half = NST // 2
    for part in range(2):
        base = part * half
        a = [a_ref[base + n] for n in range(half)]

        def ahead(t, h):
            u = at(us, t)
            for n in range(half):
                hist[t, n] = h[n]
            return tuple(a[n] * h[n] + u for n in range(half))

        lax.fori_loop(0, ROWS, ahead, tuple(h_ref[base + n] for n in range(half)), unroll=4)

        def behind(i, carry):
            q, qu, r = carry
            t = ROWS - 1 - i
            u = at(us, t)
            d = at(ds, t)
            q = tuple(a[n] * q[n] + d for n in range(half))
            terms = [cb_ref[base + n] * q[n] for n in range(half)]
            while len(terms) > 1:
                terms = [terms[k] + terms[k + 1] for k in range(0, len(terms), 2)]
            du = terms[0]
            if part:
                du = du + at(dus, t)
            dus[pl.ds(t, 8, stride=ROWS), :] = du
            qu = tuple(qu[n] + q[n] * u for n in range(half))
            r = tuple(r[n] + q[n] * hist[t, n] for n in range(half))
            return (q, qu, r)

        zero = tuple(jnp.zeros((8, 128), F32) for _ in range(half))
        _, qu, r = lax.fori_loop(
            0, ROWS, behind, (tuple(q_ref[base + n] for n in range(half)), zero, zero), unroll=2
        )
        for n in range(half):
            qu_ref[base + n] = qu[n]
            r_ref[base + n] = r[n]
    collect(dus, du_ref)


STATE = jax.ShapeDtypeStruct((NST, 8, 128), F32)
SPREAD = pltpu.VMEM((8 * ROWS, 128), F32)
PARAMS = pltpu.CompilerParams(vmem_limit_bytes=40 * 1024 * 1024)


def state_end(u, a, reverse):
    return pl.pallas_call(
        lambda *refs: end_kernel(reverse, *refs),
        out_shape=STATE,
        scratch_shapes=[SPREAD],
        compiler_params=PARAMS,
        cost_estimate=pl.CostEstimate(flops=16_000_000, bytes_accessed=1_200_000, transcendentals=0),
        name="state_end",
    )(u, a)


def state_run(u, a, cb, h):
    return pl.pallas_call(
        run_kernel,
        out_shape=jax.ShapeDtypeStruct((2, ROWS, HALF), BF),
        scratch_shapes=[SPREAD, SPREAD],
        compiler_params=PARAMS,
        cost_estimate=pl.CostEstimate(flops=32_000_000, bytes_accessed=2_000_000, transcendentals=0),
        name="state_run",
    )(u, a, cb, h)


def state_back(u, d, a, cb, h, q):
    return pl.pallas_call(
        back_kernel,
        out_shape=(jax.ShapeDtypeStruct((2, ROWS, HALF), F32), STATE, STATE),
        scratch_shapes=[SPREAD, SPREAD, SPREAD, pltpu.VMEM((ROWS, NST // 2, 8, 128), F32)],
        compiler_params=PARAMS,
        cost_estimate=pl.CostEstimate(flops=80_000_000, bytes_accessed=4_000_000, transcendentals=0),
        name="state_back",
    )(u, d, a, cb, h, q)


STEPS = (("x", "a"), ("x", "b"), ("z", "a"), ("z", "b"), ("y", "a"))


def carry(total, rate, chip, reverse):
    lane_one = (lax.broadcasted_iota(jnp.int32, (8, 128), 0) >= 4)[None]
    entering = jnp.zeros_like(total)
    for k, (axis, kind) in enumerate(STEPS):
        other = flip(total, axis, kind)
        upper = (chip >> k) & 1
        within = chip & ((1 << k) - 1)
        if reverse:
            takes, gap = upper == 0, (1 << k) - 1 - within
        else:
            takes, gap = upper == 1, within
        reach = jnp.exp(-rate * (ROWS * gap).astype(F32)) * other
        whole = jnp.exp(-rate * float(ROWS << k))
        far = jnp.where(takes, other, total)
        near = jnp.where(takes, total, other)
        joined = whole * far + near
        if k >= 3:
            reach = jnp.where(lane_one, 0.0, reach)
            joined = jnp.where(lane_one, 0.0, joined)
        entering = entering + jnp.where(takes, reach, 0.0)
        total = joined
    return entering


def adam(weight, first, second, grad, factor, rate, decay):
    clipped = grad * factor
    first_new = BETA_ONE * first + (1.0 - BETA_ONE) * clipped
    second_new = BETA_TWO * second + (1.0 - BETA_TWO) * clipped * clipped
    fix_one = 1.0 - BETA_ONE**STEP
    fix_two = 1.0 - BETA_TWO**STEP
    direction = first_new / fix_one / (jnp.sqrt(second_new / fix_two) + ADAM_EPS)
    weight_new = weight - rate * (direction + decay * weight)
    return (first_new, second_new, weight_new, weight_new.astype(BF))


def body(
    tokens, cotangent, lengths, attn_weight, up_weight, down_weight, state_param, norm_gain,
    attn_first, attn_second, up_first, up_second, down_first, down_second,
    state_first, state_second, gain_first, gain_second,
):
    core = lax.axis_index("core")
    ybit = lax.axis_index("y")
    chip = (ybit * 4 + lax.axis_index("z")) * 4 + lax.axis_index("x")

    mine = jnp.concatenate(
        [state_param.astype(BF).transpose(0, 2, 1).reshape(-1), norm_gain.astype(BF).reshape(-1)]
    )
    mine = jnp.pad(mine, (0, 1024 - mine.shape[0])).reshape(1, 8, 128)
    pair = ordered(core, mine, swap(mine), 0)
    small = lax.all_to_all(
        jnp.broadcast_to(pair[None], (32, 2, 8, 128)), CHIPS, split_axis=0, concat_axis=0, tiled=True
    ).reshape(64, 1024)
    theta = small[:, :768].reshape(64, 3, NST, 16).transpose(1, 2, 0, 3).reshape(3, NST, 1024).astype(F32)
    gains = small[:, 768:800].reshape(64, 2, 16).transpose(1, 0, 2).reshape(2, 1024).astype(F32)

    x = ordered(core, tokens[0], swap(tokens[0]), 1).astype(F32)
    dy = ordered(core, cotangent[0], swap(cotangent[0]), 1).astype(F32)
    offset = (chip % (SLOT // ROWS)) * ROWS
    live_len = lax.dynamic_index_in_dim(lengths[0], chip // (SLOT // ROWS), 0, keepdims=False)
    steps = lax.iota(jnp.int32, ROWS)
    live = jnp.stack([jnp.ones((ROWS,), F32), (offset + steps < live_len).astype(F32)])[:, :, None]

    attn_low = attn_weight.astype(BF)
    up_low = up_weight.astype(BF).reshape(16, 32, 2, 64).transpose(2, 0, 1, 3).reshape(2, 16, 2048)
    down_low = down_weight.astype(BF)
    attn_keep = lax.dynamic_slice_in_dim(attn_low, core * HALF, HALF, 2)
    attn_give = lax.dynamic_slice_in_dim(attn_low, (1 - core) * HALF, HALF, 2)
    attn_chip = ordered(core, attn_keep, swap(attn_give), 1)
    up_keep = lax.dynamic_index_in_dim(up_low, core, 0, keepdims=False)
    up_give = lax.dynamic_index_in_dim(up_low, 1 - core, 0, keepdims=False)
    up_chip = ordered(core, up_keep, swap(up_give), 0)

    def gather(v):
        both = ordered(ybit, v[None], flip(v, "y")[None], 0)
        every = lax.all_gather(both, ("z", "x"), axis=0)
        return jnp.swapaxes(every, 0, 1)

    attn_all = gather(attn_chip)
    attn_full = attn_all.transpose(2, 0, 1, 3, 4).reshape(4, 1024, HALF)
    ffn_all = gather(jnp.concatenate([up_chip.reshape(64, 1024), down_low], axis=0))
    up_full = ffn_all[:, :, :64].reshape(1024, 2048)
    down_full = ffn_all[:, :, 64:].reshape(2048, 1024)
    wq, wk, wv = attn_full[0], attn_full[1], attn_full[2]
    wo_cols = attn_full[3]
    wo_got = swap(lax.dynamic_slice_in_dim(wo_cols, (1 - core) * HALF, HALF, 0))
    wo_mine = lax.dynamic_slice_in_dim(wo_cols, core * HALF, HALF, 0)
    wo = ordered(core, wo_mine, wo_got, 1)

    theta_c = lax.dynamic_slice_in_dim(theta, core * HALF, HALF, 2).reshape(3, NST, 4, 128)
    theta_c = jnp.concatenate([theta_c, theta_c], axis=2)
    rate = jnp.exp(theta_c[0]) / BLOCK
    decay = jnp.exp(-rate)
    norm_scale = jnp.sqrt(-jnp.expm1(-2.0 * rate))
    cb = norm_scale * theta_c[1] * theta_c[2]

    inverse_one = rms_scale(x)
    unit_one = x * inverse_one
    u = unit_one * gains[0]
    u_low = u.astype(BF)
    u_half = lax.dynamic_slice_in_dim(u, core * HALF, HALF, 2)

    entering = carry(state_end(u_half, decay, False), rate, chip, False)
    sb_half = state_run(u_half, decay, cb, entering)
    prev_half = lax.ppermute(sb_half, "x", [(0, 1), (2, 3)])
    sb_two = jnp.concatenate([prev_half, sb_half], axis=1)
    sb = ordered(core, sb_two, swap(sb_two), 2)

    query = mm(u_low, wq).astype(BF)
    keys = mm(sb, wk).astype(BF)
    values = mm(sb, wv).astype(BF)
    query_h = query.reshape(2, ROWS, 4, HEAD_DIM)
    key_h = keys.reshape(2, 2 * ROWS, 4, HEAD_DIM)
    value_h = values.reshape(2, 2 * ROWS, 4, HEAD_DIM)
    scale = HEAD_DIM ** (-0.5)
    reach = lax.iota(jnp.int32, 2 * ROWS)[None, :] - ROWS
    allowed = (reach <= steps[:, None]) & (reach >= -(chip % 2) * ROWS)
    scores = jnp.einsum("lqhd,lkhd->lhqk", query_h, key_h, preferred_element_type=F32) * scale
    scores = jnp.where(allowed, scores, MASKED)
    top = jnp.max(scores, axis=-1, keepdims=True)
    weights = jnp.exp(scores - top)
    probs = weights / jnp.sum(weights, axis=-1, keepdims=True)
    probs_low = probs.astype(BF)
    mixed = (
        jnp.einsum("lhqk,lkhd->lqhd", probs_low, value_h, preferred_element_type=F32)
        .reshape(2, ROWS, HALF)
        .astype(BF)
    )
    part = mm(mixed, wo).astype(BF)
    branch = part.astype(F32) + swap(part).astype(F32)
    middle = x + live * branch
    inverse_two = rms_scale(middle)
    z_low = (middle * inverse_two * gains[1]).astype(BF)

    grad_ffn = (live * dy).astype(BF)
    gate = mm(z_low, up_full)
    hidden = jax.nn.gelu(gate).astype(BF)
    out_part = mm(hidden, down_full)
    down_grad = outer(hidden, grad_ffn)
    grad_hidden = mm_back(grad_ffn, down_full)
    grad_gate = jax.vjp(jax.nn.gelu, gate)[1](grad_hidden)[0].astype(BF)
    up_grad = outer(z_low, grad_gate)
    dz_part = mm_back(grad_gate, up_full).astype(BF)

    def own(v, which):
        return lax.dynamic_slice_in_dim(v, which * 128, 128, 1)

    out_got = swap(own(out_part, 1 - core).astype(BF)).astype(F32)
    output = (own(middle, core) + own(live, core) * (own(out_part, core) + out_got)).astype(BF)

    def to_owners(v, axis):
        got = lax.all_to_all(v.astype(BF), CHIPS, split_axis=axis, concat_axis=axis, tiled=True)
        shape = got.shape[:axis] + (32, got.shape[axis] // 32) + got.shape[axis + 1 :]
        return jnp.sum(got.reshape(shape).astype(F32), axis=axis)

    def both_groups(v):
        low = v.astype(BF)
        return low.astype(F32) + flip(low, "grp").astype(F32)

    up_sum = both_groups(to_owners(up_grad, 0))
    down_sum = both_groups(to_owners(down_grad, 0))

    dz = dz_part.astype(F32) + swap(dz_part).astype(F32)
    unit_two = middle * inverse_two
    gain_two_grad = jnp.sum(dz * unit_two, axis=(0, 1))
    dm = dy + norm_back(dz, middle, inverse_two, gains[1])
    dbranch = (live * dm).astype(BF)
    out_grad = outer(mixed, dbranch)
    grad_mixed = mm_back(dbranch, wo).astype(BF).reshape(2, ROWS, 4, HEAD_DIM)
    grad_probs = jnp.einsum("lqhd,lkhd->lhqk", grad_mixed, value_h, preferred_element_type=F32)
    total = jnp.sum(probs * grad_probs, axis=-1, keepdims=True)
    grad_scores = (probs * (grad_probs - total)).astype(BF)
    grad_query = (
        (jnp.einsum("lhqk,lkhd->lqhd", grad_scores, key_h, preferred_element_type=F32) * scale)
        .reshape(2, ROWS, HALF)
        .astype(BF)
    )
    grad_keys = (
        (jnp.einsum("lhqk,lqhd->lkhd", grad_scores, query_h, preferred_element_type=F32) * scale)
        .reshape(2, 2 * ROWS, HALF)
        .astype(BF)
    )
    grad_values = (
        jnp.einsum("lhqk,lqhd->lkhd", probs_low, grad_mixed, preferred_element_type=F32)
        .reshape(2, 2 * ROWS, HALF)
        .astype(BF)
    )
    ds_part = (mm_back(grad_keys, wk) + mm_back(grad_values, wv)).astype(BF)
    du_part = mm_back(grad_query, wq).astype(BF)

    def half(v, which):
        return lax.dynamic_slice_in_dim(v, which * HALF, HALF, 2)

    ds_sum = half(ds_part, core).astype(F32) + swap(half(ds_part, 1 - core)).astype(F32)
    du_sum = half(du_part, core).astype(F32) + swap(half(du_part, 1 - core)).astype(F32)
    ds_back = lax.ppermute(ds_sum[:, :ROWS].astype(BF), "x", [(1, 0), (3, 2)])
    ds_half = ds_sum[:, ROWS:] + ds_back.astype(F32)

    wo_give = lax.dynamic_slice_in_dim(out_grad, (1 - core) * HALF, HALF, 1).astype(BF)
    wo_keep = lax.dynamic_slice_in_dim(out_grad, core * HALF, HALF, 1).astype(BF)
    out_cols = ordered(core, wo_keep, swap(wo_give), 0)
    attn_grad = jnp.stack(
        [
            outer(u_low, grad_query).astype(BF),
            outer(sb, grad_keys).astype(BF),
            outer(sb, grad_values).astype(BF),
            out_cols,
        ]
    )
    attn_sum = both_groups(to_owners(attn_grad, 1))

    leaving = carry(state_end(ds_half, decay, True), rate, chip, True)
    du_state, qu, rr = state_back(u_half, ds_half, decay, cb, entering, leaving)
    du_half = du_state + du_sum
    unit_half = lax.dynamic_slice_in_dim(unit_one, core * HALF, HALF, 2)
    gain_one_grad = jnp.sum(du_half * unit_half, axis=(0, 1))

    du_got = swap(own(du_half, 1 - core))
    du_own = ordered(core, own(du_half, core), du_got, 2)
    grad_in = norm_back(du_own, own(x, core), own(inverse_one, core), gains[0])
    token_grad = (grad_in + own(dm, core)).astype(BF)

    lanes = jnp.stack([qu, rr]).reshape(2, NST, 2, HALF).sum(axis=2).reshape(2 * NST, HALF)
    gain_two_half = lax.dynamic_slice_in_dim(gain_two_grad, core * HALF, HALF, 0)
    lanes = jnp.concatenate([lanes, gain_one_grad[None], gain_two_half[None]], axis=0)
    packed = lanes.reshape(34, 32, 16).transpose(1, 0, 2)
    got = lax.all_to_all(packed, CHIPS, split_axis=0, concat_axis=0, tiled=True)
    small_sum = jnp.sum(got, axis=0)
    small_sum = small_sum + flip(small_sum, "grp")
    hand = []
    for y in range(2):
        for z in range(4):
            for xx in range(4):
                for c in range(2):
                    j = (y * 4 + z) * 4 + xx
                    hand.append((j * 2 + c, c * 32 + j))
    mine_sum = lax.ppermute(small_sum, SHARD, hand)

    t_own = state_param.astype(BF).astype(F32).transpose(0, 2, 1)
    rate_o = jnp.exp(t_own[0]) / BLOCK
    decay_o = jnp.exp(-rate_o)
    scale_o = jnp.sqrt(-jnp.expm1(-2.0 * rate_o))
    b_o = scale_o * t_own[1]
    qu_o, rr_o = mine_sum[:NST], mine_sum[NST : 2 * NST]
    gb = t_own[2] * qu_o
    log_rate_grad = rate_o * (
        -decay_o * t_own[2] * b_o * rr_o + decay_o * decay_o / scale_o * t_own[1] * gb
    )
    state_grad = jnp.stack([log_rate_grad, scale_o * gb, b_o * qu_o]).transpose(0, 2, 1)
    gain_grad = mine_sum[2 * NST :]

    def split_rows(v, axis):
        keep = lax.dynamic_slice_in_dim(v, core * 16, 16, axis)
        give = lax.dynamic_slice_in_dim(v, (1 - core) * 16, 16, axis)
        return keep, swap(give)

    up_keep, up_got = split_rows(up_sum, 0)
    up_own = ordered(core, up_keep.reshape(16, 32, 1, 64), up_got.reshape(16, 32, 1, 64), 2).reshape(16, 4096)
    attn_keep, attn_got = split_rows(attn_sum, 1)
    attn_own = ordered(core, attn_keep, attn_got, 2)

    squares = F32(0.0)
    for piece in (attn_own, up_own, down_sum, state_grad, gain_grad):
        squares = squares + jnp.sum(piece * piece)
    squares = jnp.broadcast_to(squares, (8, 128))
    squares = squares + swap(squares)
    every = lax.all_to_all(
        jnp.broadcast_to(squares[None], (32, 8, 128)), CHIPS, split_axis=0, concat_axis=0, tiled=True
    )
    grad_norm = jnp.sqrt(jnp.sum(every[:, 0, 0]))
    factor = jnp.minimum(1.0, CLIP_NORM / grad_norm)

    attn_new = adam(attn_weight, attn_first, attn_second, attn_own, factor, RATE_MATRIX, WEIGHT_DECAY)
    up_new = adam(up_weight, up_first, up_second, up_own, factor, RATE_MATRIX, WEIGHT_DECAY)
    down_new = adam(down_weight, down_first, down_second, down_sum, factor, RATE_MATRIX, WEIGHT_DECAY)
    state_new = adam(state_param, state_first, state_second, state_grad, factor, RATE_STATE, 0.0)
    gain_new = adam(norm_gain, gain_first, gain_second, gain_grad, factor, RATE_GAIN, 0.0)
    return (output[None], token_grad[None], grad_norm) + attn_new + up_new + down_new + state_new + gain_new


def solution(mesh):
    inner = Mesh(mesh.devices.reshape(2, 2, 4, 4, 2), AXES)
    rows = P("grp", None, SHARD, None)
    attn = P(None, SHARD, None)
    flat = P(SHARD, None)
    gain = P(None, SHARD)
    in_specs = (rows, rows, P("grp", None), attn, flat, flat, attn, gain)
    in_specs += (attn, attn, flat, flat, flat, flat, attn, attn, gain, gain)
    out_specs = (rows, rows, P()) + (attn,) * 4 + (flat,) * 8 + (attn,) * 4 + (gain,) * 4
    return jax.shard_map(body, mesh=inner, in_specs=in_specs, out_specs=out_specs, check_vma=False)
```

```python
import jax
import jax.numpy as jnp
from jax import lax
from jax.experimental import pallas as pl
from jax.experimental.pallas import tpu as pltpu
from jax.sharding import Mesh
from jax.sharding import PartitionSpec as P

HEAD_DIM = 128
BLOCK = 512
STEP = 5
SLOT = 2048

EPS_NORM = 1e-05
BETA_ONE = 0.5
BETA_TWO = 0.5
ADAM_EPS = 1e-08
WEIGHT_DECAY = 0.1
CLIP_NORM = 0.5
RATE_MATRIX = 0.02
RATE_STATE = 1.0
RATE_GAIN = 0.6
MASKED = -1e30

AXES = ("grp", "y", "z", "x", "core")
CHIPS = ("y", "z", "x")
SHARD = ("y", "z", "x", "core")
BF = jnp.bfloat16
F32 = jnp.float32
NST = 16
ROWS = 256
HALF = 512


def flip(v, axis, kind="a"):
    if lax.axis_size(axis) == 2:
        pairs = [(0, 1), (1, 0)]
    elif kind == "a":
        pairs = [(0, 1), (1, 0), (2, 3), (3, 2)]
    else:
        pairs = [(0, 3), (3, 0), (1, 2), (2, 1)]
    return lax.ppermute(v, axis, pairs)


def swap(v):
    return flip(v, "core")


def ordered(bit, own, other, axis):
    first = jnp.where(bit == 0, own, other)
    second = jnp.where(bit == 0, other, own)
    return jnp.concatenate([first, second], axis=axis)


def rms_scale(value):
    return lax.rsqrt(jnp.mean(value * value, axis=-1, keepdims=True) + EPS_NORM)


def norm_back(grad, value, inverse, gain):
    unit = value * inverse
    scaled = grad * gain
    return inverse * (scaled - unit * jnp.mean(scaled * unit, axis=-1, keepdims=True))


VMEM = 48 * 1024 * 1024


def dot(left, right):
    return jnp.dot(left, right, preferred_element_type=F32)


def dot_nt(left, right):
    return lax.dot_general(left, right, (((1,), (1,)), ((), ())), preferred_element_type=F32)


def dot_tn(left, right):
    return lax.dot_general(left, right, (((0,), (0,)), ((), ())), preferred_element_type=F32)


def params():
    return pltpu.CompilerParams(vmem_limit_bytes=VMEM)


def cost(flops, bytes_accessed):
    return pl.CostEstimate(flops=flops, bytes_accessed=bytes_accessed, transcendentals=0)


def sds(shape, dtype):
    return jax.ShapeDtypeStruct(shape, dtype)


SMEM = pl.BlockSpec(memory_space=pltpu.SMEM)
FULL = pl.BlockSpec(memory_space=pltpu.VMEM)


def live_of(info, lane):
    if lane == 0:
        return jnp.ones((ROWS, 1), F32)
    return (lax.broadcasted_iota(jnp.int32, (ROWS, 1), 0) < info[1]).astype(F32)


def at(ref, t):
    return ref[pl.ds(t, 8, stride=ROWS), :]


def tree(terms):
    while len(terms) > 1:
        terms = [terms[i] + terms[i + 1] for i in range(0, len(terms), 2)]
    return terms[0]


def sweep(u_ref, a_ref, e_ref, reverse):
    a = [a_ref[n] for n in range(NST)]

    def step(i, h):
        u = at(u_ref, ROWS - 1 - i if reverse else i)
        return tuple(a[n] * h[n] + u for n in range(NST))

    h = lax.fori_loop(0, ROWS, step, tuple(jnp.zeros((8, 128), F32) for _ in range(NST)), unroll=4)
    for n in range(NST):
        e_ref[n] = h[n]


def first_kernel(info, x_ref, gain_ref, a_ref, low_ref, us_ref, e_ref):
    for lane in range(2):
        x = x_ref[lane].astype(F32)
        u = x * rms_scale(x) * gain_ref[...]
        low_ref[lane] = u.astype(BF)
        half = jnp.where(info[0] == 0, u[:, :HALF], u[:, HALF:])
        for g in range(4):
            us_ref[pl.ds((lane * 4 + g) * ROWS, ROWS), :] = half[:, g * 128 : (g + 1) * 128]
    sweep(us_ref, a_ref, e_ref, False)


def first(info, x, gain, a):
    return pl.pallas_call(
        first_kernel,
        out_shape=(sds((2, ROWS, 1024), BF), sds((8 * ROWS, 128), F32), sds((NST, 8, 128), F32)),
        in_specs=[SMEM, FULL, FULL, FULL],
        compiler_params=params(),
        cost_estimate=cost(16_000_000, 3_000_000),
        name="first",
    )(info, x, gain, a)


def run_kernel(us, a_ref, cb_ref, h_ref, s_ref, ss):
    def step(t, h):
        u = at(us, t)
        h = tuple(a_ref[n] * h[n] + u for n in range(NST))
        ss[pl.ds(t, 8, stride=ROWS), :] = tree([cb_ref[n] * h[n] for n in range(NST)])
        return h

    lax.fori_loop(0, ROWS, step, tuple(h_ref[n] for n in range(NST)), unroll=4)
    for lane in range(2):
        for g in range(4):
            s_ref[lane, :, g * 128 : (g + 1) * 128] = ss[pl.ds((lane * 4 + g) * ROWS, ROWS), :].astype(BF)


def state_run(us, a, cb, h):
    return pl.pallas_call(
        run_kernel,
        out_shape=sds((2, ROWS, HALF), BF),
        scratch_shapes=[pltpu.VMEM((8 * ROWS, 128), F32)],
        compiler_params=params(),
        cost_estimate=cost(32_000_000, 2_000_000),
        name="state_run",
    )(us, a, cb, h)


def turn_kernel(keep_ref, got_ref, back_ref, a_ref, ds_ref, e_ref):
    for lane in range(2):
        d = keep_ref[lane, ROWS : 2 * ROWS, :] + got_ref[lane, ROWS : 2 * ROWS, :].astype(F32)
        d = d + back_ref[lane].astype(F32)
        for g in range(4):
            ds_ref[pl.ds((lane * 4 + g) * ROWS, ROWS), :] = d[:, g * 128 : (g + 1) * 128]
    sweep(ds_ref, a_ref, e_ref, True)


def state_turn(keep, got, back, a):
    return pl.pallas_call(
        turn_kernel,
        out_shape=(sds((8 * ROWS, 128), F32), sds((NST, 8, 128), F32)),
        compiler_params=params(),
        cost_estimate=cost(16_000_000, 4_000_000),
        name="state_turn",
    )(keep, got, back, a)


def back_kernel(
    info, us, ds, a_ref, cb_ref, h_ref, q_ref, keep_ref, got_ref, x_ref,
    mine_ref, give_ref, qu_ref, r_ref, g_ref, dus, hist,
):
    half = NST // 2
    for part in range(2):
        base = part * half
        a = [a_ref[base + n] for n in range(half)]

        def ahead(t, h):
            u = at(us, t)
            for n in range(half):
                hist[t, n] = h[n]
            return tuple(a[n] * h[n] + u for n in range(half))

        lax.fori_loop(0, ROWS, ahead, tuple(h_ref[base + n] for n in range(half)), unroll=4)

        def behind(i, held):
            q, qu, r = held
            t = ROWS - 1 - i
            u = at(us, t)
            d = at(ds, t)
            q = tuple(a[n] * q[n] + d for n in range(half))
            du = tree([cb_ref[base + n] * q[n] for n in range(half)])
            if part:
                du = du + at(dus, t)
            dus[pl.ds(t, 8, stride=ROWS), :] = du
            qu = tuple(qu[n] + q[n] * u for n in range(half))
            r = tuple(r[n] + q[n] * hist[t, n] for n in range(half))
            return (q, qu, r)

        zero = tuple(jnp.zeros((8, 128), F32) for _ in range(half))
        _, qu, r = lax.fori_loop(
            0, ROWS, behind, (tuple(q_ref[base + n] for n in range(half)), zero, zero), unroll=2
        )
        for n in range(half):
            qu_ref[base + n] = qu[n]
            r_ref[base + n] = r[n]
    mine_at = pl.multiple_of(info[0] * 128, 128)
    give_at = pl.multiple_of((1 - info[0]) * 128, 128)
    total = jnp.zeros((1, HALF), F32)
    for lane in range(2):
        x = x_ref[lane].astype(F32)
        unit = x * rms_scale(x)
        unit = jnp.where(info[0] == 0, unit[:, :HALF], unit[:, HALF:])
        parts = [dus[pl.ds((lane * 4 + g) * ROWS, ROWS), :] for g in range(4)]
        du = jnp.concatenate(parts, axis=1)
        du = du + keep_ref[lane, 2 * ROWS :, :] + got_ref[lane, 2 * ROWS :, :].astype(F32)
        total = total + jnp.sum(du * unit, axis=0, keepdims=True)
        low, high = du[:128], du[128:]
        mine_ref[lane] = jnp.where(info[0] == 0, low, high)
        give_ref[lane] = jnp.where(info[0] == 0, high, low)
    g_ref[...] = total


def state_back(info, us, ds, a, cb, h, q, keep, got, x):
    state = sds((NST, 8, 128), F32)
    return pl.pallas_call(
        back_kernel,
        out_shape=(sds((2, 128, HALF), F32), sds((2, 128, HALF), F32), state, state, sds((1, HALF), F32)),
        in_specs=[SMEM] + [FULL] * 9,
        scratch_shapes=[pltpu.VMEM((8 * ROWS, 128), F32), pltpu.VMEM((ROWS, NST // 2, 8, 128), F32)],
        compiler_params=params(),
        cost_estimate=cost(80_000_000, 8_000_000),
        name="state_back",
    )(info, us, ds, a, cb, h, q, keep, got, x)


def matrix(ref, n, half):
    row, col = 32 * (n // 2), HALF * (n % 2)
    return ref[:, pl.ds(half, 1), row : row + 32, col : col + HALF].reshape(HALF, HALF)


def columns(info):
    return (
        pl.ds(pl.multiple_of(info[0] * HALF, HALF), HALF),
        pl.ds(pl.multiple_of((1 - info[0]) * HALF, HALF), HALF),
    )


def wide(v):
    return v.reshape(v.shape[0] * v.shape[1], v.shape[2])


def attn_kernel(
    info, u_ref, po, oo, ps, os, w_ref, wo_ref, part_ref, q_ref, k_ref, v_ref, o_ref, p_ref
):
    me, it = info[0], 1 - info[0]
    mine, other = columns(info)
    u = u_ref[0]
    q_ref[0] = (dot(u[:, :HALF], matrix(w_ref, 0, 0)) + dot(u[:, HALF:], matrix(w_ref, 0, 1))).astype(BF)
    for n, ref in ((1, k_ref), (2, v_ref)):
        w_me, w_it = matrix(w_ref, n, me), matrix(w_ref, n, it)
        ref[0, :ROWS] = (dot(po[0], w_me) + dot(ps[0], w_it)).astype(BF)
        ref[0, ROWS:] = (dot(oo[0], w_me) + dot(os[0], w_it)).astype(BF)
    row = lax.broadcasted_iota(jnp.int32, (ROWS, 2 * ROWS), 0)
    col = lax.broadcasted_iota(jnp.int32, (ROWS, 2 * ROWS), 1) - ROWS
    allowed = (col <= row) & (col >= -info[2] * ROWS)
    for h in range(4):
        at_h = slice(h * HEAD_DIM, (h + 1) * HEAD_DIM)
        s = dot_nt(q_ref[0, :, at_h], k_ref[0, :, at_h]) * HEAD_DIM**-0.5
        s = jnp.where(allowed, s, MASKED)
        w = jnp.exp(s - jnp.max(s, axis=-1, keepdims=True))
        p = w / jnp.sum(w, axis=-1, keepdims=True)
        p_ref[0, h] = p
        o_ref[0, :, at_h] = dot(p.astype(BF), v_ref[0, :, at_h]).astype(BF)
    o = o_ref[0]
    part_ref[0, :, mine] = dot(o, matrix(w_ref, 3, me)).astype(BF)
    part_ref[0, :, other] = dot(o, wide(wo_ref[...])).astype(BF)


def lane_block(*shape):
    return pl.BlockSpec((1,) + shape, lambda i: (i,) + (0,) * len(shape))


def whole_block(*shape):
    return pl.BlockSpec(shape, lambda i: (0,) * len(shape))


ATTN_BLOCK = pl.BlockSpec((16, 2, 64, 1024), lambda i: (0, 0, 2, 0))


def attention(info, u, po, oo, ps, os, w, wo):
    q_block, k_block = lane_block(ROWS, HALF), lane_block(2 * ROWS, HALF)
    return pl.pallas_call(
        attn_kernel,
        grid=(2,),
        out_shape=(
            sds((2, ROWS, 1024), BF), sds((2, ROWS, HALF), BF), sds((2, 2 * ROWS, HALF), BF),
            sds((2, 2 * ROWS, HALF), BF), sds((2, ROWS, HALF), BF), sds((2, 4, ROWS, 2 * ROWS), F32),
        ),
        in_specs=[SMEM, lane_block(ROWS, 1024)] + [q_block] * 4
        + [ATTN_BLOCK, whole_block(16, 32, HALF)],
        out_specs=(
            lane_block(ROWS, 1024), q_block, k_block, k_block, q_block, lane_block(4, ROWS, 2 * ROWS),
        ),
        compiler_params=params(),
        cost_estimate=cost(4_000_000_000, 16_000_000),
        name="attention",
    )(info, u, po, oo, ps, os, w, wo)


def attn_back_kernel(
    info, own_ref, sib_ref, mid_ref, dy_ref, gain_ref, w_ref, wo_ref, q_ref, k_ref, v_ref, o_ref, p_ref,
    dm_ref, g_ref, keep_ref, send_ref, dq_ref, dk_ref, dv_ref, wk_ref, ws_ref, acc_me, acc_it,
):
    lane = pl.program_id(0)
    me, it = info[0], 1 - info[0]
    m = mid_ref[0]
    dz = own_ref[0].astype(F32) + sib_ref[0].astype(F32)
    inverse = rms_scale(m)
    unit = m * inverse
    gain_part = jnp.sum(dz * unit, axis=0, keepdims=True)
    scaled = dz * gain_ref[...]
    dm = dy_ref[0].astype(F32) + inverse * (scaled - unit * jnp.mean(scaled * unit, axis=-1, keepdims=True))
    dm_ref[0] = dm
    count = jnp.where(lane == 0, ROWS, info[1])
    live = (lax.broadcasted_iota(jnp.int32, (ROWS, 1), 0) < count).astype(F32)
    branch = (live * dm).astype(BF)
    branch_me = jnp.where(info[0] == 0, branch[:, :HALF], branch[:, HALF:])
    branch_it = jnp.where(info[0] == 0, branch[:, HALF:], branch[:, :HALF])
    d_o = (
        dot_nt(branch_me, matrix(w_ref, 3, me)) + dot_nt(branch_it, wide(wo_ref[...]))
    ).astype(BF)
    o = o_ref[0]
    grad_me, grad_it = dot_tn(o, branch_me), dot_tn(o, branch_it)

    @pl.when(lane == 0)
    def _():
        g_ref[...] = gain_part
        acc_me[...] = grad_me
        acc_it[...] = grad_it

    @pl.when(lane == 1)
    def _():
        g_ref[...] += gain_part
        wk_ref[...] = (acc_me[...] + grad_me).astype(BF).reshape(16, 32, HALF)
        ws_ref[...] = (acc_it[...] + grad_it).astype(BF).reshape(16, 32, HALF)

    scale = HEAD_DIM**-0.5
    for h in range(4):
        at_h = slice(h * HEAD_DIM, (h + 1) * HEAD_DIM)
        p = p_ref[0, h]
        dp = dot_nt(d_o[:, at_h], v_ref[0, :, at_h])
        total = jnp.sum(p * dp, axis=-1, keepdims=True)
        ds = (p * (dp - total)).astype(BF)
        dq_ref[0, :, at_h] = (dot(ds, k_ref[0, :, at_h]) * scale).astype(BF)
        dk_ref[0, :, at_h] = (dot_tn(ds, q_ref[0, :, at_h]) * scale).astype(BF)
        dv_ref[0, :, at_h] = dot_tn(p.astype(BF), d_o[:, at_h]).astype(BF)
    for ref, at_c in ((keep_ref, me), (send_ref, it)):
        ds = dot_nt(dk_ref[0], matrix(w_ref, 1, at_c)) + dot_nt(dv_ref[0], matrix(w_ref, 2, at_c))
        ref[0, : 2 * ROWS] = ds.astype(ref.dtype)
        ref[0, 2 * ROWS :] = dot_nt(dq_ref[0], matrix(w_ref, 0, at_c)).astype(ref.dtype)


def attention_back(info, own, sib, mid, dy, gain, w, wo, q, k, v, o, p):
    q_block, k_block, t_block = lane_block(ROWS, HALF), lane_block(2 * ROWS, HALF), lane_block(ROWS, 1024)
    s_block = lane_block(3 * ROWS, HALF)
    wo_block = whole_block(16, 32, HALF)
    return pl.pallas_call(
        attn_back_kernel,
        grid=(2,),
        out_shape=(
            sds((2, ROWS, 1024), F32), sds((1, 1024), F32), sds((2, 3 * ROWS, HALF), F32),
            sds((2, 3 * ROWS, HALF), BF), sds((2, ROWS, HALF), BF), sds((2, 2 * ROWS, HALF), BF),
            sds((2, 2 * ROWS, HALF), BF), sds((16, 32, HALF), BF), sds((16, 32, HALF), BF),
        ),
        in_specs=[SMEM, t_block, t_block, t_block, t_block, whole_block(1, 1024), ATTN_BLOCK]
        + [wo_block, q_block, k_block, k_block, q_block, lane_block(4, ROWS, 2 * ROWS)],
        out_specs=(
            t_block, whole_block(1, 1024), s_block, s_block, q_block, k_block, k_block, wo_block, wo_block,
        ),
        scratch_shapes=[pltpu.VMEM((HALF, HALF), F32)] * 2,
        compiler_params=params(),
        cost_estimate=cost(8_000_000_000, 24_000_000),
        name="attention_back",
    )(info, own, sib, mid, dy, gain, w, wo, q, k, v, o, p)


def attn_grad_kernel(
    info, u_ref, po, oo, ps, os, dq_ref, dk_ref, dv_ref, keep_ref, got_ref, held_ref, out_ref, full, sems
):
    del held_ref
    me, it = info[0], 1 - info[0]
    sent = []
    for n in range(4):
        if n == 0:
            full[0] = dot_tn(wide(u_ref[...]), wide(dq_ref[...])).astype(BF).reshape(2, 16, 32, HALF)
        elif n == 3:
            full[n, pl.ds(me, 1)] = keep_ref[...].reshape(1, 16, 32, HALF)
            full[n, pl.ds(it, 1)] = got_ref[...].reshape(1, 16, 32, HALF)
        else:
            ref = (dk_ref, dv_ref)[n - 1]
            prev = jnp.concatenate([ref[0, :ROWS], ref[1, :ROWS]], axis=0)
            own = jnp.concatenate([ref[0, ROWS:], ref[1, ROWS:]], axis=0)
            for at_c, p_c, o_c in ((me, po, oo), (it, ps, os)):
                grad = dot_tn(wide(p_c[...]), prev) + dot_tn(wide(o_c[...]), own)
                full[n, pl.ds(at_c, 1)] = grad.astype(BF).reshape(1, 16, 32, HALF)
        at_r = pl.ds(128 + 32 * (n // 2), 32)
        at_c = pl.ds(HALF * (n % 2), HALF)
        for y in range(2):
            copy = pltpu.make_async_copy(full.at[n, y], out_ref.at[:, y, at_r, at_c], sems.at[n, y])
            copy.start()
            sent.append(copy)
    for copy in sent:
        copy.wait()


def attention_grads(info, u, po, oo, ps, os, dq, dk, dv, keep, got, held):
    return pl.pallas_call(
        attn_grad_kernel,
        out_shape=sds(held.shape, BF),
        in_specs=[SMEM] + [FULL] * 10 + [pl.BlockSpec(memory_space=pl.ANY)],
        out_specs=pl.BlockSpec(memory_space=pl.ANY),
        input_output_aliases={11: 0},
        scratch_shapes=[pltpu.VMEM((4, 2, 16, 32, HALF), BF), pltpu.SemaphoreType.DMA((4, 2))],
        compiler_params=params(),
        cost_estimate=cost(3_000_000_000, 12_000_000),
        name="attention_grads",
    )(info, u, po, oo, ps, os, dq, dk, dv, keep, got, held)


def added(left, right):
    return left.astype(F32) + right.astype(F32)


GELU_C = 0.7978845608028654
GELU_K = 0.044715


def ffn_kernel(
    info, x_ref, part_ref, sib_ref, gain_ref, dy_ref, up_ref, down_ref,
    mid_ref, keep_ref, send_ref, dz_ref, grad_ref, z_s, d_s, out_s, dz_s, gu_s, gd_s, sems,
):
    step = pl.program_id(0)
    slot = step % 2
    quarter, side = step % 4, step // 4

    def copies(slot, quarter, side):
        at_c = pl.ds(pl.multiple_of(quarter * 256, 256), 256)
        at_r = pl.ds(pl.multiple_of(side * 32, 32), 32)
        at_z = pl.ds(quarter * 4, 4)
        return (
            pltpu.make_async_copy(gu_s.at[slot], grad_ref.at[:, :, at_r, at_c], sems.at[0, slot]),
            pltpu.make_async_copy(gd_s.at[slot], grad_ref.at[at_z, side, pl.ds(64, 64), :], sems.at[1, slot]),
        )

    @pl.when(step == 0)
    def _():
        for lane in range(2):
            live = live_of(info, lane)
            branch = part_ref[lane].astype(F32) + sib_ref[lane].astype(F32)
            m = x_ref[lane].astype(F32) + live * branch
            mid_ref[lane] = m
            z_s[lane * ROWS : (lane + 1) * ROWS] = (m * rms_scale(m) * gain_ref[...]).astype(BF)
            d_s[lane * ROWS : (lane + 1) * ROWS] = (live * dy_ref[lane].astype(F32)).astype(BF)
        out_s[...] = jnp.zeros_like(out_s)
        dz_s[...] = jnp.zeros_like(dz_s)

    z, d = z_s[...], d_s[...]
    up_0, up_1 = wide(up_ref[:, 0]), wide(up_ref[:, 1])
    down = wide(down_ref[:, 0])
    f = dot(z[:, :HALF], up_0) + dot(z[:, HALF:], up_1)
    square = f * f
    t = jnp.tanh(GELU_C * f * (1.0 + GELU_K * square))
    hidden = (0.5 * f * (1.0 + t)).astype(BF)
    slope = 0.5 * (1.0 + t) + 0.5 * f * (1.0 - t * t) * (GELU_C * (1.0 + 3.0 * GELU_K * square))
    out_s[...] += dot(hidden, down)
    back = (slope * dot_nt(d, down)).astype(BF)

    @pl.when(step >= 2)
    def _():
        for c in copies(slot, quarter, side):
            c.wait()

    gd_s[slot] = dot_tn(hidden, d).astype(BF).reshape(4, 64, 1024)
    gu = dot_tn(z, back).astype(BF).reshape(2, 16, 32, 256)
    gu_s[slot, :, 0] = gu[0]
    gu_s[slot, :, 1] = gu[1]
    for c in copies(slot, quarter, side):
        c.start()
    dz_s[:, :HALF] += dot_nt(back, up_0)
    dz_s[:, HALF:] += dot_nt(back, up_1)

    @pl.when(step == pl.num_programs(0) - 1)
    def _():
        for lane in range(2):
            out = live_of(info, lane) * out_s[lane * ROWS : (lane + 1) * ROWS]
            total = out + mid_ref[lane]
            keep_ref[lane] = jnp.where(info[0] == 0, total[:128], total[128:])
            send_ref[lane] = jnp.where(info[0] == 0, out[128:], out[:128]).astype(BF)
            dz_ref[lane] = dz_s[lane * ROWS : (lane + 1) * ROWS].astype(BF)
        for k in range(2):
            for c in copies(k, quarter, side):
                c.wait()


def feed_forward(info, x, part, sib, gain, dy, weights):
    t_block = whole_block(2, ROWS, 1024)
    o_block = whole_block(2, 128, 1024)
    return pl.pallas_call(
        ffn_kernel,
        grid=(8,),
        out_shape=(
            sds((2, ROWS, 1024), F32), sds((2, 128, 1024), F32), sds((2, 128, 1024), BF),
            sds((2, ROWS, 1024), BF), sds((16, 2, 192, 1024), BF),
        ),
        in_specs=[
            SMEM, t_block, t_block, t_block, whole_block(1, 1024), t_block,
            pl.BlockSpec((16, 2, 32, 256), lambda i: (0, 0, i // 4, i % 4)),
            pl.BlockSpec((4, 1, 64, 1024), lambda i: (i % 4, i // 4, 1, 0)),
        ],
        out_specs=(
            t_block, o_block, o_block, t_block, pl.BlockSpec(memory_space=pl.ANY),
        ),
        scratch_shapes=[
            pltpu.VMEM((2 * ROWS, 1024), BF), pltpu.VMEM((2 * ROWS, 1024), BF),
            pltpu.VMEM((2 * ROWS, 1024), F32), pltpu.VMEM((2 * ROWS, 1024), F32),
            pltpu.VMEM((2, 16, 2, 32, 256), BF), pltpu.VMEM((2, 4, 64, 1024), BF),
            pltpu.SemaphoreType.DMA((2, 2)),
        ],
        compiler_params=params(),
        cost_estimate=cost(13_000_000_000, 32_000_000),
        name="feed_forward",
    )(info, x, part, sib, gain, dy, weights, weights)


STEPS = (("x", "a"), ("x", "b"), ("z", "a"), ("z", "b"), ("y", "a"))


def carry(total, rate, chip, reverse):
    lane_one = (lax.broadcasted_iota(jnp.int32, (8, 128), 0) >= 4)[None]
    entering = jnp.zeros_like(total)
    for k, (axis, kind) in enumerate(STEPS):
        other = flip(total, axis, kind)
        upper = (chip >> k) & 1
        within = chip & ((1 << k) - 1)
        if reverse:
            takes, gap = upper == 0, (1 << k) - 1 - within
        else:
            takes, gap = upper == 1, within
        reach = jnp.exp(-rate * (ROWS * gap).astype(F32)) * other
        whole = jnp.exp(-rate * float(ROWS << k))
        far = jnp.where(takes, other, total)
        near = jnp.where(takes, total, other)
        joined = whole * far + near
        if k >= 3:
            reach = jnp.where(lane_one, 0.0, reach)
            joined = jnp.where(lane_one, 0.0, joined)
        entering = entering + jnp.where(takes, reach, 0.0)
        total = joined
    return entering


def adam(factor, w_ref, f_ref, s_ref, grad, outs, rate, decay):
    clipped = grad * factor
    first_new = BETA_ONE * f_ref[...] + (1.0 - BETA_ONE) * clipped
    second_new = BETA_TWO * s_ref[...] + (1.0 - BETA_TWO) * clipped * clipped
    fix_one = 1.0 - BETA_ONE**STEP
    fix_two = 1.0 - BETA_TWO**STEP
    direction = first_new / fix_one / (jnp.sqrt(second_new / fix_two) + ADAM_EPS)
    weight = w_ref[...]
    weight_new = weight - rate * (direction + decay * weight)
    for ref, v in zip(outs, (first_new, second_new, weight_new, weight_new.astype(BF))):
        ref[...] = v


def update_kernel(info, norm, *refs):
    ins, outs = refs[:22], refs[22:]
    weights, firsts, seconds = ins[:5], ins[5:10], ins[10:15]
    a_mine, a_other, u_mine, u_other, down, state, gain = ins[15:]
    factor = jnp.minimum(1.0, CLIP_NORM / norm[0, 0])
    zero = info[0] == 0

    def pair(mine, other):
        return jnp.where(zero, mine, other), jnp.where(zero, other, mine)

    first, second = pair(a_mine[...], a_other[...])
    attn_grad = jnp.concatenate([first, second], axis=2)
    first, second = pair(u_mine[...], u_other[...])
    pieces = []
    for side in range(2):
        for k in range(16):
            at_c = slice(64 * k, 64 * k + 64)
            pieces += [first[side, :, at_c], second[side, :, at_c]]
    up_grad = jnp.concatenate(pieces, axis=1)
    grads = (attn_grad, up_grad, down[...], state[...], gain[...])
    rates = ((RATE_MATRIX, WEIGHT_DECAY),) * 3 + ((RATE_STATE, 0.0), (RATE_GAIN, 0.0))
    for k in range(5):
        adam(factor, weights[k], firsts[k], seconds[k], grads[k], outs[4 * k : 4 * k + 4], *rates[k])


def update(info, norm, weights, firsts, seconds, grads):
    shapes = []
    for w in weights:
        shapes += [sds(w.shape, F32)] * 3 + [sds(w.shape, BF)]
    return pl.pallas_call(
        update_kernel,
        out_shape=tuple(shapes),
        in_specs=[SMEM, SMEM] + [FULL] * 22,
        compiler_params=pltpu.CompilerParams(vmem_limit_bytes=24 * 1024 * 1024),
        cost_estimate=cost(4_000_000, 6_000_000),
        name="update",
    )(info, norm, *weights, *firsts, *seconds, *grads)


def body(
    tokens, cotangent, lengths, attn_weight, up_weight, down_weight, state_param, norm_gain,
    attn_first, attn_second, up_first, up_second, down_first, down_second,
    state_first, state_second, gain_first, gain_second,
):
    core = lax.axis_index("core")
    ybit = lax.axis_index("y")
    chip = (ybit * 4 + lax.axis_index("z")) * 4 + lax.axis_index("x")

    mine = jnp.concatenate(
        [state_param.astype(BF).transpose(0, 2, 1).reshape(-1), norm_gain.astype(BF).reshape(-1)]
    )
    mine = jnp.pad(mine, (0, 1024 - mine.shape[0])).reshape(1, 8, 128)
    pair = ordered(core, mine, swap(mine), 0)
    pair, tokens_now, cotangent_now = lax.optimization_barrier((pair, tokens, cotangent))
    small = lax.all_to_all(
        jnp.broadcast_to(pair[None], (32, 2, 8, 128)), CHIPS, split_axis=0, concat_axis=0, tiled=True
    ).reshape(64, 1024)
    theta = small[:, :768].reshape(64, 3, NST, 16).transpose(1, 2, 0, 3).reshape(3, NST, 1024).astype(F32)
    gains = small[:, 768:800].reshape(64, 2, 16).transpose(1, 0, 2).reshape(2, 1024).astype(F32)

    x = ordered(core, tokens_now[0], swap(tokens_now[0]), 1)
    dy = ordered(core, cotangent_now[0], swap(cotangent_now[0]), 1)
    slot_chips = SLOT // ROWS
    live_len = lax.dynamic_index_in_dim(lengths[0], chip // slot_chips, 0, keepdims=False)
    live_rows = jnp.clip(live_len - (chip % slot_chips) * ROWS, 0, ROWS)
    info = jnp.stack([core, live_rows, chip % 2]).astype(jnp.int32)

    attn_low = attn_weight.astype(BF)
    up_low = up_weight.astype(BF).reshape(16, 32, 2, 64).transpose(2, 0, 1, 3).reshape(2, 16, 2048)
    down_low = down_weight.astype(BF)
    attn_keep = lax.dynamic_slice_in_dim(attn_low, core * HALF, HALF, 2)
    attn_give = lax.dynamic_slice_in_dim(attn_low, (1 - core) * HALF, HALF, 2)
    attn_chip = ordered(core, attn_keep, swap(attn_give), 1)
    up_keep = lax.dynamic_index_in_dim(up_low, core, 0, keepdims=False)
    up_give = lax.dynamic_index_in_dim(up_low, 1 - core, 0, keepdims=False)
    up_chip = ordered(core, up_keep, swap(up_give), 0)
    up_chip = up_chip.reshape(32, 2, 1024).transpose(1, 0, 2).reshape(64, 1024)
    attn_rows = attn_chip.reshape(2, 2, 32, HALF).transpose(0, 2, 1, 3).reshape(64, 1024)
    all_chip = jnp.concatenate([up_chip, down_low, attn_rows], axis=0)
    all_chip, pair = lax.optimization_barrier((all_chip, pair))
    all_two = ordered(ybit, all_chip[None], flip(all_chip, "y")[None], 0)
    full = lax.all_gather(all_two, ("z", "x"), axis=0)
    wo_give = lax.dynamic_slice(full, (0, 1 - core, 160, HALF), (16, 1, 32, HALF)).reshape(16, 32, HALF)
    wo_got = swap(wo_give)

    theta_c = lax.dynamic_slice_in_dim(theta, core * HALF, HALF, 2).reshape(3, NST, 4, 128)
    theta_c = jnp.concatenate([theta_c, theta_c], axis=2)
    rate = jnp.exp(theta_c[0]) / BLOCK
    decay = jnp.exp(-rate)
    norm_scale = jnp.sqrt(-jnp.expm1(-2.0 * rate))
    cb = norm_scale * theta_c[1] * theta_c[2]

    u_low, us, ended = first(info, x, gains[:1], decay)
    entering = carry(ended, rate, chip, False)
    entering, dy = lax.optimization_barrier((entering, dy))
    sb_own = state_run(us, decay, cb, entering)
    sb_sib = swap(sb_own)
    prev_own = lax.ppermute(sb_own, "x", [(0, 1), (2, 3)])
    prev_sib = swap(prev_own)

    part, q, k, v, o, p = attention(info, u_low, prev_own, sb_own, prev_sib, sb_sib, full, wo_got)
    middle, out_keep, out_send, dz_part, ffn_grad = feed_forward(
        info, x, part, swap(part), gains[1:], dy, full
    )
    dm, gain_two_grad, keep, send, dq, dk, dv, wo_keep, wo_send = attention_back(
        info, dz_part, swap(dz_part), middle, dy, gains[1:], full, wo_got, q, k, v, o, p
    )
    got = swap(send)
    back = added(keep[:, :ROWS], got[:, :ROWS]).astype(BF)
    back = lax.ppermute(back, "x", [(1, 0), (3, 2)])
    ds, started = state_turn(keep, got, back, decay)
    grad = attention_grads(
        info, u_low, prev_own, sb_own, prev_sib, sb_sib, dq, dk, dv, wo_keep, swap(wo_send), ffn_grad
    )
    grad_part = lax.psum_scatter(
        grad.reshape(6144, 1024), ("z", "x"), scatter_dimension=0, tiled=True
    ).reshape(2, 192, 1024)
    started, grad = lax.optimization_barrier((started, grad))
    leaving = carry(started, rate, chip, True)
    du_mine, du_give, qu, rr, gain_one_grad = state_back(
        info, us, ds, decay, cb, entering, leaving, keep, got, x
    )

    mine_y = lax.dynamic_index_in_dim(grad_part, ybit, 0, keepdims=False)
    give_y = lax.dynamic_index_in_dim(grad_part, 1 - ybit, 0, keepdims=False)
    near = added(mine_y, flip(give_y, "y"))
    cross = lax.ppermute(give_y, ("grp", "y"), [(0, 3), (3, 0), (1, 2), (2, 1)])
    grad_sum = near + added(flip(mine_y, "grp"), cross)
    up_sum, down_sum = grad_sum[:64].reshape(2, 32, 1024), grad_sum[64:128]
    attn_sum = grad_sum[128:].reshape(2, 32, 2, HALF).transpose(0, 2, 1, 3).reshape(4, 32, HALF)

    output = (out_keep + swap(out_send).astype(F32)).astype(BF)

    du_own = ordered(core, du_mine, swap(du_give), 2)
    x_own = tokens[0].astype(F32)
    dm_own = lax.dynamic_slice_in_dim(dm, core * 128, 128, 1)
    token_grad = (norm_back(du_own, x_own, rms_scale(x_own), gains[0]) + dm_own).astype(BF)

    lanes = jnp.stack([qu, rr]).reshape(2, NST, 2, HALF).sum(axis=2).reshape(2 * NST, HALF)
    gain_two_half = lax.dynamic_slice_in_dim(gain_two_grad, core * HALF, HALF, 1)
    lanes = jnp.concatenate([lanes, gain_one_grad, gain_two_half], axis=0)
    packed = lanes.reshape(34, 32, 16).transpose(1, 0, 2)
    small_got = lax.all_to_all(packed, CHIPS, split_axis=0, concat_axis=0, tiled=True)
    small_sum = jnp.sum(small_got, axis=0)
    small_sum = small_sum + flip(small_sum, "grp")
    hand = []
    for j in range(32):
        for c in range(2):
            hand.append((j * 2 + c, c * 32 + j))
    mine_sum = lax.ppermute(small_sum, SHARD, hand)

    t_own = state_param.astype(BF).astype(F32).transpose(0, 2, 1)
    rate_o = jnp.exp(t_own[0]) / BLOCK
    decay_o = jnp.exp(-rate_o)
    scale_o = jnp.sqrt(-jnp.expm1(-2.0 * rate_o))
    b_o = scale_o * t_own[1]
    qu_o, rr_o = mine_sum[:NST], mine_sum[NST : 2 * NST]
    gb = t_own[2] * qu_o
    log_rate_grad = rate_o * (
        -decay_o * t_own[2] * b_o * rr_o + decay_o * decay_o / scale_o * t_own[1] * gb
    )
    state_grad = jnp.stack([log_rate_grad, scale_o * gb, b_o * qu_o]).transpose(0, 2, 1)
    gain_grad = mine_sum[2 * NST :]

    def split_rows(v, axis):
        keep = lax.dynamic_slice_in_dim(v, core * 16, 16, axis)
        give = lax.dynamic_slice_in_dim(v, (1 - core) * 16, 16, axis)
        return keep, swap(give)

    up_mine, up_theirs = split_rows(up_sum, 1)
    attn_mine, attn_theirs = split_rows(attn_sum, 1)

    squares = F32(0.0)
    for piece in (grad_sum, state_grad, gain_grad):
        squares = squares + jnp.sum(piece * piece)
    squares = jnp.broadcast_to(squares, (1, 128))
    squares = squares + swap(squares)
    every = lax.all_to_all(
        jnp.broadcast_to(squares, (32, 128)), CHIPS, split_axis=0, concat_axis=0, tiled=True
    )
    grad_norm = jnp.sqrt(jnp.sum(every[:, 0]))
    grad_norm, output, token_grad = lax.optimization_barrier((grad_norm, output, token_grad))
    new = update(
        info, grad_norm.reshape(1, 1),
        (attn_weight, up_weight, down_weight, state_param, norm_gain),
        (attn_first, up_first, down_first, state_first, gain_first),
        (attn_second, up_second, down_second, state_second, gain_second),
        (attn_mine, attn_theirs, up_mine, up_theirs, down_sum, state_grad, gain_grad),
    )
    return (output[None], token_grad[None], grad_norm) + tuple(new)


def solution(mesh):
    inner = Mesh(mesh.devices.reshape(2, 2, 4, 4, 2), AXES)
    rows = P("grp", None, SHARD, None)
    attn = P(None, SHARD, None)
    flat = P(SHARD, None)
    gain = P(None, SHARD)
    in_specs = (rows, rows, P("grp", None), attn, flat, flat, attn, gain)
    in_specs += (attn, attn, flat, flat, flat, flat, attn, attn, gain, gain)
    out_specs = (rows, rows, P()) + (attn,) * 4 + (flat,) * 8 + (attn,) * 4 + (gain,) * 4
    return jax.shard_map(body, mesh=inner, in_specs=in_specs, out_specs=out_specs, check_vma=False)
```

```python
import jax
import jax.numpy as jnp
from jax import lax
from jax.experimental import pallas as pl
from jax.experimental.pallas import tpu as pltpu
from jax.sharding import Mesh
from jax.sharding import PartitionSpec as P

HEAD_DIM = 128
BLOCK = 512
STEP = 5
SLOT = 2048

EPS_NORM = 1e-05
BETA_ONE = 0.5
BETA_TWO = 0.5
ADAM_EPS = 1e-08
WEIGHT_DECAY = 0.1
CLIP_NORM = 0.5
RATE_MATRIX = 0.02
RATE_STATE = 1.0
RATE_GAIN = 0.6
MASKED = -1e30

AXES = ("grp", "y", "z", "x", "core")
CHIPS = ("y", "z", "x")
SHARD = ("y", "z", "x", "core")
BF = jnp.bfloat16
F32 = jnp.float32
NST = 16
ROWS = 256
HALF = 512


def flip(v, axis, kind="a"):
    if lax.axis_size(axis) == 2:
        pairs = [(0, 1), (1, 0)]
    elif kind == "c":
        pairs = [(0, 2), (2, 0), (1, 3), (3, 1)]
    elif kind == "a":
        pairs = [(0, 1), (1, 0), (2, 3), (3, 2)]
    else:
        pairs = [(0, 3), (3, 0), (1, 2), (2, 1)]
    return lax.ppermute(v, axis, pairs)


def swap(v):
    return flip(v, "core")


def ordered(bit, own, other, axis):
    first = jnp.where(bit == 0, own, other)
    second = jnp.where(bit == 0, other, own)
    return jnp.concatenate([first, second], axis=axis)


def rms_scale(value):
    return lax.rsqrt(jnp.mean(value * value, axis=-1, keepdims=True) + EPS_NORM)


def norm_back(grad, value, inverse, gain):
    unit = value * inverse
    scaled = grad * gain
    return inverse * (scaled - unit * jnp.mean(scaled * unit, axis=-1, keepdims=True))


def dot(left, right):
    return jnp.dot(left, right, preferred_element_type=F32)


def dot_nt(left, right):
    return lax.dot_general(left, right, (((1,), (1,)), ((), ())), preferred_element_type=F32)


def dot_tn(left, right):
    return lax.dot_general(left, right, (((0,), (0,)), ((), ())), preferred_element_type=F32)


def params(mib=16):
    return pltpu.CompilerParams(vmem_limit_bytes=mib * 1024 * 1024)


BIG = 60


def cost(flops, bytes_accessed):
    return pl.CostEstimate(flops=flops, bytes_accessed=bytes_accessed, transcendentals=0)


def sds(shape, dtype):
    return jax.ShapeDtypeStruct(shape, dtype)


SMEM = pl.BlockSpec(memory_space=pltpu.SMEM)
FULL = pl.BlockSpec(memory_space=pltpu.VMEM)


def live_of(info, half):
    return (lax.broadcasted_iota(jnp.int32, (ROWS, 1), 0) + half * ROWS < info[1]).astype(F32)


def at(ref, t):
    return ref[pl.ds(t, 8, stride=ROWS), :]


def tree(terms):
    while len(terms) > 1:
        terms = [terms[i] + terms[i + 1] for i in range(0, len(terms), 2)]
    return terms[0]


def first_kernel(info, x_ref, gain_ref, a_ref, low_ref, us_ref, e_ref, f_ref):
    for lane in range(2):
        x = x_ref[lane].astype(F32)
        unit = x * rms_scale(x)
        low_ref[lane] = (unit * gain_ref[...]).astype(BF)
        half = jnp.where(info[0] == 0, unit[:, :HALF], unit[:, HALF:])
        for g in range(4):
            us_ref[pl.ds((lane * 4 + g) * ROWS, ROWS), :] = half[:, g * 128 : (g + 1) * 128]
    half = NST // 2
    for base in (0, half):
        a = [a_ref[base + n] for n in range(half)]

        def step(t, held):
            e, f = held
            u = at(us_ref, t)
            f = tuple(a[n] * (f[n] + e[n]) for n in range(half))
            e = tuple(a[n] * e[n] + u for n in range(half))
            return e, f

        zero = tuple(jnp.zeros((8, 128), F32) for _ in range(half))
        e, f = lax.fori_loop(0, ROWS, step, (zero, zero), unroll=4)
        for n in range(half):
            e_ref[base + n] = e[n]
            f_ref[base + n] = f[n]


STATE = sds((NST, 8, 128), F32)
SPREAD = sds((8 * ROWS, 128), F32)


def first(info, x, gain, a):
    return pl.pallas_call(
        first_kernel,
        out_shape=(sds((2, ROWS, 1024), BF), SPREAD, STATE, STATE),
        in_specs=[SMEM, FULL, FULL, FULL],
        compiler_params=params(),
        cost_estimate=cost(32_000_000, 3_000_000),
        name="first",
    )(info, x, gain, a)


def run_kernel(us, a_ref, cb_ref, h_ref, s_ref, ss):
    def step(t, h):
        u = at(us, t)
        h = tuple(a_ref[n] * h[n] + u for n in range(NST))
        ss[pl.ds(t, 8, stride=ROWS), :] = tree([cb_ref[n] * h[n] for n in range(NST)])
        return h

    lax.fori_loop(0, ROWS, step, tuple(h_ref[n] for n in range(NST)), unroll=4)
    for lane in range(2):
        for g in range(4):
            s_ref[lane, :, g * 128 : (g + 1) * 128] = ss[pl.ds((lane * 4 + g) * ROWS, ROWS), :].astype(BF)


def state_run(us, a, cb, h):
    return pl.pallas_call(
        run_kernel,
        out_shape=sds((2, ROWS, HALF), BF),
        scratch_shapes=[pltpu.VMEM((8 * ROWS, 128), F32)],
        compiler_params=params(),
        cost_estimate=cost(32_000_000, 2_000_000),
        name="state_run",
    )(us, a, cb, h)


def turn_kernel(keep_ref, got_ref, a_ref, ds_ref, e_ref):
    for half in range(2):
        d = added(keep_ref[0, half], got_ref[0, half])
        for g in range(4):
            ds_ref[pl.ds((half * 4 + g) * ROWS, ROWS), :] = d[:, g * 128 : (g + 1) * 128]
    a = [a_ref[n] for n in range(NST)]

    def step(i, h):
        d = at(ds_ref, ROWS - 1 - i)
        return tuple(a[n] * h[n] + d for n in range(NST))

    h = lax.fori_loop(0, ROWS, step, tuple(jnp.zeros((8, 128), F32) for _ in range(NST)), unroll=4)
    for n in range(NST):
        e_ref[n] = h[n]


def state_turn(keep, got, a):
    return pl.pallas_call(
        turn_kernel,
        out_shape=(SPREAD, STATE),
        compiler_params=params(),
        cost_estimate=cost(16_000_000, 4_000_000),
        name="state_turn",
    )(keep, got, a)


def mid_kernel(base, us, ds, a_ref, cb_ref, h_ref, dus_in, dus, qu_ref, r_ref):
    half = NST // 2
    a = [a_ref[base + n] for n in range(half)]

    def step(i, held):
        q, v, qu, r = held
        t = ROWS - 1 - i
        u, d = at(us, t), at(ds, t)
        v = tuple(a[n] * v[n] + q[n] for n in range(half))
        q = tuple(a[n] * q[n] + d for n in range(half))
        du = tree([cb_ref[base + n] * q[n] for n in range(half)])
        dus[pl.ds(t, 8, stride=ROWS), :] = at(dus_in, t) + du
        qu = tuple(qu[n] + q[n] * u for n in range(half))
        r = tuple(r[n] + v[n] * u for n in range(half))
        return (q, v, qu, r)

    zero = tuple(jnp.zeros((8, 128), F32) for _ in range(half))
    q, v, qu, r = lax.fori_loop(0, ROWS, step, (zero,) * 4, unroll=2)
    for n in range(half):
        qu_ref[n] = qu[n]
        r_ref[n] = r[n] + h_ref[base + n] * (a[n] * v[n] + q[n])


def mid_first_kernel(us, ds, a_ref, cb_ref, h_ref, keep_ref, got_ref, dus, qu_ref, r_ref, g_ref, dq):
    for half in range(2):
        du = added(keep_ref[1, half], got_ref[1, half])
        for g in range(4):
            k = half * 4 + g
            piece = du[:, g * 128 : (g + 1) * 128]
            dq[pl.ds(k * ROWS, ROWS), :] = piece
            g_ref[k : k + 1, :] = jnp.sum(piece * us[pl.ds(k * ROWS, ROWS), :], axis=0, keepdims=True)
    mid_kernel(0, us, ds, a_ref, cb_ref, h_ref, dq, dus, qu_ref, r_ref)


def state_mid(us, ds, a, cb, h, keep, got):
    part = sds((NST // 2, 8, 128), F32)
    return pl.pallas_call(
        mid_first_kernel,
        out_shape=(SPREAD, part, part, sds((8, 128), F32)),
        scratch_shapes=[pltpu.VMEM((8 * ROWS, 128), F32)],
        compiler_params=params(),
        cost_estimate=cost(40_000_000, 4_000_000),
        name="state_mid_0",
    )(us, ds, a, cb, h, keep, got)


def state_mid_more(us, ds, a, cb, h, dus):
    part = sds((NST // 2, 8, 128), F32)
    return pl.pallas_call(
        lambda *refs: mid_kernel(NST // 2, *refs),
        out_shape=(SPREAD, part, part),
        compiler_params=params(),
        cost_estimate=cost(40_000_000, 4_000_000),
        name="state_mid_1",
    )(us, ds, a, cb, h, dus)


def fix_kernel(info, q_ref, a_ref, cb_ref, e_ref, f_ref, h_ref, far_ref, qu_0, qu_1, r_0, r_1, g_ref, gain, gain_two, out):
    half = NST // 2

    def halved(v):
        return jnp.where(info[0] == 0, v[:, :HALF], v[:, HALF:])

    def put(row, v, scale):
        both = v[:4] + v[4:]
        for g in range(4):
            at_c = slice(g * 128, (g + 1) * 128)
            value = both[g : g + 1]
            out[row : row + 1, at_c] = value * scale[:, at_c] if scale is not None else value

    gain_c = halved(gain[...])
    total = g_ref[...]
    for n in range(NST):
        q = q_ref[n]
        qu = (qu_0, qu_1)[n // half][n % half] + q * a_ref[n] * e_ref[n]
        r = (r_0, r_1)[n // half][n % half] + q * (f_ref[n] + h_ref[n] * (float(ROWS) * far_ref[n]))
        total = total + cb_ref[n] * qu
        put(n, qu, gain_c)
        put(NST + n, r, gain_c)
    put(2 * NST, total, None)
    out[2 * NST + 1 :] = halved(gain_two[...])


def state_fix(info, q, a, cb, e, f, h, far, qu, r, g, gain, gain_two):
    return pl.pallas_call(
        fix_kernel,
        out_shape=sds((2 * NST + 2, HALF), F32),
        in_specs=[SMEM] + [FULL] * 14,
        compiler_params=params(),
        cost_estimate=cost(1_000_000, 1_000_000),
        name="state_fix",
    )(info, q, a, cb, e, f, h, far, *qu, *r, g, gain, gain_two)


def last_kernel(info, dus, a_ref, cb_ref, q_ref, mine_ref, give_ref, out):
    def step(i, q):
        t = ROWS - 1 - i
        q = tuple(a_ref[n] * q[n] for n in range(NST))
        out[pl.ds(t, 8, stride=ROWS), :] = at(dus, t) + tree([cb_ref[n] * q[n] for n in range(NST)])
        return q

    lax.fori_loop(0, ROWS, step, tuple(q_ref[n] for n in range(NST)), unroll=4)
    mine = pl.multiple_of(info[0] * 128, 128)
    give = pl.multiple_of((1 - info[0]) * 128, 128)
    for lane in range(2):
        for g in range(4):
            base = (lane * 4 + g) * ROWS
            at_c = slice(g * 128, (g + 1) * 128)
            mine_ref[lane, :, at_c] = out[pl.ds(base + mine, 128), :]
            give_ref[lane, :, at_c] = out[pl.ds(base + give, 128), :]


def state_last(info, dus, a, cb, q):
    half = sds((2, 128, HALF), F32)
    return pl.pallas_call(
        last_kernel,
        out_shape=(half, half),
        in_specs=[SMEM] + [FULL] * 4,
        scratch_shapes=[pltpu.VMEM((8 * ROWS, 128), F32)],
        compiler_params=params(),
        cost_estimate=cost(32_000_000, 2_000_000),
        name="state_last",
    )(info, dus, a, cb, q)


def added(left, right):
    return left.astype(F32) + right.astype(F32)


def wide(v):
    return v.reshape(v.shape[0] * v.shape[1], v.shape[2])


class Weights:
    def __init__(self, info, full_ref, w, sems):
        self.y, self.full, self.w, self.sems = info[3], full_ref, w, sems
        self.copies = {}

    def start(self, order):
        for n in order:
            rows, cols = pl.ds(128 + 32 * (n // 2), 32), pl.ds(HALF * (n % 2), HALF)
            self.copies[n] = [
                pltpu.make_async_copy(self.full.at[:, r, rows, cols], self.w.at[n, r], self.sems.at[n, r])
                for r in range(2)
            ]
            for c in self.copies[n]:
                c.start()

    def wait(self, n):
        for c in self.copies[n]:
            c.wait()

    def half(self, n, half):
        return wide(self.w[n, half ^ self.y])

    def out(self, half):
        return wide(self.w[3, half])


WEIGHTS = [pltpu.VMEM((4, 2, 16, 32, HALF), BF), pltpu.SemaphoreType.DMA((4, 2))]
HBM = pl.BlockSpec(memory_space=pltpu.HBM)


def bring(pairs, sems):
    sems = sems if isinstance(sems, list) else [sems.at[n] for n in range(len(pairs))]
    copies = [pltpu.make_async_copy(src, dst, sem) for (src, dst), sem in zip(pairs, sems)]
    for copy in copies:
        copy.start()
    return copies


INPUTS = [pltpu.VMEM((2, ROWS, 1024), BF)] + [pltpu.VMEM((2 * ROWS, HALF), BF)] * 2 + [pltpu.SemaphoreType.DMA((6,))]


def attn_kernel(
    info, u_in, own_in, sib_in, full_ref, part_ref, q_out, k_out, v_out, o_out, p_out,
    q_ref, k_ref, v_ref, o_ref, p_ref, out_sems, w_s, sems, u_ref, own, sib, in_sems,
):
    w = Weights(info, full_ref, w_s, sems)
    w.start((0,))
    arriving = bring(((u_in, u_ref), (own_in, own), (sib_in, sib)), in_sems)
    w.start((1, 2, 3))
    me, it = info[0], 1 - info[0]
    leaving = []

    def leave(src, dst, *place):
        copy = pltpu.make_async_copy(src, dst, out_sems.at[place])
        copy.start()
        leaving.append(copy)

    arriving[0].wait()
    w.wait(0)
    for half in range(2):
        u = u_ref[half]
        q_ref[half] = (dot(u[:, :HALF], w.half(0, 0)) + dot(u[:, HALF:], w.half(0, 1))).astype(BF)
    leave(q_ref, q_out, 0, 0)
    for copy in arriving[1:]:
        copy.wait()
    for n, ref, out in ((1, k_ref, k_out), (2, v_ref, v_out)):
        w.wait(n)
        ref[...] = (dot(own[...], w.half(n, me)) + dot(sib[...], w.half(n, it))).astype(BF)
        leave(ref, out, n, 0)
    w.wait(3)
    for half in range(2):
        seen = ROWS * (half + 1)
        row = lax.broadcasted_iota(jnp.int32, (ROWS, seen), 0) + half * ROWS
        allowed = lax.broadcasted_iota(jnp.int32, (ROWS, seen), 1) <= row
        for h in range(4):
            at_h = slice(h * HEAD_DIM, (h + 1) * HEAD_DIM)
            s = dot_nt(q_ref[half, :, at_h], k_ref[:seen, at_h]) * HEAD_DIM**-0.5
            s = jnp.where(allowed, s, MASKED)
            e = jnp.exp(s - jnp.max(s, axis=-1, keepdims=True))
            p = (e / jnp.sum(e, axis=-1, keepdims=True)).astype(BF)
            p_ref[half, h, :, :seen] = p
            o_ref[half, :, at_h] = dot(p, v_ref[:seen, at_h]).astype(BF)
        leave(p_ref.at[half], p_out.at[half], 3, half)
        leave(o_ref.at[half], o_out.at[half], 4, half)
        o = o_ref[half]
        for side in range(2):
            part_ref[half, :, side * HALF : (side + 1) * HALF] = dot(o, w.out(side)).astype(BF)
    for copy in leaving:
        copy.wait()


KEPT = [
    pltpu.VMEM((2, ROWS, HALF), BF), pltpu.VMEM((2 * ROWS, HALF), BF), pltpu.VMEM((2 * ROWS, HALF), BF),
    pltpu.VMEM((2, ROWS, HALF), BF), pltpu.VMEM((2, 4, ROWS, 2 * ROWS), BF), pltpu.SemaphoreType.DMA((5, 2)),
]


def attention(info, u, own, sib, full):
    return pl.pallas_call(
        attn_kernel,
        out_shape=(
            sds((2, ROWS, 1024), BF), sds((2, ROWS, HALF), BF), sds((2 * ROWS, HALF), BF),
            sds((2 * ROWS, HALF), BF), sds((2, ROWS, HALF), BF), sds((2, 4, ROWS, 2 * ROWS), BF),
        ),
        in_specs=[SMEM] + [HBM] * 4,
        out_specs=(FULL, HBM, HBM, HBM, HBM, HBM),
        scratch_shapes=KEPT + WEIGHTS + INPUTS,
        compiler_params=params(BIG),
        cost_estimate=cost(4_000_000_000, 16_000_000),
        name="attention",
    )(info, u, own, sib, full)


def attn_back_kernel(
    info, own_in, sib_in, mid_in, dy_in, gain_ref, full_ref, q_in, k_in, v_in, o_in, p_in,
    os_in, u_in, so_in, ss_in, held_ref, dm_out, g_ref, dq_out, dk_out, dv_out, grad_ref,
    q_ref, k_ref, v_ref, o_ref, p_ref, in_sems, w_s, sems, grads, out_sems,
    u_ref, s_own, s_sib, late_sems, os_ref, own_ref, sib_ref, mid_ref, dy_ref, dm_ref, first_sems,
    dq_ref, dk_ref, dv_ref, made_sems,
):
    del held_ref
    early = []
    for lane in range(2):
        pairs = ((own_in, own_ref), (sib_in, sib_ref), (mid_in, mid_ref), (dy_in, dy_ref))
        early.append(bring([(a.at[lane], b.at[lane]) for a, b in pairs], first_sems.at[lane]))
    w = Weights(info, full_ref, w_s, sems)
    w.start((3,))
    pairs = ((v_in, v_ref), (p_in, p_ref), (k_in, k_ref), (q_in, q_ref), (o_in, o_ref))
    arriving = bring(pairs, [in_sems.at[n, 0] for n in range(5)])
    late = bring(((u_in, u_ref), (so_in, s_own), (ss_in, s_sib), (os_in, os_ref)), late_sems)
    me, it = info[0], 1 - info[0]
    scale = HEAD_DIM**-0.5
    gain_grad = jnp.zeros((1, 1024), F32)
    branches = []
    leaving = []

    def leave(src, dst, sem):
        copy = pltpu.make_async_copy(src, dst, sem)
        copy.start()
        leaving.append(copy)

    for lane in range(2):
        for copy in early[lane]:
            copy.wait()
        m = mid_ref[lane]
        dz = added(own_ref[lane], sib_ref[lane])
        inverse = rms_scale(m)
        unit = m * inverse
        gain_grad = gain_grad + jnp.sum(dz * unit, axis=0, keepdims=True)
        scaled = dz * gain_ref[...]
        dm = dy_ref[lane].astype(F32) + inverse * (
            scaled - unit * jnp.mean(scaled * unit, axis=-1, keepdims=True)
        )
        dm_ref[lane] = dm
        leave(dm_ref.at[lane], dm_out.at[lane], made_sems.at[0, lane])
        branch = (live_of(info, lane) * dm).astype(BF)
        branches.append(branch)
    g_ref[...] = gain_grad
    w.wait(3)
    for copy in arriving:
        copy.wait()
    d_o = []
    for half in range(2):
        branch = branches[half]
        d_o.append((dot_nt(branch[:, :HALF], w.out(0)) + dot_nt(branch[:, HALF:], w.out(1))).astype(BF))
    for h in range(4):
        at_h = slice(h * HEAD_DIM, (h + 1) * HEAD_DIM)
        dk, dv = [], []
        for half in range(2):
            seen = ROWS * (half + 1)
            p_low = p_ref[half, h, :, :seen]
            p = p_low.astype(F32)
            d_o_h = d_o[half][:, at_h]
            dp = dot_nt(d_o_h, v_ref[:seen, at_h])
            total = jnp.sum(p * dp, axis=-1, keepdims=True)
            ds = (p * (dp - total)).astype(BF)
            dq_ref[half, :, at_h] = (dot(ds, k_ref[:seen, at_h]) * scale).astype(BF)
            dk.append(dot_tn(ds, q_ref[half, :, at_h]))
            dv.append(dot_tn(p_low, d_o_h))
        for ref, parts, factor in ((dk_ref, dk, scale), (dv_ref, dv, 1.0)):
            ref[:ROWS, at_h] = ((parts[0] + parts[1][:ROWS]) * factor).astype(BF)
            ref[ROWS:, at_h] = (parts[1][ROWS:] * factor).astype(BF)
    for n, (src, dst) in enumerate(((dq_ref, dq_out), (dk_ref, dk_out), (dv_ref, dv_out))):
        leave(src, dst, made_sems.at[1 + n, 0])

    def leave_grad(n):
        at_r, at_c = pl.ds(128 + 32 * (n // 2), 32), pl.ds(HALF * (n % 2), HALF)
        for y in range(2):
            leave(grads.at[n, y], grad_ref.at[:, y ^ info[3], at_r, at_c], out_sems.at[n, y])

    def put(n, half, value):
        grads[n, pl.ds(half, 1)] = value.astype(BF).reshape(1, 16, 32, HALF)

    for copy in late:
        copy.wait()
    branch = jnp.concatenate(branches, axis=0)
    branch = jnp.where(info[0] == 0, branch[:, :HALF], branch[:, HALF:])
    for half, ref in ((me, o_ref), (it, os_ref)):
        put(3, half, dot_tn(wide(ref[...]), branch))
    leave_grad(3)
    for n, ref in ((1, dk_ref), (2, dv_ref)):
        for half, s_c in ((me, s_own), (it, s_sib)):
            put(n, half, dot_tn(s_c[...], ref[...]))
        leave_grad(n)
    for half in range(2):
        put(0, half, dot_tn(wide(u_ref[...])[:, half * HALF : (half + 1) * HALF], wide(dq_ref[...])))
    leave_grad(0)
    for copy in leaving:
        copy.wait()


def attention_back(info, own, sib, mid, dy, gain, full, q, k, v, o, p, o_sib, u, s_own, s_sib, held):
    return pl.pallas_call(
        attn_back_kernel,
        out_shape=(
            sds((2, ROWS, 1024), F32), sds((1, 1024), F32), sds((2, ROWS, HALF), BF),
            sds((2 * ROWS, HALF), BF), sds((2 * ROWS, HALF), BF), sds(held.shape, BF),
        ),
        in_specs=[SMEM] + [HBM] * 4 + [FULL] + [HBM] * 11,
        out_specs=(HBM, FULL, HBM, HBM, HBM, HBM),
        input_output_aliases={16: 5},
        scratch_shapes=KEPT + WEIGHTS + WEIGHTS + INPUTS + [
            pltpu.VMEM((2, ROWS, HALF), BF), pltpu.VMEM((2, ROWS, 1024), BF), pltpu.VMEM((2, ROWS, 1024), BF),
            pltpu.VMEM((2, ROWS, 1024), F32), pltpu.VMEM((2, ROWS, 1024), BF), pltpu.VMEM((2, ROWS, 1024), F32),
            pltpu.SemaphoreType.DMA((2, 4)),
            pltpu.VMEM((2, ROWS, HALF), BF), pltpu.VMEM((2 * ROWS, HALF), BF), pltpu.VMEM((2 * ROWS, HALF), BF),
            pltpu.SemaphoreType.DMA((4, 2)),
        ],
        compiler_params=params(BIG),
        cost_estimate=cost(6_000_000_000, 24_000_000),
        name="attention_back",
    )(info, own, sib, mid, dy, gain, full, q, k, v, o, p, o_sib, u, s_own, s_sib, held)


def inputs_back_kernel(
    info, dq_in, dk_in, dv_in, full_ref, keep_ref, send_ref, w_s, sems, dq_ref, dk_ref, dv_ref, in_sems
):
    w = Weights(info, full_ref, w_s, sems)
    w.start((1, 2))
    arriving = bring(((dk_in, dk_ref), (dv_in, dv_ref), (dq_in, dq_ref)), in_sems)
    w.start((0,))
    for copy in arriving:
        copy.wait()
    for n in (1, 2):
        w.wait(n)
    for ref, half in ((send_ref, 1 - info[0]), (keep_ref, info[0])):
        ds = dot_nt(dk_ref[...], w.half(1, half)) + dot_nt(dv_ref[...], w.half(2, half))
        ref[0] = ds.astype(BF).reshape(2, ROWS, HALF)
    w.wait(0)
    for ref, half in ((send_ref, 1 - info[0]), (keep_ref, info[0])):
        ref[1] = dot_nt(wide(dq_ref[...]), w.half(0, half)).astype(BF).reshape(2, ROWS, HALF)


def inputs_back(info, dq, dk, dv, full):
    return pl.pallas_call(
        inputs_back_kernel,
        out_shape=(sds((2, 2, ROWS, HALF), BF), sds((2, 2, ROWS, HALF), BF)),
        in_specs=[SMEM] + [HBM] * 4,
        scratch_shapes=WEIGHTS + [
            pltpu.VMEM((2, ROWS, HALF), BF), pltpu.VMEM((2 * ROWS, HALF), BF), pltpu.VMEM((2 * ROWS, HALF), BF),
            pltpu.SemaphoreType.DMA((3,)),
        ],
        compiler_params=params(BIG),
        cost_estimate=cost(2_000_000_000, 7_000_000),
        name="inputs_back",
    )(info, dq, dk, dv, full)


GELU_C = 0.7978845608028654
GELU_K = 0.044715


def ffn_kernel(
    info, x_in, part_in, sib_in, gain_ref, dy_in, up_ref, down_ref,
    mid_out, keep_ref, send_ref, dz_ref, grad_ref, z_s, d_s, out_s, dz_s, gu_s, gd_s, sems,
    x_ref, part_ref, sib_ref, dy_ref, mid_ref, in_sems, mid_sems,
):
    step = pl.program_id(0)

    def mid_copy(k):
        return pltpu.make_async_copy(mid_ref.at[k], mid_out.at[k], mid_sems.at[k])

    slot = step % 2
    place, near = step % 2, step // 2
    side = near ^ info[3]

    def copies(slot, place, near):
        at_c = pl.ds(pl.multiple_of(place * HALF, HALF), HALF)
        at_r = pl.ds(pl.multiple_of((near ^ info[3]) * 32, 32), 32)
        at_z = pl.ds(place * 8, 8)
        return (
            pltpu.make_async_copy(gu_s.at[slot], grad_ref.at[:, :, at_r, at_c], sems.at[0, slot]),
            pltpu.make_async_copy(gd_s.at[slot], grad_ref.at[at_z, near, pl.ds(64, 64), :], sems.at[1, slot]),
        )

    @pl.when(step == 0)
    def _():
        arriving = []
        for lane in range(2):
            pairs = ((part_in, part_ref), (sib_in, sib_ref), (x_in, x_ref), (dy_in, dy_ref))
            arriving.append(bring([(a.at[lane], b.at[lane]) for a, b in pairs], in_sems.at[lane]))
        for lane in range(2):
            for copy in arriving[lane]:
                copy.wait()
            live = live_of(info, lane)
            m = x_ref[lane].astype(F32) + live * added(part_ref[lane], sib_ref[lane])
            mid_ref[lane] = m
            mid_copy(lane).start()
            z_s[lane * ROWS : (lane + 1) * ROWS] = (m * rms_scale(m) * gain_ref[...]).astype(BF)
            d_s[lane * ROWS : (lane + 1) * ROWS] = (live * dy_ref[lane].astype(F32)).astype(BF)
        out_s[...] = jnp.zeros_like(out_s)
        dz_s[...] = jnp.zeros_like(dz_s)

    z, d = z_s[...], d_s[...]
    up_0, up_1 = (up_ref[:, pl.ds(y ^ info[3], 1)].reshape(HALF, HALF) for y in range(2))
    down = wide(down_ref[:, 0])
    f = dot(z[:, :HALF], up_0) + dot(z[:, HALF:], up_1)
    square = f * f
    t = jnp.tanh(GELU_C * f * (1.0 + GELU_K * square))
    hidden = (0.5 * f * (1.0 + t)).astype(BF)
    slope = 0.5 * (1.0 + t) + 0.5 * f * (1.0 - t * t) * (GELU_C * (1.0 + 3.0 * GELU_K * square))
    out_s[...] += dot(hidden, down)
    back = (slope * dot_nt(d, down)).astype(BF)

    @pl.when(step >= 2)
    def _():
        for c in copies(slot, place, near):
            c.wait()

    gd_s[slot] = dot_tn(hidden, d).astype(BF).reshape(8, 64, 1024)
    gu = dot_tn(z, back).astype(BF).reshape(2, 16, 32, HALF)
    for y in range(2):
        gu_s[slot, :, pl.ds(y ^ info[3], 1)] = gu[y].reshape(16, 1, 32, HALF)
    for c in copies(slot, place, near):
        c.start()
    dz_s[:, :HALF] += dot_nt(back, up_0)
    dz_s[:, HALF:] += dot_nt(back, up_1)

    @pl.when(step == pl.num_programs(0) - 1)
    def _():
        for lane in range(2):
            out = live_of(info, lane) * out_s[lane * ROWS : (lane + 1) * ROWS]
            total = out + mid_ref[lane]
            keep_ref[lane] = jnp.where(info[0] == 0, total[:128], total[128:])
            send_ref[lane] = jnp.where(info[0] == 0, out[128:], out[:128]).astype(BF)
            dz_ref[lane] = dz_s[lane * ROWS : (lane + 1) * ROWS].astype(BF)
            mid_copy(lane).wait()
        for k in range(2):
            for c in copies(k, place, near):
                c.wait()


def feed_forward(info, x, part, sib, gain, dy, weights):
    return pl.pallas_call(
        ffn_kernel,
        grid_spec=pltpu.PrefetchScalarGridSpec(
            num_scalar_prefetch=1,
            grid=(4,),
            in_specs=[
                HBM, HBM, HBM, FULL, HBM,
                pl.BlockSpec((16, 2, 32, HALF), lambda i, info: (0, 0, (i // 2) ^ info[3], i % 2)),
                pl.BlockSpec((8, 1, 64, 1024), lambda i, info: (i % 2, i // 2, 1, 0)),
            ],
            out_specs=(HBM, FULL, FULL, FULL, HBM),
            scratch_shapes=[
                pltpu.VMEM((2 * ROWS, 1024), BF), pltpu.VMEM((2 * ROWS, 1024), BF),
                pltpu.VMEM((2 * ROWS, 1024), F32), pltpu.VMEM((2 * ROWS, 1024), F32),
                pltpu.VMEM((2, 16, 2, 32, HALF), BF), pltpu.VMEM((2, 8, 64, 1024), BF),
                pltpu.SemaphoreType.DMA((2, 2)),
                pltpu.VMEM((2, ROWS, 1024), BF), pltpu.VMEM((2, ROWS, 1024), BF), pltpu.VMEM((2, ROWS, 1024), BF),
                pltpu.VMEM((2, ROWS, 1024), BF), pltpu.VMEM((2, ROWS, 1024), F32),
                pltpu.SemaphoreType.DMA((2, 4)), pltpu.SemaphoreType.DMA((2,)),
            ],
        ),
        out_shape=(
            sds((2, ROWS, 1024), F32), sds((2, 128, 1024), F32), sds((2, 128, 1024), BF),
            sds((2, ROWS, 1024), BF), sds((16, 2, 192, 1024), BF),
        ),
        compiler_params=params(BIG),
        cost_estimate=cost(13_000_000_000, 32_000_000),
        name="feed_forward",
    )(info, x, part, sib, gain, dy, weights, weights)


STEPS = (("x", "c"), ("z", "a"), ("z", "b"), ("y", "a"))


def carry(ends, far, rate, block, lane, reverse, between=None):
    low, high = ends[:, :4], ends[:, 4:]
    far, rate = far[:, :4], rate[:, :4]
    first, second = (high, low) if reverse else (low, high)
    total = far * first + second
    entering = jnp.zeros_like(total)
    for k, (axis, kind) in enumerate(STEPS):
        if between is not None:
            total = between(k, total)
        other = flip(total, axis, kind)
        upper = (block >> k) & 1
        within = block & ((1 << k) - 1)
        if reverse:
            takes, gap = upper == 0, (1 << k) - 1 - within
        else:
            takes, gap = upper == 1, within
        reach = jnp.exp(-rate * (BLOCK * gap).astype(F32)) * other
        whole = jnp.exp(-rate * float(BLOCK << k))
        joined = whole * jnp.where(takes, other, total) + jnp.where(takes, total, other)
        if k >= 2:
            reach = jnp.where(lane == 1, 0.0, reach)
            joined = jnp.where(lane == 1, 0.0, joined)
        entering = entering + jnp.where(takes, reach, 0.0)
        total = joined
    inner = first + far * entering
    return jnp.concatenate([inner, entering] if reverse else [entering, inner], axis=1)


def adam(factor, w_ref, f_ref, s_ref, grad, outs, rate, decay):
    clipped = grad * factor
    first_new = BETA_ONE * f_ref[...] + (1.0 - BETA_ONE) * clipped
    second_new = BETA_TWO * s_ref[...] + (1.0 - BETA_TWO) * clipped * clipped
    fix_one = 1.0 - BETA_ONE**STEP
    fix_two = 1.0 - BETA_TWO**STEP
    direction = first_new / fix_one / (jnp.sqrt(second_new / fix_two) + ADAM_EPS)
    weight = w_ref[...]
    weight_new = weight - rate * (direction + decay * weight)
    for ref, v in zip(outs, (first_new, second_new, weight_new, weight_new.astype(BF))):
        ref[...] = v


def finish_kernel(info, mine, near, over, cross, state, gain, keep_ref, give_ref, down_ref, squares_ref):
    total = added(mine[...], near[...]) + added(over[...], cross[...])
    squares = jnp.sum(total * total, axis=0, keepdims=True)
    squares = jnp.sum(squares.reshape(1, 8, 128), axis=1)
    squares = jnp.sum(squares, axis=1, keepdims=True)
    for ref in (state, gain):
        piece = ref[...].reshape(-1, 16)
        piece = jnp.sum(piece * piece, axis=0, keepdims=True)
        squares = squares + jnp.sum(piece, axis=1, keepdims=True)
    squares_ref[...] = jnp.broadcast_to(squares, (32, 128))
    down_ref[...] = total[64:128]
    for k, row in enumerate((0, 32, 128, 160)):
        low, high = total[row : row + 16], total[row + 16 : row + 32]
        keep_ref[k] = jnp.where(info[0] == 0, low, high)
        give_ref[k] = jnp.where(info[0] == 0, high, low)


def finish(info, mine, near, over, cross, state, gain):
    rows = sds((4, 16, 1024), F32)
    return pl.pallas_call(
        finish_kernel,
        out_shape=(rows, rows, sds((64, 1024), F32), sds((32, 128), F32)),
        in_specs=[SMEM] + [FULL] * 6,
        compiler_params=params(),
        cost_estimate=cost(2_000_000, 3_000_000),
        name="finish",
    )(info, mine, near, over, cross, state, gain)


def update_kernel(info, *refs):
    ins, outs = refs[:21], refs[21:]
    weights, firsts, seconds = ins[:5], ins[5:10], ins[10:15]
    every, mine, other, down, state, gain = ins[15:]
    norm = jnp.sqrt(jnp.sum(every[...], axis=0, keepdims=True)[:, :1])
    outs[20][...] = norm
    factor = jnp.minimum(1.0, CLIP_NORM / norm)
    zero = info[0] == 0

    def pair(mine, other):
        return jnp.where(zero, mine, other), jnp.where(zero, other, mine)

    first, second = pair(mine[...], other[...])
    matrices = []
    for n in range(4):
        at_c = slice(HALF * (n % 2), HALF * (n % 2) + HALF)
        matrices.append(jnp.concatenate([first[2 + n // 2, :, at_c], second[2 + n // 2, :, at_c]], axis=1))
    attn_grad = jnp.stack(matrices)
    pieces = []
    for side in range(2):
        for k in range(16):
            at_c = slice(64 * k, 64 * k + 64)
            pieces += [first[side, :, at_c], second[side, :, at_c]]
    up_grad = jnp.concatenate(pieces, axis=1)
    grads = (attn_grad, up_grad, down[...], state[...], gain[...])
    rates = ((RATE_MATRIX, WEIGHT_DECAY),) * 3 + ((RATE_STATE, 0.0), (RATE_GAIN, 0.0))
    for k in range(5):
        adam(factor, weights[k], firsts[k], seconds[k], grads[k], outs[4 * k : 4 * k + 4], *rates[k])


def update(info, weights, firsts, seconds, grads):
    shapes = []
    for w in weights:
        shapes += [sds(w.shape, F32)] * 3 + [sds(w.shape, BF)]
    return pl.pallas_call(
        update_kernel,
        out_shape=tuple(shapes) + (sds((1, 1), F32),),
        in_specs=[SMEM] + [FULL] * 21,
        compiler_params=pltpu.CompilerParams(vmem_limit_bytes=24 * 1024 * 1024),
        cost_estimate=cost(4_000_000, 6_000_000),
        name="update",
    )(info, *weights, *firsts, *seconds, *grads)


def body(
    tokens, cotangent, lengths, attn_weight, up_weight, down_weight, state_param, norm_gain,
    attn_first, attn_second, up_first, up_second, down_first, down_second,
    state_first, state_second, gain_first, gain_second,
):
    core = lax.axis_index("core")
    ybit = lax.axis_index("y")
    chip = (ybit * 4 + lax.axis_index("z")) * 4 + lax.axis_index("x")

    mine = jnp.concatenate(
        [state_param.astype(BF).transpose(0, 2, 1).reshape(-1), norm_gain.astype(BF).reshape(-1)]
    )
    mine = jnp.pad(mine, (0, 1024 - mine.shape[0])).reshape(1, 8, 128)
    pair = ordered(core, mine, swap(mine), 0)
    pair, tokens_now, cotangent_now = lax.optimization_barrier((pair, tokens, cotangent))
    small = lax.all_to_all(
        jnp.broadcast_to(pair[None], (32, 2, 8, 128)), CHIPS, split_axis=0, concat_axis=0, tiled=True
    ).reshape(64, 1024)
    theta = small[:, :768].reshape(64, 3, NST, 16).transpose(1, 2, 0, 3).reshape(3, NST, 1024).astype(F32)
    gains = small[:, 768:800].reshape(64, 2, 16).transpose(1, 0, 2).reshape(2, 1024).astype(F32)

    lane = chip % 2
    block = chip // 2

    def trade(mine, give):
        got = flip(give, "x")
        return jnp.stack([jnp.where(lane == 0, mine, got), jnp.where(lane == 0, got, mine)])

    def of_lane(v, which):
        return lax.dynamic_index_in_dim(v, which, 0, keepdims=False)

    def whole_block_of(v):
        halves = trade(of_lane(v, lane), of_lane(v, 1 - lane))
        return halves, ordered(core, halves, swap(halves), 1)

    x_own, x = whole_block_of(tokens_now[0])
    _, dy = whole_block_of(cotangent_now[0])
    slot_blocks = SLOT // BLOCK
    live_len = lax.dynamic_index_in_dim(lengths[0], block // slot_blocks, 0, keepdims=False)
    live_rows = jnp.clip(live_len - (block % slot_blocks) * BLOCK, 0, BLOCK)
    live_rows = jnp.where(lane == 0, BLOCK, live_rows)
    info = jnp.stack([core, live_rows, lane, ybit, chip]).astype(jnp.int32)

    attn_low = attn_weight.astype(BF)
    up_low = up_weight.astype(BF).reshape(16, 32, 2, 64).transpose(2, 0, 1, 3).reshape(2, 16, 2048)
    down_low = down_weight.astype(BF)
    qkv_keep = lax.dynamic_slice_in_dim(attn_low[:3], core * HALF, HALF, 2)
    qkv_give = lax.dynamic_slice_in_dim(attn_low[:3], (1 - core) * HALF, HALF, 2)
    qkv_chip = ordered(core, qkv_keep, swap(qkv_give), 1)
    out_chip = ordered(core, attn_low[3], swap(attn_low[3]), 0)
    up_keep = lax.dynamic_index_in_dim(up_low, core, 0, keepdims=False)
    up_give = lax.dynamic_index_in_dim(up_low, 1 - core, 0, keepdims=False)
    up_chip = ordered(core, up_keep, swap(up_give), 0)
    up_chip = up_chip.reshape(32, 2, 1024).transpose(1, 0, 2).reshape(64, 1024)
    qk_rows = jnp.concatenate([qkv_chip[0], qkv_chip[1]], axis=1)
    own_rows = jnp.concatenate([up_chip, down_low, qk_rows], axis=0)
    across = [(0, 3), (3, 0), (1, 2), (2, 1)]
    low = jnp.concatenate([own_rows[:96], out_chip[:, :HALF].reshape(16, 1024)], axis=0)
    high = jnp.concatenate([own_rows[96:], jnp.concatenate([qkv_chip[2], out_chip[:, HALF:]], axis=1)], axis=0)
    low, high, pair = lax.optimization_barrier((low, high, pair))
    low_got, high_got = flip(low, "y"), lax.ppermute(high, ("grp", "y"), across)
    out_got = jnp.concatenate([low_got[96:].reshape(32, HALF), high_got[64:, HALF:]], axis=1)
    out_rows = jnp.where(ybit == core, out_chip, out_got)
    own_last = jnp.concatenate([qkv_chip[2], out_rows[:, :HALF]], axis=1)
    other_last = jnp.concatenate([high_got[64:, :HALF], out_rows[:, HALF:]], axis=1)
    all_two = jnp.concatenate([own_rows, own_last, low_got[:96], high_got[:64], other_last], axis=0)
    full = lax.all_gather(all_two.reshape(2, 192, 1024), ("z", "x"), axis=0)

    theta_c = lax.dynamic_slice_in_dim(theta, core * HALF, HALF, 2).reshape(3, NST, 4, 128)
    theta_c = jnp.concatenate([theta_c, theta_c], axis=2)
    rate = jnp.exp(theta_c[0]) / BLOCK
    decay = jnp.exp(-rate)
    norm_scale = jnp.sqrt(-jnp.expm1(-2.0 * rate))
    cb = norm_scale * theta_c[1] * theta_c[2]
    far = jnp.exp(-rate * float(ROWS))
    gain_c = lax.dynamic_slice_in_dim(gains[0], core * HALF, HALF, 0).reshape(4, 128)
    gain_c = jnp.concatenate([gain_c, gain_c], axis=0)

    u_low, us, ended, ramp = first(info, x, gains[:1], decay)
    entering = carry(ended, far, rate, block, lane, False)
    entering, dy = lax.optimization_barrier((entering, dy))
    sb_own = state_run(us, decay, cb * gain_c, entering).reshape(2 * ROWS, HALF)
    sb_sib = swap(sb_own)

    part, q, k, v, o, p = attention(info, u_low, sb_own, sb_sib, full)
    o_sib = swap(o)
    middle, out_keep, out_send, dz_part, ffn_grad = feed_forward(
        info, x, part, swap(part), gains[1:], dy, full
    )
    dm, gain_two_grad, dq, dk, dv, grad = attention_back(
        info, dz_part, swap(dz_part), middle, dy, gains[1:], full, q, k, v, o, p,
        o_sib, u_low, sb_own, sb_sib, ffn_grad,
    )
    grad_part = lax.psum_scatter(grad.reshape(6144, 1024), ("z", "x"), scatter_dimension=0, tiled=True)
    keep, send = inputs_back(info, dq, dk, dv, full)
    got = swap(send)
    ds, started = state_turn(keep, got, decay)
    mids = {}

    def before(k, total):
        if k == 2:
            made = state_mid(us, ds, decay, cb, entering, keep, got)
            total, *mids["first"] = lax.optimization_barrier((total,) + tuple(made))
        if k == 3:
            made = state_mid_more(us, ds, decay, cb, entering, mids["first"][0])
            total, *mids["second"] = lax.optimization_barrier((total,) + tuple(made))
        return total

    leaving = carry(started, far, rate, block, lane, True, before)
    _, qu_0, r_0, gain_q = mids["first"]
    dus, qu_1, r_1 = mids["second"]
    qu, rr = (qu_0, qu_1), (r_0, r_1)
    lanes = state_fix(
        info, leaving, decay, cb, ended, ramp, entering, far, qu, rr, gain_q, gains[:1], gain_two_grad
    )
    du_mine, du_give = state_last(info, dus, decay, cb, leaving)

    out_own = (out_keep + swap(out_send).astype(F32)).astype(BF)
    output = trade(of_lane(out_own, lane), of_lane(out_own, 1 - lane))

    du_own = ordered(core, du_mine, swap(du_give), 2)
    x_own = x_own.astype(F32)
    dm_own = lax.dynamic_slice_in_dim(dm, core * 128, 128, 1)
    grad_own = (norm_back(du_own, x_own, rms_scale(x_own), gains[0]) + dm_own).astype(BF)
    token_grad = trade(of_lane(grad_own, lane), of_lane(grad_own, 1 - lane))

    packed = lanes.reshape(34, 32, 16).transpose(1, 0, 2)
    small_got = lax.all_to_all(packed, CHIPS, split_axis=0, concat_axis=0, tiled=True)
    small_sum = jnp.sum(small_got, axis=0)
    small_sum = small_sum + flip(small_sum, "grp")
    hand = []
    for j in range(32):
        for c in range(2):
            hand.append((j * 2 + c, c * 32 + j))
    mine_sum = lax.ppermute(small_sum, SHARD, hand)

    t_own = state_param.astype(BF).astype(F32).transpose(0, 2, 1)
    rate_o = jnp.exp(t_own[0]) / BLOCK
    decay_o = jnp.exp(-rate_o)
    scale_o = jnp.sqrt(-jnp.expm1(-2.0 * rate_o))
    b_o = scale_o * t_own[1]
    qu_o, rr_o = mine_sum[:NST], mine_sum[NST : 2 * NST]
    gb = t_own[2] * qu_o
    log_rate_grad = rate_o * (
        -decay_o * t_own[2] * b_o * rr_o + decay_o * decay_o / scale_o * t_own[1] * gb
    )
    state_grad = jnp.stack([log_rate_grad, scale_o * gb, b_o * qu_o]).transpose(0, 2, 1)
    gain_grad = mine_sum[2 * NST :]

    grad_part, state_grad, gain_grad = lax.optimization_barrier((grad_part, state_grad, gain_grad))
    mine_y, give_y = grad_part[:192], grad_part[192:]
    grad_keep, grad_give, down_grad, squares = finish(
        info, mine_y, flip(give_y, "y"), flip(mine_y, "grp"), lax.ppermute(give_y, ("grp", "y"), across),
        state_grad, gain_grad,
    )
    every = lax.all_to_all(squares + swap(squares), CHIPS, split_axis=0, concat_axis=0, tiled=True)
    every, output, token_grad = lax.optimization_barrier((every, output, token_grad))
    new = update(
        info,
        (attn_weight, up_weight, down_weight, state_param, norm_gain),
        (attn_first, up_first, down_first, state_first, gain_first),
        (attn_second, up_second, down_second, state_second, gain_second),
        (every, grad_keep, swap(grad_give), down_grad, state_grad, gain_grad),
    )
    return (output[None], token_grad[None], new[20][0, 0]) + tuple(new[:20])


def solution(mesh):
    inner = Mesh(mesh.devices.reshape(2, 2, 4, 4, 2), AXES)
    rows = P("grp", None, SHARD, None)
    attn = P(None, SHARD, None)
    flat = P(SHARD, None)
    gain = P(None, SHARD)
    in_specs = (rows, rows, P("grp", None), attn, flat, flat, attn, gain)
    in_specs += (attn, attn, flat, flat, flat, flat, attn, attn, gain, gain)
    out_specs = (rows, rows, P()) + (attn,) * 4 + (flat,) * 8 + (attn,) * 4 + (gain,) * 4
    return jax.shard_map(body, mesh=inner, in_specs=in_specs, out_specs=out_specs, check_vma=False)
```

```python
import jax
import jax.numpy as jnp
from jax import lax
from jax.experimental import pallas as pl
from jax.experimental.pallas import tpu as pltpu
from jax.sharding import Mesh
from jax.sharding import PartitionSpec as P

HEAD_DIM = 128
BLOCK = 512
STEP = 5
SLOT = 2048

EPS_NORM = 1e-05
BETA_ONE = 0.5
BETA_TWO = 0.5
ADAM_EPS = 1e-08
WEIGHT_DECAY = 0.1
CLIP_NORM = 0.5
RATE_MATRIX = 0.02
RATE_STATE = 1.0
RATE_GAIN = 0.6
MASKED = -1e30

AXES = ("grp", "y", "z", "x", "core")
CHIPS = ("y", "z", "x")
SHARD = ("y", "z", "x", "core")
BF = jnp.bfloat16
F32 = jnp.float32
NST = 16
ROWS = 256
HALF = 512


def flip(v, axis, kind="a"):
    if lax.axis_size(axis) == 2:
        pairs = [(0, 1), (1, 0)]
    elif kind == "c":
        pairs = [(0, 2), (2, 0), (1, 3), (3, 1)]
    elif kind == "a":
        pairs = [(0, 1), (1, 0), (2, 3), (3, 2)]
    else:
        pairs = [(0, 3), (3, 0), (1, 2), (2, 1)]
    return lax.ppermute(v, axis, pairs)


def swap(v):
    return flip(v, "core")


def ordered(bit, own, other, axis):
    first = jnp.where(bit == 0, own, other)
    second = jnp.where(bit == 0, other, own)
    return jnp.concatenate([first, second], axis=axis)


def rms_scale(value):
    return lax.rsqrt(jnp.mean(value * value, axis=-1, keepdims=True) + EPS_NORM)


def norm_back(grad, value, inverse, gain):
    unit = value * inverse
    scaled = grad * gain
    return inverse * (scaled - unit * jnp.mean(scaled * unit, axis=-1, keepdims=True))


def dot(left, right):
    return jnp.dot(left, right, preferred_element_type=F32)


def dot_nt(left, right):
    return lax.dot_general(left, right, (((1,), (1,)), ((), ())), preferred_element_type=F32)


def dot_tn(left, right):
    return lax.dot_general(left, right, (((0,), (0,)), ((), ())), preferred_element_type=F32)


def params(mib=16):
    return pltpu.CompilerParams(vmem_limit_bytes=mib * 1024 * 1024)


BIG = 53


def cost(flops, bytes_accessed):
    return pl.CostEstimate(flops=flops, bytes_accessed=bytes_accessed, transcendentals=0)


def sds(shape, dtype):
    return jax.ShapeDtypeStruct(shape, dtype)


SMEM = pl.BlockSpec(memory_space=pltpu.SMEM)
FULL = pl.BlockSpec(memory_space=pltpu.VMEM)


def live_of(info, half):
    return (lax.broadcasted_iota(jnp.int32, (ROWS, 1), 0) + half * ROWS < info[1]).astype(F32)


def at(ref, t):
    return ref[pl.ds(t, 8, stride=ROWS), :]


def tree(terms):
    while len(terms) > 1:
        terms = [terms[i] + terms[i + 1] for i in range(0, len(terms), 2)]
    return terms[0]


def first_kernel(info, x_ref, gain_ref, a_ref, low_ref, us_ref, e_ref, f_ref):
    for lane in range(2):
        x = x_ref[lane].astype(F32)
        unit = x * rms_scale(x)
        low_ref[lane] = (unit * gain_ref[...]).astype(BF)
        half = jnp.where(info[0] == 0, unit[:, :HALF], unit[:, HALF:])
        for g in range(4):
            us_ref[pl.ds((lane * 4 + g) * ROWS, ROWS), :] = half[:, g * 128 : (g + 1) * 128]
    half = NST // 2
    for base in (0, half):
        a = [a_ref[base + n] for n in range(half)]

        def step(t, held):
            e, f = held
            u = at(us_ref, t)
            f = tuple(a[n] * (f[n] + e[n]) for n in range(half))
            e = tuple(a[n] * e[n] + u for n in range(half))
            return e, f

        zero = tuple(jnp.zeros((8, 128), F32) for _ in range(half))
        e, f = lax.fori_loop(0, ROWS, step, (zero, zero), unroll=4)
        for n in range(half):
            e_ref[base + n] = e[n]
            f_ref[base + n] = f[n]


STATE = sds((NST, 8, 128), F32)
SPREAD = sds((8 * ROWS, 128), F32)


def first(info, x, gain, a):
    return pl.pallas_call(
        first_kernel,
        out_shape=(sds((2, ROWS, 1024), BF), SPREAD, STATE, STATE),
        in_specs=[SMEM, FULL, FULL, FULL],
        compiler_params=params(),
        cost_estimate=cost(32_000_000, 3_000_000),
        name="first",
    )(info, x, gain, a)


def run_kernel(us, a_ref, cb_ref, h_ref, s_ref, ss):
    def step(t, h):
        u = at(us, t)
        h = tuple(a_ref[n] * h[n] + u for n in range(NST))
        ss[pl.ds(t, 8, stride=ROWS), :] = tree([cb_ref[n] * h[n] for n in range(NST)])
        return h

    lax.fori_loop(0, ROWS, step, tuple(h_ref[n] for n in range(NST)), unroll=4)
    for lane in range(2):
        for g in range(4):
            s_ref[lane, :, g * 128 : (g + 1) * 128] = ss[pl.ds((lane * 4 + g) * ROWS, ROWS), :].astype(BF)


def state_run(us, a, cb, h):
    return pl.pallas_call(
        run_kernel,
        out_shape=sds((2, ROWS, HALF), BF),
        scratch_shapes=[pltpu.VMEM((8 * ROWS, 128), F32)],
        compiler_params=params(),
        cost_estimate=cost(32_000_000, 2_000_000),
        name="state_run",
    )(us, a, cb, h)


def turn_kernel(keep_ref, got_ref, a_ref, ds_ref, e_ref):
    for half in range(2):
        d = added(keep_ref[0, half], got_ref[0, half])
        for g in range(4):
            ds_ref[pl.ds((half * 4 + g) * ROWS, ROWS), :] = d[:, g * 128 : (g + 1) * 128]
    a = [a_ref[n] for n in range(NST)]

    def step(i, h):
        d = at(ds_ref, ROWS - 1 - i)
        return tuple(a[n] * h[n] + d for n in range(NST))

    h = lax.fori_loop(0, ROWS, step, tuple(jnp.zeros((8, 128), F32) for _ in range(NST)), unroll=4)
    for n in range(NST):
        e_ref[n] = h[n]


def state_turn(keep, got, a):
    return pl.pallas_call(
        turn_kernel,
        out_shape=(SPREAD, STATE),
        compiler_params=params(),
        cost_estimate=cost(16_000_000, 4_000_000),
        name="state_turn",
    )(keep, got, a)


def mid_kernel(base, us, ds, a_ref, cb_ref, h_ref, dus_in, dus, qu_ref, r_ref):
    half = NST // 2
    a = [a_ref[base + n] for n in range(half)]

    def step(i, held):
        q, v, qu, r = held
        t = ROWS - 1 - i
        u, d = at(us, t), at(ds, t)
        v = tuple(a[n] * v[n] + q[n] for n in range(half))
        q = tuple(a[n] * q[n] + d for n in range(half))
        du = tree([cb_ref[base + n] * q[n] for n in range(half)])
        dus[pl.ds(t, 8, stride=ROWS), :] = at(dus_in, t) + du
        qu = tuple(qu[n] + q[n] * u for n in range(half))
        r = tuple(r[n] + v[n] * u for n in range(half))
        return (q, v, qu, r)

    zero = tuple(jnp.zeros((8, 128), F32) for _ in range(half))
    q, v, qu, r = lax.fori_loop(0, ROWS, step, (zero,) * 4, unroll=2)
    for n in range(half):
        qu_ref[n] = qu[n]
        r_ref[n] = r[n] + h_ref[base + n] * (a[n] * v[n] + q[n])


def mid_first_kernel(us, ds, a_ref, cb_ref, h_ref, keep_ref, got_ref, dus, qu_ref, r_ref, g_ref, dq):
    for half in range(2):
        du = added(keep_ref[1, half], got_ref[1, half])
        for g in range(4):
            k = half * 4 + g
            piece = du[:, g * 128 : (g + 1) * 128]
            dq[pl.ds(k * ROWS, ROWS), :] = piece
            g_ref[k : k + 1, :] = jnp.sum(piece * us[pl.ds(k * ROWS, ROWS), :], axis=0, keepdims=True)
    mid_kernel(0, us, ds, a_ref, cb_ref, h_ref, dq, dus, qu_ref, r_ref)


def state_mid(us, ds, a, cb, h, keep, got):
    part = sds((NST // 2, 8, 128), F32)
    return pl.pallas_call(
        mid_first_kernel,
        out_shape=(SPREAD, part, part, sds((8, 128), F32)),
        scratch_shapes=[pltpu.VMEM((8 * ROWS, 128), F32)],
        compiler_params=params(),
        cost_estimate=cost(40_000_000, 4_000_000),
        name="state_mid_0",
    )(us, ds, a, cb, h, keep, got)


def state_mid_more(us, ds, a, cb, h, dus):
    part = sds((NST // 2, 8, 128), F32)
    return pl.pallas_call(
        lambda *refs: mid_kernel(NST // 2, *refs),
        out_shape=(SPREAD, part, part),
        compiler_params=params(),
        cost_estimate=cost(40_000_000, 4_000_000),
        name="state_mid_1",
    )(us, ds, a, cb, h, dus)


def fix_kernel(info, q_ref, a_ref, cb_ref, e_ref, f_ref, h_ref, far_ref, qu_0, qu_1, r_0, r_1, g_ref, gain, gain_two, out):
    half = NST // 2

    def halved(v):
        return jnp.where(info[0] == 0, v[:, :HALF], v[:, HALF:])

    def put(row, v, scale):
        both = v[:4] + v[4:]
        for g in range(4):
            at_c = slice(g * 128, (g + 1) * 128)
            value = both[g : g + 1]
            out[row : row + 1, at_c] = value * scale[:, at_c] if scale is not None else value

    gain_c = halved(gain[...])
    total = g_ref[...]
    for n in range(NST):
        q = q_ref[n]
        qu = (qu_0, qu_1)[n // half][n % half] + q * a_ref[n] * e_ref[n]
        r = (r_0, r_1)[n // half][n % half] + q * (f_ref[n] + h_ref[n] * (float(ROWS) * far_ref[n]))
        total = total + cb_ref[n] * qu
        put(n, qu, gain_c)
        put(NST + n, r, gain_c)
    put(2 * NST, total, None)
    out[2 * NST + 1 :] = halved(gain_two[...])


def state_fix(info, q, a, cb, e, f, h, far, qu, r, g, gain, gain_two):
    return pl.pallas_call(
        fix_kernel,
        out_shape=sds((2 * NST + 2, HALF), F32),
        in_specs=[SMEM] + [FULL] * 14,
        compiler_params=params(),
        cost_estimate=cost(1_000_000, 1_000_000),
        name="state_fix",
    )(info, q, a, cb, e, f, h, far, *qu, *r, g, gain, gain_two)


def last_kernel(info, dus, a_ref, cb_ref, q_ref, mine_ref, give_ref, out):
    def step(i, q):
        t = ROWS - 1 - i
        q = tuple(a_ref[n] * q[n] for n in range(NST))
        out[pl.ds(t, 8, stride=ROWS), :] = at(dus, t) + tree([cb_ref[n] * q[n] for n in range(NST)])
        return q

    lax.fori_loop(0, ROWS, step, tuple(q_ref[n] for n in range(NST)), unroll=4)
    mine = pl.multiple_of(info[0] * 128, 128)
    give = pl.multiple_of((1 - info[0]) * 128, 128)
    for lane in range(2):
        for g in range(4):
            base = (lane * 4 + g) * ROWS
            at_c = slice(g * 128, (g + 1) * 128)
            mine_ref[lane, :, at_c] = out[pl.ds(base + mine, 128), :]
            give_ref[lane, :, at_c] = out[pl.ds(base + give, 128), :]


def state_last(info, dus, a, cb, q):
    half = sds((2, 128, HALF), F32)
    return pl.pallas_call(
        last_kernel,
        out_shape=(half, half),
        in_specs=[SMEM] + [FULL] * 4,
        scratch_shapes=[pltpu.VMEM((8 * ROWS, 128), F32)],
        compiler_params=params(),
        cost_estimate=cost(32_000_000, 2_000_000),
        name="state_last",
    )(info, dus, a, cb, q)


def added(left, right):
    return left.astype(F32) + right.astype(F32)


def wide(v):
    return v.reshape(v.shape[0] * v.shape[1], v.shape[2])


class Weights:
    def __init__(self, info, full_ref, w, sems):
        self.y, self.full, self.w, self.sems = info[3], full_ref, w, sems
        self.copies = {}

    def start(self, order):
        for n in order:
            rows, cols = pl.ds(128 + 32 * (n // 2), 32), pl.ds(HALF * (n % 2), HALF)
            self.copies[n] = [
                pltpu.make_async_copy(self.full.at[:, r, rows, cols], self.w.at[n, r], self.sems.at[n, r])
                for r in range(2)
            ]
            for c in self.copies[n]:
                c.start()

    def wait(self, n):
        for c in self.copies[n]:
            c.wait()

    def half(self, n, half):
        return wide(self.w[n, half ^ self.y])

    def out(self, half):
        return wide(self.w[3, half])


WEIGHTS = [pltpu.VMEM((4, 2, 16, 32, HALF), BF), pltpu.SemaphoreType.DMA((4, 2))]
HBM = pl.BlockSpec(memory_space=pltpu.HBM)


def bring(pairs, sems):
    sems = sems if isinstance(sems, list) else [sems.at[n] for n in range(len(pairs))]
    copies = [pltpu.make_async_copy(src, dst, sem) for (src, dst), sem in zip(pairs, sems)]
    for copy in copies:
        copy.start()
    return copies


INPUTS = [pltpu.VMEM((2, ROWS, 1024), BF)] + [pltpu.VMEM((2 * ROWS, HALF), BF)] * 2 + [pltpu.SemaphoreType.DMA((6,))]


def attn_kernel(
    info, u_in, own_in, sib_in, full_ref, part_ref, q_out, k_out, v_out, o_out, p_out,
    q_ref, k_ref, v_ref, o_ref, p_ref, out_sems, w_s, sems, u_ref, own, sib, in_sems,
):
    w = Weights(info, full_ref, w_s, sems)
    w.start((0,))
    arriving = bring(((u_in, u_ref), (own_in, own), (sib_in, sib)), in_sems)
    w.start((1, 2, 3))
    me, it = info[0], 1 - info[0]
    leaving = []

    def leave(src, dst, *place):
        copy = pltpu.make_async_copy(src, dst, out_sems.at[place])
        copy.start()
        leaving.append(copy)

    arriving[0].wait()
    w.wait(0)
    for half in range(2):
        u = u_ref[half]
        q_ref[half] = (dot(u[:, :HALF], w.half(0, 0)) + dot(u[:, HALF:], w.half(0, 1))).astype(BF)
    leave(q_ref, q_out, 0, 0)
    for copy in arriving[1:]:
        copy.wait()
    for n, ref, out in ((1, k_ref, k_out), (2, v_ref, v_out)):
        w.wait(n)
        ref[...] = (dot(own[...], w.half(n, me)) + dot(sib[...], w.half(n, it))).astype(BF)
        leave(ref, out, n, 0)
    w.wait(3)
    for half in range(2):
        seen = ROWS * (half + 1)
        row = lax.broadcasted_iota(jnp.int32, (ROWS, seen), 0) + half * ROWS
        allowed = lax.broadcasted_iota(jnp.int32, (ROWS, seen), 1) <= row
        for h in range(4):
            at_h = slice(h * HEAD_DIM, (h + 1) * HEAD_DIM)
            s = dot_nt(q_ref[half, :, at_h], k_ref[:seen, at_h]) * HEAD_DIM**-0.5
            s = jnp.where(allowed, s, MASKED)
            e = jnp.exp(s - jnp.max(s, axis=-1, keepdims=True))
            p = (e / jnp.sum(e, axis=-1, keepdims=True)).astype(BF)
            p_ref[half, h, :, :seen] = p
            o_ref[half, :, at_h] = dot(p, v_ref[:seen, at_h]).astype(BF)
        leave(p_ref.at[half], p_out.at[half], 3, half)
        leave(o_ref.at[half], o_out.at[half], 4, half)
        o = o_ref[half]
        for side in range(2):
            part_ref[half, :, side * HALF : (side + 1) * HALF] = dot(o, w.out(side)).astype(BF)
    for copy in leaving:
        copy.wait()


KEPT = [
    pltpu.VMEM((2, ROWS, HALF), BF), pltpu.VMEM((2 * ROWS, HALF), BF), pltpu.VMEM((2 * ROWS, HALF), BF),
    pltpu.VMEM((2, ROWS, HALF), BF), pltpu.VMEM((2, 4, ROWS, 2 * ROWS), BF), pltpu.SemaphoreType.DMA((5, 2)),
]


def attention(info, u, own, sib, full):
    return pl.pallas_call(
        attn_kernel,
        out_shape=(
            sds((2, ROWS, 1024), BF), sds((2, ROWS, HALF), BF), sds((2 * ROWS, HALF), BF),
            sds((2 * ROWS, HALF), BF), sds((2, ROWS, HALF), BF), sds((2, 4, ROWS, 2 * ROWS), BF),
        ),
        in_specs=[SMEM] + [HBM] * 4,
        out_specs=(FULL, HBM, HBM, HBM, HBM, HBM),
        scratch_shapes=KEPT + WEIGHTS + INPUTS,
        compiler_params=params(BIG),
        cost_estimate=cost(4_000_000_000, 16_000_000),
        name="attention",
    )(info, u, own, sib, full)


def attn_back_kernel(
    info, own_in, sib_in, mid_in, dy_in, gain_ref, full_ref, q_in, k_in, v_in, o_in, p_in,
    os_in, u_in, so_in, ss_in, held_ref, dm_out, g_ref, dq_out, dk_out, dv_out, grad_ref,
    q_ref, k_ref, v_ref, o_ref, p_ref, in_sems, w_s, sems, grads, out_sems,
    u_ref, s_own, s_sib, late_sems, os_ref, own_ref, sib_ref, mid_ref, dy_ref, dm_ref, first_sems,
    dq_ref, dk_ref, dv_ref, made_sems,
):
    del held_ref
    early = []
    for lane in range(2):
        pairs = ((own_in, own_ref), (sib_in, sib_ref), (mid_in, mid_ref), (dy_in, dy_ref))
        early.append(bring([(a.at[lane], b.at[lane]) for a, b in pairs], first_sems.at[lane]))
    w = Weights(info, full_ref, w_s, sems)
    w.start((3,))
    pairs = ((v_in, v_ref), (p_in, p_ref), (k_in, k_ref), (q_in, q_ref), (o_in, o_ref))
    arriving = bring(pairs, [in_sems.at[n, 0] for n in range(5)])
    late = bring(((u_in, u_ref), (so_in, s_own), (ss_in, s_sib), (os_in, os_ref)), late_sems)
    me, it = info[0], 1 - info[0]
    scale = HEAD_DIM**-0.5
    gain_grad = jnp.zeros((1, 1024), F32)
    branches = []
    leaving = []

    def leave(src, dst, sem):
        copy = pltpu.make_async_copy(src, dst, sem)
        copy.start()
        leaving.append(copy)

    for lane in range(2):
        for copy in early[lane]:
            copy.wait()
        m = mid_ref[lane]
        dz = added(own_ref[lane], sib_ref[lane])
        inverse = rms_scale(m)
        unit = m * inverse
        gain_grad = gain_grad + jnp.sum(dz * unit, axis=0, keepdims=True)
        scaled = dz * gain_ref[...]
        dm = dy_ref[lane].astype(F32) + inverse * (
            scaled - unit * jnp.mean(scaled * unit, axis=-1, keepdims=True)
        )
        dm_ref[lane] = dm
        leave(dm_ref.at[lane], dm_out.at[lane], made_sems.at[0, lane])
        branch = (live_of(info, lane) * dm).astype(BF)
        branches.append(branch)
    g_ref[...] = gain_grad
    w.wait(3)
    for copy in arriving:
        copy.wait()
    d_o = []
    for half in range(2):
        branch = branches[half]
        d_o.append((dot_nt(branch[:, :HALF], w.out(0)) + dot_nt(branch[:, HALF:], w.out(1))).astype(BF))
    for h in range(4):
        at_h = slice(h * HEAD_DIM, (h + 1) * HEAD_DIM)
        dk, dv = [], []
        for half in range(2):
            seen = ROWS * (half + 1)
            p_low = p_ref[half, h, :, :seen]
            p = p_low.astype(F32)
            d_o_h = d_o[half][:, at_h]
            dp = dot_nt(d_o_h, v_ref[:seen, at_h])
            total = jnp.sum(p * dp, axis=-1, keepdims=True)
            ds = (p * (dp - total)).astype(BF)
            dq_ref[half, :, at_h] = (dot(ds, k_ref[:seen, at_h]) * scale).astype(BF)
            dk.append(dot_tn(ds, q_ref[half, :, at_h]))
            dv.append(dot_tn(p_low, d_o_h))
        for ref, parts, factor in ((dk_ref, dk, scale), (dv_ref, dv, 1.0)):
            ref[:ROWS, at_h] = ((parts[0] + parts[1][:ROWS]) * factor).astype(BF)
            ref[ROWS:, at_h] = (parts[1][ROWS:] * factor).astype(BF)
    for n, (src, dst) in enumerate(((dq_ref, dq_out), (dk_ref, dk_out), (dv_ref, dv_out))):
        leave(src, dst, made_sems.at[1 + n, 0])

    def leave_grad(n):
        at_r = pl.ds(pl.multiple_of(info[8 + n // 2], 32), 32)
        at_c = pl.ds(HALF * (n % 2), HALF)
        for y in range(2):
            leave(grads.at[n, y], grad_ref.at[:, y ^ info[3], at_r, at_c], out_sems.at[n, y])

    def put(n, half, value):
        grads[n, pl.ds(half, 1)] = value.astype(BF).reshape(1, 16, 32, HALF)

    for copy in late:
        copy.wait()
    branch = jnp.concatenate(branches, axis=0)
    branch = jnp.where(info[0] == 0, branch[:, :HALF], branch[:, HALF:])
    for half, ref in ((me, o_ref), (it, os_ref)):
        put(3, half, dot_tn(wide(ref[...]), branch))
    leave_grad(3)
    for n, ref in ((1, dk_ref), (2, dv_ref)):
        for half, s_c in ((me, s_own), (it, s_sib)):
            put(n, half, dot_tn(s_c[...], ref[...]))
        leave_grad(n)
    for half in range(2):
        put(0, half, dot_tn(wide(u_ref[...])[:, half * HALF : (half + 1) * HALF], wide(dq_ref[...])))
    leave_grad(0)
    for copy in leaving:
        copy.wait()


def attention_back(info, own, sib, mid, dy, gain, full, q, k, v, o, p, o_sib, u, s_own, s_sib, held):
    return pl.pallas_call(
        attn_back_kernel,
        out_shape=(
            sds((2, ROWS, 1024), F32), sds((1, 1024), F32), sds((2, ROWS, HALF), BF),
            sds((2 * ROWS, HALF), BF), sds((2 * ROWS, HALF), BF), sds(held.shape, BF),
        ),
        in_specs=[SMEM] + [HBM] * 4 + [FULL] + [HBM] * 11,
        out_specs=(HBM, FULL, HBM, HBM, HBM, HBM),
        input_output_aliases={16: 5},
        scratch_shapes=KEPT + WEIGHTS + WEIGHTS + INPUTS + [
            pltpu.VMEM((2, ROWS, HALF), BF), pltpu.VMEM((2, ROWS, 1024), BF), pltpu.VMEM((2, ROWS, 1024), BF),
            pltpu.VMEM((2, ROWS, 1024), F32), pltpu.VMEM((2, ROWS, 1024), BF), pltpu.VMEM((2, ROWS, 1024), F32),
            pltpu.SemaphoreType.DMA((2, 4)),
            pltpu.VMEM((2, ROWS, HALF), BF), pltpu.VMEM((2 * ROWS, HALF), BF), pltpu.VMEM((2 * ROWS, HALF), BF),
            pltpu.SemaphoreType.DMA((4, 2)),
        ],
        compiler_params=params(BIG),
        cost_estimate=cost(6_000_000_000, 24_000_000),
        name="attention_back",
    )(info, own, sib, mid, dy, gain, full, q, k, v, o, p, o_sib, u, s_own, s_sib, held)


def inputs_back_kernel(
    info, dq_in, dk_in, dv_in, full_ref, keep_ref, send_ref, w_s, sems, dq_ref, dk_ref, dv_ref, in_sems
):
    w = Weights(info, full_ref, w_s, sems)
    w.start((1, 2))
    arriving = bring(((dk_in, dk_ref), (dv_in, dv_ref), (dq_in, dq_ref)), in_sems)
    w.start((0,))
    for copy in arriving:
        copy.wait()
    for n in (1, 2):
        w.wait(n)
    for ref, half in ((send_ref, 1 - info[0]), (keep_ref, info[0])):
        ds = dot_nt(dk_ref[...], w.half(1, half)) + dot_nt(dv_ref[...], w.half(2, half))
        ref[0] = ds.astype(BF).reshape(2, ROWS, HALF)
    w.wait(0)
    for ref, half in ((send_ref, 1 - info[0]), (keep_ref, info[0])):
        ref[1] = dot_nt(wide(dq_ref[...]), w.half(0, half)).astype(BF).reshape(2, ROWS, HALF)


def inputs_back(info, dq, dk, dv, full):
    return pl.pallas_call(
        inputs_back_kernel,
        out_shape=(sds((2, 2, ROWS, HALF), BF), sds((2, 2, ROWS, HALF), BF)),
        in_specs=[SMEM] + [HBM] * 4,
        scratch_shapes=WEIGHTS + [
            pltpu.VMEM((2, ROWS, HALF), BF), pltpu.VMEM((2 * ROWS, HALF), BF), pltpu.VMEM((2 * ROWS, HALF), BF),
            pltpu.SemaphoreType.DMA((3,)),
        ],
        compiler_params=params(BIG),
        cost_estimate=cost(2_000_000_000, 7_000_000),
        name="inputs_back",
    )(info, dq, dk, dv, full)


GELU_C = 0.7978845608028654
GELU_K = 0.044715


def ffn_kernel(
    info, x_in, part_in, sib_in, gain_ref, dy_in, up_ref, down_ref,
    mid_out, dz_ref, hidden_ref, grad_ref, z_s, d_s, dz_s, gu_s, gd_s, sems,
    x_ref, part_ref, sib_ref, dy_ref, mid_ref, in_sems, mid_sems,
):
    step = pl.program_id(0)

    def mid_copy(k):
        return pltpu.make_async_copy(mid_ref.at[k], mid_out.at[k], mid_sems.at[k])

    slot = step % 2
    place, near = step % 2, step // 2
    side = near ^ info[3]

    def copies(slot, place, near):
        at_c = pl.ds(pl.multiple_of(place * HALF, HALF), HALF)
        at_r = pl.ds(pl.multiple_of(info[5 + (near ^ info[3])], 32), 32)
        at_z = pl.ds(place * 8, 8)
        made = [pltpu.make_async_copy(gu_s.at[slot], grad_ref.at[:, :, at_r, at_c], sems.at[0, slot])]
        for k in range(2):
            at_r = pl.ds(pl.multiple_of(info[7 + 3 * k], 32), 32)
            src = gd_s.at[slot, :, pl.ds(32 * k, 32), :]
            made.append(pltpu.make_async_copy(src, grad_ref.at[at_z, near, at_r, :], sems.at[1 + k, slot]))
        return made

    @pl.when(step == 0)
    def _():
        arriving = []
        for lane in range(2):
            pairs = ((part_in, part_ref), (sib_in, sib_ref), (x_in, x_ref), (dy_in, dy_ref))
            arriving.append(bring([(a.at[lane], b.at[lane]) for a, b in pairs], in_sems.at[lane]))
        for lane in range(2):
            for copy in arriving[lane]:
                copy.wait()
            live = live_of(info, lane)
            m = x_ref[lane].astype(F32) + live * added(part_ref[lane], sib_ref[lane])
            mid_ref[lane] = m
            mid_copy(lane).start()
            z_s[lane * ROWS : (lane + 1) * ROWS] = (m * rms_scale(m) * gain_ref[...]).astype(BF)
            d_s[lane * ROWS : (lane + 1) * ROWS] = (live * dy_ref[lane].astype(F32)).astype(BF)
        dz_s[...] = jnp.zeros_like(dz_s)

    z, d = z_s[...], d_s[...]
    down = wide(down_ref[:, 0])
    up_0, up_1 = (up_ref[:, pl.ds(y ^ info[3], 1)].reshape(HALF, HALF) for y in range(2))
    f = dot(z[:, :HALF], up_0) + dot(z[:, HALF:], up_1)
    square = f * f
    h = 0.5 + 0.5 * jnp.tanh(GELU_C * f + (GELU_C * GELU_K) * f * square)
    hidden = (f * h).astype(BF)
    slope = h + (h - h * h) * (2.0 * GELU_C * f + (6.0 * GELU_C * GELU_K) * f * square)
    hidden_ref[...] = hidden
    back = (slope * dot_nt(d, down)).astype(BF)

    @pl.when(step >= 2)
    def _():
        for c in copies(slot, place, near):
            c.wait()

    gd_s[slot] = dot_tn(hidden, d).astype(BF).reshape(8, 64, 1024)
    gu = dot_tn(z, back).astype(BF).reshape(2, 16, 32, HALF)
    for y in range(2):
        gu_s[slot, :, pl.ds(y ^ info[3], 1)] = gu[y].reshape(16, 1, 32, HALF)
    for c in copies(slot, place, near):
        c.start()
    dz_s[:, :HALF] += dot_nt(back, up_0)
    dz_s[:, HALF:] += dot_nt(back, up_1)

    @pl.when(step == pl.num_programs(0) - 1)
    def _():
        for lane in range(2):
            dz_ref[lane] = dz_s[lane * ROWS : (lane + 1) * ROWS].astype(BF)
            mid_copy(lane).wait()
        for k in range(2):
            for c in copies(k, place, near):
                c.wait()


def feed_forward(info, x, part, sib, gain, dy, weights):
    chunk = pl.BlockSpec((2 * ROWS, HALF), lambda i, info: (0, i))
    return pl.pallas_call(
        ffn_kernel,
        grid_spec=pltpu.PrefetchScalarGridSpec(
            num_scalar_prefetch=1,
            grid=(4,),
            in_specs=[
                HBM, HBM, HBM, FULL, HBM,
                pl.BlockSpec((16, 2, 32, HALF), lambda i, info: (0, 0, (i // 2) ^ info[3], i % 2)),
                pl.BlockSpec((8, 1, 64, 1024), lambda i, info: (i % 2, i // 2, 1, 0)),
            ],
            out_specs=(HBM, FULL, chunk, HBM),
            scratch_shapes=[
                pltpu.VMEM((2 * ROWS, 1024), BF), pltpu.VMEM((2 * ROWS, 1024), BF), pltpu.VMEM((2 * ROWS, 1024), F32),
                pltpu.VMEM((2, 16, 2, 32, HALF), BF), pltpu.VMEM((2, 8, 64, 1024), BF),
                pltpu.SemaphoreType.DMA((3, 2)),
                pltpu.VMEM((2, ROWS, 1024), BF), pltpu.VMEM((2, ROWS, 1024), BF), pltpu.VMEM((2, ROWS, 1024), BF),
                pltpu.VMEM((2, ROWS, 1024), BF), pltpu.VMEM((2, ROWS, 1024), F32),
                pltpu.SemaphoreType.DMA((2, 4)), pltpu.SemaphoreType.DMA((2,)),
            ],
        ),
        out_shape=(
            sds((2, ROWS, 1024), F32), sds((2, ROWS, 1024), BF), sds((2 * ROWS, 2048), BF),
            sds((16, 2, 192, 1024), BF),
        ),
        compiler_params=params(BIG),
        cost_estimate=cost(9_000_000_000, 28_000_000),
        name="feed_forward",
    )(info, x, part, sib, gain, dy, weights, weights)


DOWN = pl.BlockSpec((8, 1, 64, 1024), lambda i: (i % 2, i // 2, 1, 0))
CHUNK = pl.BlockSpec((2 * ROWS, HALF), lambda i: (0, i))


def hidden_out_kernel(info, hidden_ref, mid_ref, down_ref, keep_ref, send_ref, out_s):
    step = pl.program_id(0)
    more = dot(hidden_ref[...], wide(down_ref[:, 0]))

    @pl.when(step == 0)
    def _():
        out_s[...] = more

    @pl.when(step > 0)
    def _():
        out_s[...] += more

    @pl.when(step == pl.num_programs(0) - 1)
    def _():
        for half in range(2):
            out = live_of(info, half) * out_s[half * ROWS : (half + 1) * ROWS]
            total = out + mid_ref[half]
            keep_ref[half] = jnp.where(info[0] == 0, total[:128], total[128:])
            send_ref[half] = jnp.where(info[0] == 0, out[128:], out[:128]).astype(BF)


def hidden_out(info, hidden, mid, weights):
    return pl.pallas_call(
        hidden_out_kernel,
        grid=(4,),
        out_shape=(sds((2, 128, 1024), F32), sds((2, 128, 1024), BF)),
        in_specs=[SMEM, CHUNK, FULL, DOWN],
        out_specs=(FULL, FULL),
        scratch_shapes=[pltpu.VMEM((2 * ROWS, 1024), F32)],
        compiler_params=params(BIG),
        cost_estimate=cost(2_100_000_000, 8_000_000),
        name="hidden_out",
    )(info, hidden, mid, weights)


STEPS = (("x", "c"), ("z", "a"), ("z", "b"), ("y", "a"))


def carry(ends, far, rate, block, lane, reverse, between=None):
    low, high = ends[:, :4], ends[:, 4:]
    far, rate = far[:, :4], rate[:, :4]
    first, second = (high, low) if reverse else (low, high)
    total = far * first + second
    entering = jnp.zeros_like(total)
    for k, (axis, kind) in enumerate(STEPS):
        if between is not None:
            total = between(k, total)
        other = flip(total, axis, kind)
        upper = (block >> k) & 1
        within = block & ((1 << k) - 1)
        if reverse:
            takes, gap = upper == 0, (1 << k) - 1 - within
        else:
            takes, gap = upper == 1, within
        reach = jnp.exp(-rate * (BLOCK * gap).astype(F32)) * other
        whole = jnp.exp(-rate * float(BLOCK << k))
        joined = whole * jnp.where(takes, other, total) + jnp.where(takes, total, other)
        if k >= 2:
            reach = jnp.where(lane == 1, 0.0, reach)
            joined = jnp.where(lane == 1, 0.0, joined)
        entering = entering + jnp.where(takes, reach, 0.0)
        total = joined
    inner = first + far * entering
    return jnp.concatenate([inner, entering] if reverse else [entering, inner], axis=1)


def adam(factor, w_ref, f_ref, s_ref, grad, outs, rate, decay):
    clipped = grad * factor
    first_new = BETA_ONE * f_ref[...] + (1.0 - BETA_ONE) * clipped
    second_new = BETA_TWO * s_ref[...] + (1.0 - BETA_TWO) * clipped * clipped
    fix_one = 1.0 - BETA_ONE**STEP
    fix_two = 1.0 - BETA_TWO**STEP
    direction = first_new / fix_one / (jnp.sqrt(second_new / fix_two) + ADAM_EPS)
    weight = w_ref[...]
    weight_new = weight - rate * (direction + decay * weight)
    for ref, v in zip(outs, (first_new, second_new, weight_new, weight_new.astype(BF))):
        ref[...] = v


def finish_kernel(info, mine, near, over, cross, state, gain, own_ref, give_ref, squares_ref):
    total = added(mine[...], near[...]) + added(over[...], cross[...])
    squares = jnp.sum(total * total, axis=0, keepdims=True)
    squares = jnp.sum(squares.reshape(1, 8, 128), axis=1)
    squares = jnp.sum(squares, axis=1, keepdims=True)
    for ref in (state, gain):
        piece = ref[...].reshape(-1, 16)
        piece = jnp.sum(piece * piece, axis=0, keepdims=True)
        squares = squares + 0.5 * jnp.sum(piece, axis=1, keepdims=True)
    squares_ref[...] = jnp.broadcast_to(squares, (64, 128))
    own_ref[32:] = total[64:]
    for k in range(2):
        low, high = total[32 * k : 32 * k + 16], total[32 * k + 16 : 32 * k + 32]
        own_ref[16 * k : 16 * k + 16] = jnp.where(info[0] == 0, low, high)
        give_ref[16 * k : 16 * k + 16] = jnp.where(info[0] == 0, high, low)


def finish(info, mine, near, over, cross, state, gain):
    return pl.pallas_call(
        finish_kernel,
        out_shape=(sds((64, 1024), F32), sds((32, 1024), F32), sds((64, 128), F32)),
        in_specs=[SMEM] + [FULL] * 6,
        compiler_params=params(),
        cost_estimate=cost(2_000_000, 3_000_000),
        name="finish",
    )(info, mine, near, over, cross, state, gain)


def update_kernel(info, *refs):
    ins, outs = refs[:22], refs[22:]
    weights, firsts, seconds = ins[:5], ins[5:10], ins[10:15]
    every, mine, got, mine_far, got_far, state, gain = ins[15:]
    norm = jnp.sqrt(jnp.sum(every[...], axis=0, keepdims=True)[:, :1])
    outs[20][...] = norm
    factor = jnp.minimum(1.0, CLIP_NORM / norm)
    zero = info[0] == 0
    here = info[11] == 0

    def pair(one, two):
        first, second = jnp.where(zero, one, two), jnp.where(zero, two, one)
        return first.reshape(2, 16, 1024), second.reshape(2, 16, 1024)

    down = jnp.concatenate(
        [jnp.where(here, mine[32:], mine_far[32:]), jnp.where(here, mine_far[32:], mine[32:])], axis=0
    )
    near, far = pair(mine[:32], got[...]), pair(mine_far[:32], got_far[...])
    first, second = (jnp.where(here, b, a) for a, b in zip(near, far))
    matrices = []
    for n in range(4):
        at_c = slice(HALF * (n % 2), HALF * (n % 2) + HALF)
        matrices.append(jnp.concatenate([first[n // 2, :, at_c], second[n // 2, :, at_c]], axis=1))
    attn_grad = jnp.stack(matrices)
    first, second = (jnp.where(here, a, b) for a, b in zip(near, far))
    pieces = []
    for side in range(2):
        for k in range(16):
            at_c = slice(64 * k, 64 * k + 64)
            pieces += [first[side, :, at_c], second[side, :, at_c]]
    up_grad = jnp.concatenate(pieces, axis=1)
    grads = (attn_grad, up_grad, down, state[...], gain[...])
    rates = ((RATE_MATRIX, WEIGHT_DECAY),) * 3 + ((RATE_STATE, 0.0), (RATE_GAIN, 0.0))
    for k in range(5):
        adam(factor, weights[k], firsts[k], seconds[k], grads[k], outs[4 * k : 4 * k + 4], *rates[k])


def update(info, weights, firsts, seconds, grads):
    shapes = []
    for w in weights:
        shapes += [sds(w.shape, F32)] * 3 + [sds(w.shape, BF)]
    return pl.pallas_call(
        update_kernel,
        out_shape=tuple(shapes) + (sds((1, 1), F32),),
        in_specs=[SMEM] + [FULL] * 22,
        compiler_params=pltpu.CompilerParams(vmem_limit_bytes=24 * 1024 * 1024),
        cost_estimate=cost(4_000_000, 6_000_000),
        name="update",
    )(info, *weights, *firsts, *seconds, *grads)


def body(
    tokens, cotangent, lengths, attn_weight, up_weight, down_weight, state_param, norm_gain,
    attn_first, attn_second, up_first, up_second, down_first, down_second,
    state_first, state_second, gain_first, gain_second,
):
    core = lax.axis_index("core")
    ybit = lax.axis_index("y")
    chip = (ybit * 4 + lax.axis_index("z")) * 4 + lax.axis_index("x")

    mine = jnp.concatenate(
        [state_param.astype(BF).transpose(0, 2, 1).reshape(-1), norm_gain.astype(BF).reshape(-1)]
    )
    mine = jnp.pad(mine, (0, 1024 - mine.shape[0])).reshape(1, 8, 128)
    pair = ordered(core, mine, swap(mine), 0)
    pair, tokens_now, cotangent_now = lax.optimization_barrier((pair, tokens, cotangent))
    small = lax.all_to_all(
        jnp.broadcast_to(pair[None], (32, 2, 8, 128)), CHIPS, split_axis=0, concat_axis=0, tiled=True
    ).reshape(64, 1024)
    theta = small[:, :768].reshape(64, 3, NST, 16).transpose(1, 2, 0, 3).reshape(3, NST, 1024).astype(F32)
    gains = small[:, 768:800].reshape(64, 2, 16).transpose(1, 0, 2).reshape(2, 1024).astype(F32)

    lane = chip % 2
    block = chip // 2

    def trade(mine, give):
        got = flip(give, "x")
        return jnp.stack([jnp.where(lane == 0, mine, got), jnp.where(lane == 0, got, mine)])

    def of_lane(v, which):
        return lax.dynamic_index_in_dim(v, which, 0, keepdims=False)

    def whole_block_of(v):
        halves = trade(of_lane(v, lane), of_lane(v, 1 - lane))
        return halves, ordered(core, halves, swap(halves), 1)

    x_own, x = whole_block_of(tokens_now[0])
    _, dy = whole_block_of(cotangent_now[0])
    slot_blocks = SLOT // BLOCK
    live_len = lax.dynamic_index_in_dim(lengths[0], block // slot_blocks, 0, keepdims=False)
    live_rows = jnp.clip(live_len - (block % slot_blocks) * BLOCK, 0, BLOCK)
    live_rows = jnp.where(lane == 0, BLOCK, live_rows)
    group = lax.axis_index("grp")
    places = [((b + 3 * group) % 6) * 32 for b in range(6)]
    info = jnp.stack([core, live_rows, lane, ybit, chip] + places + [group]).astype(jnp.int32)

    attn_low = attn_weight.astype(BF)
    up_low = up_weight.astype(BF).reshape(16, 32, 2, 64).transpose(2, 0, 1, 3).reshape(2, 16, 2048)
    down_low = down_weight.astype(BF)
    qkv_keep = lax.dynamic_slice_in_dim(attn_low[:3], core * HALF, HALF, 2)
    qkv_give = lax.dynamic_slice_in_dim(attn_low[:3], (1 - core) * HALF, HALF, 2)
    qkv_chip = ordered(core, qkv_keep, swap(qkv_give), 1)
    out_chip = ordered(core, attn_low[3], swap(attn_low[3]), 0)
    up_keep = lax.dynamic_index_in_dim(up_low, core, 0, keepdims=False)
    up_give = lax.dynamic_index_in_dim(up_low, 1 - core, 0, keepdims=False)
    up_chip = ordered(core, up_keep, swap(up_give), 0)
    up_chip = up_chip.reshape(32, 2, 1024).transpose(1, 0, 2).reshape(64, 1024)
    qk_rows = jnp.concatenate([qkv_chip[0], qkv_chip[1]], axis=1)
    own_rows = jnp.concatenate([up_chip, down_low, qk_rows], axis=0)
    across = [(0, 3), (3, 0), (1, 2), (2, 1)]
    low = jnp.concatenate([own_rows[:96], out_chip[:, :HALF].reshape(16, 1024)], axis=0)
    high = jnp.concatenate([own_rows[96:], jnp.concatenate([qkv_chip[2], out_chip[:, HALF:]], axis=1)], axis=0)
    low, high, pair = lax.optimization_barrier((low, high, pair))
    low_got, high_got = flip(low, "y"), lax.ppermute(high, ("grp", "y"), across)
    out_got = jnp.concatenate([low_got[96:].reshape(32, HALF), high_got[64:, HALF:]], axis=1)
    out_rows = jnp.where(ybit == core, out_chip, out_got)
    own_last = jnp.concatenate([qkv_chip[2], out_rows[:, :HALF]], axis=1)
    other_last = jnp.concatenate([high_got[64:, :HALF], out_rows[:, HALF:]], axis=1)
    all_two = jnp.concatenate([own_rows, own_last, low_got[:96], high_got[:64], other_last], axis=0)
    full = lax.all_gather(all_two.reshape(2, 192, 1024), ("z", "x"), axis=0)

    theta_c = lax.dynamic_slice_in_dim(theta, core * HALF, HALF, 2).reshape(3, NST, 4, 128)
    theta_c = jnp.concatenate([theta_c, theta_c], axis=2)
    rate = jnp.exp(theta_c[0]) / BLOCK
    decay = jnp.exp(-rate)
    norm_scale = jnp.sqrt(-jnp.expm1(-2.0 * rate))
    cb = norm_scale * theta_c[1] * theta_c[2]
    far = jnp.exp(-rate * float(ROWS))
    gain_c = lax.dynamic_slice_in_dim(gains[0], core * HALF, HALF, 0).reshape(4, 128)
    gain_c = jnp.concatenate([gain_c, gain_c], axis=0)

    u_low, us, ended, ramp = first(info, x, gains[:1], decay)
    entering = carry(ended, far, rate, block, lane, False)
    entering, dy = lax.optimization_barrier((entering, dy))
    sb_own = state_run(us, decay, cb * gain_c, entering).reshape(2 * ROWS, HALF)
    sb_sib = swap(sb_own)

    part, q, k, v, o, p = attention(info, u_low, sb_own, sb_sib, full)
    part_sib, o_sib = lax.optimization_barrier((swap(part), swap(o)))
    middle, dz_part, hidden, ffn_grad = feed_forward(info, x, part, part_sib, gains[1:], dy, full)
    dm, gain_two_grad, dq, dk, dv, grad = attention_back(
        info, dz_part, swap(dz_part), middle, dy, gains[1:], full, q, k, v, o, p,
        o_sib, u_low, sb_own, sb_sib, ffn_grad,
    )
    grad_part = lax.psum_scatter(grad.reshape(6144, 1024), ("z", "x"), scatter_dimension=0, tiled=True)
    keep, send = inputs_back(info, dq, dk, dv, full)
    got = swap(send)
    ds, started = state_turn(keep, got, decay)
    mids = {}

    def before(k, total):
        if k == 2:
            made = state_mid(us, ds, decay, cb, entering, keep, got)
            total, *mids["first"] = lax.optimization_barrier((total,) + tuple(made))
        if k == 3:
            made = state_mid_more(us, ds, decay, cb, entering, mids["first"][0])
            total, *mids["second"] = lax.optimization_barrier((total,) + tuple(made))
        return total

    leaving = carry(started, far, rate, block, lane, True, before)
    _, qu_0, r_0, gain_q = mids["first"]
    dus, qu_1, r_1 = mids["second"]
    qu, rr = (qu_0, qu_1), (r_0, r_1)
    lanes = state_fix(
        info, leaving, decay, cb, ended, ramp, entering, far, qu, rr, gain_q, gains[:1], gain_two_grad
    )
    du_mine, du_give = state_last(info, dus, decay, cb, leaving)

    out_keep, out_send = hidden_out(info, hidden, middle, full)
    out_own = (out_keep + swap(out_send).astype(F32)).astype(BF)
    output = trade(of_lane(out_own, lane), of_lane(out_own, 1 - lane))

    du_own = ordered(core, du_mine, swap(du_give), 2)
    x_own = x_own.astype(F32)
    dm_own = lax.dynamic_slice_in_dim(dm, core * 128, 128, 1)
    grad_own = (norm_back(du_own, x_own, rms_scale(x_own), gains[0]) + dm_own).astype(BF)
    token_grad = trade(of_lane(grad_own, lane), of_lane(grad_own, 1 - lane))

    packed = lanes.reshape(34, 32, 16).transpose(1, 0, 2)
    small_got = lax.all_to_all(packed, CHIPS, split_axis=0, concat_axis=0, tiled=True)
    small_sum = jnp.sum(small_got, axis=0)
    small_sum = small_sum + flip(small_sum, "grp")
    hand = []
    for j in range(32):
        for c in range(2):
            hand.append((j * 2 + c, c * 32 + j))
    mine_sum = lax.ppermute(small_sum, SHARD, hand)

    t_own = state_param.astype(BF).astype(F32).transpose(0, 2, 1)
    rate_o = jnp.exp(t_own[0]) / BLOCK
    decay_o = jnp.exp(-rate_o)
    scale_o = jnp.sqrt(-jnp.expm1(-2.0 * rate_o))
    b_o = scale_o * t_own[1]
    qu_o, rr_o = mine_sum[:NST], mine_sum[NST : 2 * NST]
    gb = t_own[2] * qu_o
    log_rate_grad = rate_o * (
        -decay_o * t_own[2] * b_o * rr_o + decay_o * decay_o / scale_o * t_own[1] * gb
    )
    state_grad = jnp.stack([log_rate_grad, scale_o * gb, b_o * qu_o]).transpose(0, 2, 1)
    gain_grad = mine_sum[2 * NST :]

    grad_part, state_grad, gain_grad, output, token_grad = lax.optimization_barrier(
        (grad_part, state_grad, gain_grad, output, token_grad)
    )
    here, there, give_here, give_there = (grad_part[96 * k : 96 * k + 96] for k in range(4))
    own, give, squares = finish(
        info, here, flip(give_here, "y"), flip(there, "grp"), lax.ppermute(give_there, ("grp", "y"), across),
        state_grad, gain_grad,
    )
    squares, own, got = lax.optimization_barrier((squares + swap(squares), own, swap(give)))
    every = lax.all_to_all(squares, ("grp",) + CHIPS, split_axis=0, concat_axis=0, tiled=True)
    new = update(
        info,
        (attn_weight, up_weight, down_weight, state_param, norm_gain),
        (attn_first, up_first, down_first, state_first, gain_first),
        (attn_second, up_second, down_second, state_second, gain_second),
        (every, own, got, flip(own, "grp"), flip(got, "grp"), state_grad, gain_grad),
    )
    return (output[None], token_grad[None], new[20][0, 0]) + tuple(new[:20])


def solution(mesh):
    inner = Mesh(mesh.devices.reshape(2, 2, 4, 4, 2), AXES)
    rows = P("grp", None, SHARD, None)
    attn = P(None, SHARD, None)
    flat = P(SHARD, None)
    gain = P(None, SHARD)
    in_specs = (rows, rows, P("grp", None), attn, flat, flat, attn, gain)
    in_specs += (attn, attn, flat, flat, flat, flat, attn, attn, gain, gain)
    out_specs = (rows, rows, P()) + (attn,) * 4 + (flat,) * 8 + (attn,) * 4 + (gain,) * 4
    return jax.shard_map(body, mesh=inner, in_specs=in_specs, out_specs=out_specs, check_vma=False)
```

```python
import jax
import jax.numpy as jnp
from jax import lax
from jax.experimental import pallas as pl
from jax.experimental.pallas import tpu as pltpu
from jax.sharding import Mesh
from jax.sharding import PartitionSpec as P

HEAD_DIM = 128
BLOCK = 512
STEP = 5
SLOT = 2048

EPS_NORM = 1e-05
BETA_ONE = 0.5
BETA_TWO = 0.5
ADAM_EPS = 1e-08
WEIGHT_DECAY = 0.1
CLIP_NORM = 0.5
RATE_MATRIX = 0.02
RATE_STATE = 1.0
RATE_GAIN = 0.6
MASKED = -1e30

AXES = ("grp", "y", "z", "x", "core")
CHIPS = ("y", "z", "x")
SHARD = ("y", "z", "x", "core")
BF = jnp.bfloat16
F32 = jnp.float32
NST = 16
ROWS = 256
HALF = 512


def flip(v, axis, kind="a"):
    if lax.axis_size(axis) == 2:
        pairs = [(0, 1), (1, 0)]
    elif kind == "c":
        pairs = [(0, 2), (2, 0), (1, 3), (3, 1)]
    elif kind == "a":
        pairs = [(0, 1), (1, 0), (2, 3), (3, 2)]
    else:
        pairs = [(0, 3), (3, 0), (1, 2), (2, 1)]
    return lax.ppermute(v, axis, pairs)


def swap(v):
    return flip(v, "core")


def ordered(bit, own, other, axis):
    first = jnp.where(bit == 0, own, other)
    second = jnp.where(bit == 0, other, own)
    return jnp.concatenate([first, second], axis=axis)


def rms_scale(value):
    return lax.rsqrt(jnp.mean(value * value, axis=-1, keepdims=True) + EPS_NORM)


def norm_back(grad, value, inverse, gain):
    unit = value * inverse
    scaled = grad * gain
    return inverse * (scaled - unit * jnp.mean(scaled * unit, axis=-1, keepdims=True))


def dot(left, right):
    return jnp.dot(left, right, preferred_element_type=F32)


def dot_nt(left, right):
    return lax.dot_general(left, right, (((1,), (1,)), ((), ())), preferred_element_type=F32)


def dot_tn(left, right):
    return lax.dot_general(left, right, (((0,), (0,)), ((), ())), preferred_element_type=F32)


def params(mib=16):
    return pltpu.CompilerParams(vmem_limit_bytes=mib * 1024 * 1024)


BIG = 53


def cost(flops, bytes_accessed):
    return pl.CostEstimate(flops=flops, bytes_accessed=bytes_accessed, transcendentals=0)


def sds(shape, dtype):
    return jax.ShapeDtypeStruct(shape, dtype)


SMEM = pl.BlockSpec(memory_space=pltpu.SMEM)
FULL = pl.BlockSpec(memory_space=pltpu.VMEM)


def live_of(info, half):
    return (lax.broadcasted_iota(jnp.int32, (ROWS, 1), 0) + half * ROWS < info[1]).astype(F32)


def at(ref, t):
    return ref[pl.ds(t, 8, stride=ROWS), :]


def tree(terms):
    while len(terms) > 1:
        terms = [terms[i] + terms[i + 1] for i in range(0, len(terms), 2)]
    return terms[0]


def first_kernel(info, x_ref, gain_ref, a_ref, low_ref, us_ref, e_ref, f_ref):
    for lane in range(2):
        x = x_ref[lane].astype(F32)
        unit = x * rms_scale(x)
        low_ref[lane] = (unit * gain_ref[...]).astype(BF)
        half = jnp.where(info[0] == 0, unit[:, :HALF], unit[:, HALF:])
        for g in range(4):
            us_ref[pl.ds((lane * 4 + g) * ROWS, ROWS), :] = half[:, g * 128 : (g + 1) * 128]
    half = NST // 2
    for base in (0, half):
        a = [a_ref[base + n] for n in range(half)]

        def step(t, held):
            e, f = held
            u = at(us_ref, t)
            f = tuple(a[n] * (f[n] + e[n]) for n in range(half))
            e = tuple(a[n] * e[n] + u for n in range(half))
            return e, f

        zero = tuple(jnp.zeros((8, 128), F32) for _ in range(half))
        e, f = lax.fori_loop(0, ROWS, step, (zero, zero), unroll=4)
        for n in range(half):
            e_ref[base + n] = e[n]
            f_ref[base + n] = f[n]


STATE = sds((NST, 8, 128), F32)
SPREAD = sds((9 * ROWS, 128), F32)


def first(info, x, gain, a):
    return pl.pallas_call(
        first_kernel,
        out_shape=(sds((2, ROWS, 1024), BF), SPREAD, STATE, STATE),
        in_specs=[SMEM, FULL, FULL, FULL],
        compiler_params=params(),
        cost_estimate=cost(32_000_000, 3_000_000),
        name="first",
    )(info, x, gain, a)


def run_kernel(us, a_ref, cb_ref, h_ref, s_ref, ss):
    def step(t, h):
        u = at(us, t)
        h = tuple(a_ref[n] * h[n] + u for n in range(NST))
        ss[pl.ds(t, 8, stride=ROWS), :] = tree([cb_ref[n] * h[n] for n in range(NST)])
        return h

    lax.fori_loop(0, ROWS, step, tuple(h_ref[n] for n in range(NST)), unroll=4)
    for lane in range(2):
        for g in range(4):
            s_ref[lane, :, g * 128 : (g + 1) * 128] = ss[pl.ds((lane * 4 + g) * ROWS, ROWS), :].astype(BF)


def state_run(us, a, cb, h):
    return pl.pallas_call(
        run_kernel,
        out_shape=sds((2, ROWS, HALF), BF),
        scratch_shapes=[pltpu.VMEM((9 * ROWS, 128), F32)],
        compiler_params=params(),
        cost_estimate=cost(32_000_000, 2_000_000),
        name="state_run",
    )(us, a, cb, h)


def turn_kernel(keep_ref, got_ref, a_ref, ds_ref, e_ref):
    for half in range(2):
        d = added(keep_ref[0, half], got_ref[0, half])
        for g in range(4):
            ds_ref[pl.ds((half * 4 + g) * ROWS, ROWS), :] = d[:, g * 128 : (g + 1) * 128]
    a = [a_ref[n] for n in range(NST)]

    def step(i, h):
        d = at(ds_ref, ROWS - 1 - i)
        return tuple(a[n] * h[n] + d for n in range(NST))

    h = lax.fori_loop(0, ROWS, step, tuple(jnp.zeros((8, 128), F32) for _ in range(NST)), unroll=4)
    for n in range(NST):
        e_ref[n] = h[n]


def state_turn(keep, got, a):
    return pl.pallas_call(
        turn_kernel,
        out_shape=(SPREAD, STATE),
        compiler_params=params(),
        cost_estimate=cost(16_000_000, 4_000_000),
        name="state_turn",
    )(keep, got, a)


def mid_kernel(base, us, ds, a_ref, cb_ref, h_ref, dus_in, dus, qu_ref, r_ref):
    half = NST // 2
    a = [a_ref[base + n] for n in range(half)]

    def step(i, held):
        q, v, qu, r = held
        t = ROWS - 1 - i
        u, d = at(us, t), at(ds, t)
        v = tuple(a[n] * v[n] + q[n] for n in range(half))
        q = tuple(a[n] * q[n] + d for n in range(half))
        du = tree([cb_ref[base + n] * q[n] for n in range(half)])
        dus[pl.ds(t, 8, stride=ROWS), :] = at(dus_in, t) + du
        qu = tuple(qu[n] + q[n] * u for n in range(half))
        r = tuple(r[n] + v[n] * u for n in range(half))
        return (q, v, qu, r)

    zero = tuple(jnp.zeros((8, 128), F32) for _ in range(half))
    q, v, qu, r = lax.fori_loop(0, ROWS, step, (zero,) * 4, unroll=2)
    for n in range(half):
        qu_ref[n] = qu[n]
        r_ref[n] = r[n] + h_ref[base + n] * (a[n] * v[n] + q[n])


def mid_first_kernel(us, ds, a_ref, cb_ref, h_ref, keep_ref, got_ref, dus, qu_ref, r_ref, g_ref, dq):
    for half in range(2):
        du = added(keep_ref[1, half], got_ref[1, half])
        for g in range(4):
            k = half * 4 + g
            piece = du[:, g * 128 : (g + 1) * 128]
            dq[pl.ds(k * ROWS, ROWS), :] = piece
            g_ref[k : k + 1, :] = jnp.sum(piece * us[pl.ds(k * ROWS, ROWS), :], axis=0, keepdims=True)
    mid_kernel(0, us, ds, a_ref, cb_ref, h_ref, dq, dus, qu_ref, r_ref)


def state_mid(us, ds, a, cb, h, keep, got):
    part = sds((NST // 2, 8, 128), F32)
    return pl.pallas_call(
        mid_first_kernel,
        out_shape=(SPREAD, part, part, sds((8, 128), F32)),
        scratch_shapes=[pltpu.VMEM((9 * ROWS, 128), F32)],
        compiler_params=params(),
        cost_estimate=cost(40_000_000, 4_000_000),
        name="state_mid_0",
    )(us, ds, a, cb, h, keep, got)


def state_mid_more(us, ds, a, cb, h, dus):
    part = sds((NST // 2, 8, 128), F32)
    return pl.pallas_call(
        lambda *refs: mid_kernel(NST // 2, *refs),
        out_shape=(SPREAD, part, part),
        compiler_params=params(),
        cost_estimate=cost(40_000_000, 4_000_000),
        name="state_mid_1",
    )(us, ds, a, cb, h, dus)


def fix_kernel(info, q_ref, a_ref, cb_ref, e_ref, f_ref, h_ref, far_ref, qu_0, qu_1, r_0, r_1, g_ref, gain, gain_two, out):
    half = NST // 2

    def halved(v):
        return jnp.where(info[0] == 0, v[:, :HALF], v[:, HALF:])

    def put(row, v, scale):
        both = v[:4] + v[4:]
        for g in range(4):
            at_c = slice(g * 128, (g + 1) * 128)
            value = both[g : g + 1]
            out[row : row + 1, at_c] = value * scale[:, at_c] if scale is not None else value

    gain_c = halved(gain[...])
    total = g_ref[...]
    for n in range(NST):
        q = q_ref[n]
        qu = (qu_0, qu_1)[n // half][n % half] + q * a_ref[n] * e_ref[n]
        r = (r_0, r_1)[n // half][n % half] + q * (f_ref[n] + h_ref[n] * (float(ROWS) * far_ref[n]))
        total = total + cb_ref[n] * qu
        put(n, qu, gain_c)
        put(NST + n, r, gain_c)
    put(2 * NST, total, None)
    out[2 * NST + 1 :] = halved(gain_two[...])


def state_fix(info, q, a, cb, e, f, h, far, qu, r, g, gain, gain_two):
    return pl.pallas_call(
        fix_kernel,
        out_shape=sds((2 * NST + 2, HALF), F32),
        in_specs=[SMEM] + [FULL] * 14,
        compiler_params=params(),
        cost_estimate=cost(1_000_000, 1_000_000),
        name="state_fix",
    )(info, q, a, cb, e, f, h, far, *qu, *r, g, gain, gain_two)


def last_kernel(info, dus, a_ref, cb_ref, q_ref, mine_ref, give_ref, out):
    def step(i, q):
        t = ROWS - 1 - i
        q = tuple(a_ref[n] * q[n] for n in range(NST))
        out[pl.ds(t, 8, stride=ROWS), :] = at(dus, t) + tree([cb_ref[n] * q[n] for n in range(NST)])
        return q

    lax.fori_loop(0, ROWS, step, tuple(q_ref[n] for n in range(NST)), unroll=4)
    mine = pl.multiple_of(info[0] * 128, 128)
    give = pl.multiple_of((1 - info[0]) * 128, 128)
    for lane in range(2):
        for g in range(4):
            base = (lane * 4 + g) * ROWS
            at_c = slice(g * 128, (g + 1) * 128)
            mine_ref[lane, :, at_c] = out[pl.ds(base + mine, 128), :]
            give_ref[lane, :, at_c] = out[pl.ds(base + give, 128), :]


def state_last(info, dus, a, cb, q):
    half = sds((2, 128, HALF), F32)
    return pl.pallas_call(
        last_kernel,
        out_shape=(half, half),
        in_specs=[SMEM] + [FULL] * 4,
        scratch_shapes=[pltpu.VMEM((9 * ROWS, 128), F32)],
        compiler_params=params(),
        cost_estimate=cost(32_000_000, 2_000_000),
        name="state_last",
    )(info, dus, a, cb, q)


def added(left, right):
    return left.astype(F32) + right.astype(F32)


def wide(v):
    return v.reshape(v.shape[0] * v.shape[1], v.shape[2])


class Weights:
    def __init__(self, info, full_ref, w, sems):
        self.y, self.full, self.w, self.sems = info[3], full_ref, w, sems
        self.copies = {}

    def start(self, order):
        for n in order:
            rows, cols = pl.ds(128 + 32 * (n // 2), 32), pl.ds(HALF * (n % 2), HALF)
            self.copies[n] = [
                pltpu.make_async_copy(self.full.at[:, r, rows, cols], self.w.at[n, r], self.sems.at[n, r])
                for r in range(2)
            ]
            for c in self.copies[n]:
                c.start()

    def wait(self, n):
        for c in self.copies[n]:
            c.wait()

    def half(self, n, half):
        return wide(self.w[n, half ^ self.y])

    def out(self, half):
        return wide(self.w[3, half])


WEIGHTS = [pltpu.VMEM((4, 2, 16, 32, HALF), BF), pltpu.SemaphoreType.DMA((4, 2))]
HBM = pl.BlockSpec(memory_space=pltpu.HBM)


def bring(pairs, sems):
    sems = sems if isinstance(sems, list) else [sems.at[n] for n in range(len(pairs))]
    copies = [pltpu.make_async_copy(src, dst, sem) for (src, dst), sem in zip(pairs, sems)]
    for copy in copies:
        copy.start()
    return copies


INPUTS = [pltpu.VMEM((2, ROWS, 1024), BF)] + [pltpu.VMEM((2 * ROWS, HALF), BF)] * 2 + [pltpu.SemaphoreType.DMA((6,))]


def used(p_ref, half):
    return p_ref.at[half, :, :, pl.ds(0, ROWS * (half + 1))]


def attn_kernel(
    info, u_in, own_in, sib_in, full_ref, part_ref, q_out, k_out, v_out, o_out, p_out,
    q_ref, k_ref, v_ref, o_ref, p_ref, out_sems, w_s, sems, u_ref, own, sib, in_sems,
):
    w = Weights(info, full_ref, w_s, sems)
    w.start((0,))
    arriving = bring(((u_in, u_ref), (own_in, own), (sib_in, sib)), in_sems)
    w.start((1, 2, 3))
    me, it = info[0], 1 - info[0]
    leaving = []

    def leave(src, dst, *place):
        copy = pltpu.make_async_copy(src, dst, out_sems.at[place])
        copy.start()
        leaving.append(copy)

    arriving[0].wait()
    w.wait(0)
    for half in range(2):
        u = u_ref[half]
        q_ref[half] = (dot(u[:, :HALF], w.half(0, 0)) + dot(u[:, HALF:], w.half(0, 1))).astype(BF)
    leave(q_ref, q_out, 0, 0)
    for copy in arriving[1:]:
        copy.wait()
    for n, ref, out in ((1, k_ref, k_out), (2, v_ref, v_out)):
        w.wait(n)
        ref[...] = (dot(own[...], w.half(n, me)) + dot(sib[...], w.half(n, it))).astype(BF)
        leave(ref, out, n, 0)
    w.wait(3)
    for half in range(2):
        seen = ROWS * (half + 1)
        row = lax.broadcasted_iota(jnp.int32, (ROWS, seen), 0) + half * ROWS
        allowed = lax.broadcasted_iota(jnp.int32, (ROWS, seen), 1) <= row
        for h in range(4):
            at_h = slice(h * HEAD_DIM, (h + 1) * HEAD_DIM)
            s = dot_nt(q_ref[half, :, at_h], k_ref[:seen, at_h]) * HEAD_DIM**-0.5
            s = jnp.where(allowed, s, MASKED)
            e = jnp.exp(s - jnp.max(s, axis=-1, keepdims=True))
            p = (e / jnp.sum(e, axis=-1, keepdims=True)).astype(BF)
            p_ref[half, h, :, :seen] = p
            o_ref[half, :, at_h] = dot(p, v_ref[:seen, at_h]).astype(BF)
        leave(used(p_ref, half), used(p_out, half), 3, half)
        leave(o_ref.at[half], o_out.at[half], 4, half)
        o = o_ref[half]
        for side in range(2):
            part_ref[half, :, side * HALF : (side + 1) * HALF] = dot(o, w.out(side)).astype(BF)
    for copy in leaving:
        copy.wait()


KEPT = [
    pltpu.VMEM((2, ROWS, HALF), BF), pltpu.VMEM((2 * ROWS, HALF), BF), pltpu.VMEM((2 * ROWS, HALF), BF),
    pltpu.VMEM((2, ROWS, HALF), BF), pltpu.VMEM((2, 4, ROWS, 2 * ROWS), BF), pltpu.SemaphoreType.DMA((5, 2)),
]


def attention(info, u, own, sib, full):
    return pl.pallas_call(
        attn_kernel,
        out_shape=(
            sds((2, ROWS, 1024), BF), sds((2, ROWS, HALF), BF), sds((2 * ROWS, HALF), BF),
            sds((2 * ROWS, HALF), BF), sds((2, ROWS, HALF), BF), sds((2, 4, ROWS, 2 * ROWS), BF),
        ),
        in_specs=[SMEM] + [HBM] * 4,
        out_specs=(FULL, HBM, HBM, HBM, HBM, HBM),
        scratch_shapes=KEPT + WEIGHTS + INPUTS,
        compiler_params=params(BIG),
        cost_estimate=cost(4_000_000_000, 16_000_000),
        name="attention",
    )(info, u, own, sib, full)


def attn_back_kernel(
    info, own_in, sib_in, mid_in, dy_in, gain_ref, full_ref, q_in, k_in, v_in, o_in, p_in,
    os_in, u_in, so_in, ss_in, held_ref, dm_out, g_ref, dq_out, dk_out, dv_out, grad_ref,
    q_ref, k_ref, v_ref, o_ref, p_ref, in_sems, w_s, sems, grads, out_sems,
    u_ref, s_own, s_sib, late_sems, os_ref, own_ref, sib_ref, mid_ref, dy_ref, dm_ref, first_sems,
    dq_ref, dk_ref, dv_ref, made_sems,
):
    del held_ref
    early = []
    for lane in range(2):
        pairs = ((own_in, own_ref), (sib_in, sib_ref), (mid_in, mid_ref), (dy_in, dy_ref))
        early.append(bring([(a.at[lane], b.at[lane]) for a, b in pairs], first_sems.at[lane]))
    w = Weights(info, full_ref, w_s, sems)
    w.start((3,))
    pairs = ((v_in, v_ref), (k_in, k_ref), (q_in, q_ref), (o_in, o_ref))
    pairs += tuple((used(p_in, half), used(p_ref, half)) for half in range(2))
    arriving = bring(pairs, [in_sems.at[n, 0] for n in range(5)] + [in_sems.at[0, 1]])
    me, it = info[0], 1 - info[0]
    scale = HEAD_DIM**-0.5
    gain_grad = jnp.zeros((1, 1024), F32)
    branches = []
    leaving = []

    def leave(src, dst, sem):
        copy = pltpu.make_async_copy(src, dst, sem)
        copy.start()
        leaving.append(copy)

    for lane in range(2):
        for copy in early[lane]:
            copy.wait()
        if lane == 1:
            late = bring(((u_in, u_ref), (so_in, s_own), (ss_in, s_sib), (os_in, os_ref)), late_sems)
        m = mid_ref[lane]
        dz = added(own_ref[lane], sib_ref[lane])
        inverse = rms_scale(m)
        unit = m * inverse
        gain_grad = gain_grad + jnp.sum(dz * unit, axis=0, keepdims=True)
        scaled = dz * gain_ref[...]
        dm = dy_ref[lane].astype(F32) + inverse * (
            scaled - unit * jnp.mean(scaled * unit, axis=-1, keepdims=True)
        )
        dm_ref[lane] = dm
        own_rows = pl.ds(pl.multiple_of(info[0] * 128, 128), 128)
        leave(dm_ref.at[lane, own_rows], dm_out.at[lane], made_sems.at[0, lane])
        branch = (live_of(info, lane) * dm).astype(BF)
        branches.append(branch)
    g_ref[...] = gain_grad
    w.wait(3)
    for copy in arriving:
        copy.wait()
    d_o = []
    for half in range(2):
        branch = branches[half]
        d_o.append((dot_nt(branch[:, :HALF], w.out(0)) + dot_nt(branch[:, HALF:], w.out(1))).astype(BF))
    for h in range(4):
        at_h = slice(h * HEAD_DIM, (h + 1) * HEAD_DIM)
        dk, dv = [], []
        for half in range(2):
            seen = ROWS * (half + 1)
            p_low = p_ref[half, h, :, :seen]
            p = p_low.astype(F32)
            d_o_h = d_o[half][:, at_h]
            dp = dot_nt(d_o_h, v_ref[:seen, at_h])
            total = jnp.sum(p * dp, axis=-1, keepdims=True)
            ds = (p * (dp - total)).astype(BF)
            dq_ref[half, :, at_h] = (dot(ds, k_ref[:seen, at_h]) * scale).astype(BF)
            dk.append(dot_tn(ds, q_ref[half, :, at_h]))
            dv.append(dot_tn(p_low, d_o_h))
        for ref, parts, factor in ((dk_ref, dk, scale), (dv_ref, dv, 1.0)):
            ref[:ROWS, at_h] = ((parts[0] + parts[1][:ROWS]) * factor).astype(BF)
            ref[ROWS:, at_h] = (parts[1][ROWS:] * factor).astype(BF)
    for n, (src, dst) in enumerate(((dq_ref, dq_out), (dk_ref, dk_out), (dv_ref, dv_out))):
        leave(src, dst, made_sems.at[1 + n, 0])

    def leave_grad(n):
        at_r = pl.ds(pl.multiple_of(info[8 + n // 2], 32), 32)
        at_c = pl.ds(HALF * (n % 2), HALF)
        for y in range(2):
            leave(grads.at[n, y], grad_ref.at[:, y ^ info[3], at_r, at_c], out_sems.at[n, y])

    def put(n, half, value):
        grads[n, pl.ds(half, 1)] = value.astype(BF).reshape(1, 16, 32, HALF)

    for copy in late:
        copy.wait()
    branch = jnp.concatenate(branches, axis=0)
    branch = jnp.where(info[0] == 0, branch[:, :HALF], branch[:, HALF:])
    for half, ref in ((me, o_ref), (it, os_ref)):
        put(3, half, dot_tn(wide(ref[...]), branch))
    leave_grad(3)
    for n, ref in ((1, dk_ref), (2, dv_ref)):
        for half, s_c in ((me, s_own), (it, s_sib)):
            put(n, half, dot_tn(s_c[...], ref[...]))
        leave_grad(n)
    for half in range(2):
        put(0, half, dot_tn(wide(u_ref[...])[:, half * HALF : (half + 1) * HALF], wide(dq_ref[...])))
    leave_grad(0)
    for copy in leaving:
        copy.wait()


def attention_back(info, own, sib, mid, dy, gain, full, q, k, v, o, p, o_sib, u, s_own, s_sib, held):
    return pl.pallas_call(
        attn_back_kernel,
        out_shape=(
            sds((2, 128, 1024), F32), sds((1, 1024), F32), sds((2, ROWS, HALF), BF),
            sds((2 * ROWS, HALF), BF), sds((2 * ROWS, HALF), BF), sds(held.shape, BF),
        ),
        in_specs=[SMEM] + [HBM] * 4 + [FULL] + [HBM] * 11,
        out_specs=(HBM, FULL, HBM, HBM, HBM, HBM),
        input_output_aliases={16: 5},
        scratch_shapes=KEPT + WEIGHTS + WEIGHTS + INPUTS + [
            pltpu.VMEM((2, ROWS, HALF), BF), pltpu.VMEM((2, ROWS, 1024), BF), pltpu.VMEM((2, ROWS, 1024), BF),
            pltpu.VMEM((2, ROWS, 1024), F32), pltpu.VMEM((2, ROWS, 1024), BF), pltpu.VMEM((2, ROWS, 1024), F32),
            pltpu.SemaphoreType.DMA((2, 4)),
            pltpu.VMEM((2, ROWS, HALF), BF), pltpu.VMEM((2 * ROWS, HALF), BF), pltpu.VMEM((2 * ROWS, HALF), BF),
            pltpu.SemaphoreType.DMA((4, 2)),
        ],
        compiler_params=params(BIG),
        cost_estimate=cost(6_000_000_000, 24_000_000),
        name="attention_back",
    )(info, own, sib, mid, dy, gain, full, q, k, v, o, p, o_sib, u, s_own, s_sib, held)


def inputs_back_kernel(
    info, dq_in, dk_in, dv_in, full_ref, keep_ref, send_ref, w_s, sems, dq_ref, dk_ref, dv_ref, in_sems
):
    w = Weights(info, full_ref, w_s, sems)
    w.start((1, 2))
    arriving = bring(((dk_in, dk_ref), (dv_in, dv_ref), (dq_in, dq_ref)), in_sems)
    w.start((0,))
    for copy in arriving:
        copy.wait()
    for n in (1, 2):
        w.wait(n)
    for ref, half in ((send_ref, 1 - info[0]), (keep_ref, info[0])):
        ds = dot_nt(dk_ref[...], w.half(1, half)) + dot_nt(dv_ref[...], w.half(2, half))
        ref[0] = ds.astype(BF).reshape(2, ROWS, HALF)
    w.wait(0)
    for ref, half in ((send_ref, 1 - info[0]), (keep_ref, info[0])):
        ref[1] = dot_nt(wide(dq_ref[...]), w.half(0, half)).astype(BF).reshape(2, ROWS, HALF)


def inputs_back(info, dq, dk, dv, full):
    return pl.pallas_call(
        inputs_back_kernel,
        out_shape=(sds((2, 2, ROWS, HALF), BF), sds((2, 2, ROWS, HALF), BF)),
        in_specs=[SMEM] + [HBM] * 4,
        scratch_shapes=WEIGHTS + [
            pltpu.VMEM((2, ROWS, HALF), BF), pltpu.VMEM((2 * ROWS, HALF), BF), pltpu.VMEM((2 * ROWS, HALF), BF),
            pltpu.SemaphoreType.DMA((3,)),
        ],
        compiler_params=params(BIG),
        cost_estimate=cost(2_000_000_000, 7_000_000),
        name="inputs_back",
    )(info, dq, dk, dv, full)


GELU_C = 0.7978845608028654
GELU_K = 0.044715


def ffn_kernel(
    info, x_ref, part_ref, sib_ref, gain_ref, dy_ref, up_ref, down_ref,
    mid_out, dz_ref, hidden_ref, grad_ref, z_s, d_s, dz_s, gu_s, gd_s, sems, mid_ref, mid_sems,
):
    step = pl.program_id(0)

    def mid_copy(k):
        return pltpu.make_async_copy(mid_ref.at[k], mid_out.at[k], mid_sems.at[k])

    slot = step % 2
    place, near = step % 2, step // 2
    side = near ^ info[3]

    def copies(slot, place, near):
        at_c = pl.ds(pl.multiple_of(place * HALF, HALF), HALF)
        at_r = pl.ds(pl.multiple_of(info[5 + (near ^ info[3])], 32), 32)
        at_z = pl.ds(place * 8, 8)
        made = [pltpu.make_async_copy(gu_s.at[slot], grad_ref.at[:, :, at_r, at_c], sems.at[0, slot])]
        for k in range(2):
            at_r = pl.ds(pl.multiple_of(info[7 + 3 * k], 32), 32)
            src = gd_s.at[slot, :, pl.ds(32 * k, 32), :]
            made.append(pltpu.make_async_copy(src, grad_ref.at[at_z, near, at_r, :], sems.at[1 + k, slot]))
        return made

    @pl.when(step == 0)
    def _():
        for lane in range(2):
            live = live_of(info, lane)
            m = x_ref[lane].astype(F32) + live * added(part_ref[lane], sib_ref[lane])
            mid_ref[lane] = m
            mid_copy(lane).start()
            z_s[lane * ROWS : (lane + 1) * ROWS] = (m * rms_scale(m) * gain_ref[...]).astype(BF)
            d_s[lane * ROWS : (lane + 1) * ROWS] = (live * dy_ref[lane].astype(F32)).astype(BF)
        dz_s[...] = jnp.zeros_like(dz_s)

    z, d = z_s[...], d_s[...]
    down = wide(down_ref[:, 0])
    up_0, up_1 = (up_ref[:, pl.ds(y ^ info[3], 1)].reshape(HALF, HALF) for y in range(2))
    f = dot(z[:, :HALF], up_0) + dot(z[:, HALF:], up_1)
    square = f * f
    h = 0.5 + 0.5 * jnp.tanh(GELU_C * f + (GELU_C * GELU_K) * f * square)
    hidden = (f * h).astype(BF)
    slope = h + (h - h * h) * (2.0 * GELU_C * f + (6.0 * GELU_C * GELU_K) * f * square)
    hidden_ref[...] = hidden
    back = (slope * dot_nt(d, down)).astype(BF)

    @pl.when(step >= 2)
    def _():
        for c in copies(slot, place, near):
            c.wait()

    gd_s[slot] = dot_tn(hidden, d).astype(BF).reshape(8, 64, 1024)
    gu = dot_tn(z, back).astype(BF).reshape(2, 16, 32, HALF)
    for y in range(2):
        gu_s[slot, :, pl.ds(y ^ info[3], 1)] = gu[y].reshape(16, 1, 32, HALF)
    for c in copies(slot, place, near):
        c.start()
    dz_s[:, :HALF] += dot_nt(back, up_0)
    dz_s[:, HALF:] += dot_nt(back, up_1)

    @pl.when(step == pl.num_programs(0) - 1)
    def _():
        for lane in range(2):
            dz_ref[lane] = dz_s[lane * ROWS : (lane + 1) * ROWS].astype(BF)
            mid_copy(lane).wait()
        for k in range(2):
            for c in copies(k, place, near):
                c.wait()


def feed_forward(info, x, part, sib, gain, dy, weights):
    chunk = pl.BlockSpec((2 * ROWS, HALF), lambda i, info: (0, i))
    return pl.pallas_call(
        ffn_kernel,
        grid_spec=pltpu.PrefetchScalarGridSpec(
            num_scalar_prefetch=1,
            grid=(4,),
            in_specs=[
                FULL, FULL, FULL, FULL, FULL,
                pl.BlockSpec((16, 2, 32, HALF), lambda i, info: (0, 0, (i // 2) ^ info[3], i % 2)),
                pl.BlockSpec((8, 1, 64, 1024), lambda i, info: (i % 2, i // 2, 1, 0)),
            ],
            out_specs=(HBM, FULL, chunk, HBM),
            scratch_shapes=[
                pltpu.VMEM((2 * ROWS, 1024), BF), pltpu.VMEM((2 * ROWS, 1024), BF), pltpu.VMEM((2 * ROWS, 1024), F32),
                pltpu.VMEM((2, 16, 2, 32, HALF), BF), pltpu.VMEM((2, 8, 64, 1024), BF),
                pltpu.SemaphoreType.DMA((3, 2)),
                pltpu.VMEM((2, ROWS, 1024), F32), pltpu.SemaphoreType.DMA((2,)),
            ],
        ),
        out_shape=(
            sds((2, ROWS, 1024), F32), sds((2, ROWS, 1024), BF), sds((2 * ROWS, 2048), BF),
            sds((16, 2, 192, 1024), BF),
        ),
        compiler_params=params(BIG),
        cost_estimate=cost(9_000_000_000, 28_000_000),
        name="feed_forward",
    )(info, x, part, sib, gain, dy, weights, weights)


DOWN = pl.BlockSpec((8, 1, 64, 1024), lambda i: (i % 2, i // 2, 1, 0))
CHUNK = pl.BlockSpec((2 * ROWS, HALF), lambda i: (0, i))


def hidden_out_kernel(info, hidden_ref, mid_ref, down_ref, keep_ref, send_ref, out_s):
    step = pl.program_id(0)
    more = dot(hidden_ref[...], wide(down_ref[:, 0]))

    @pl.when(step == 0)
    def _():
        out_s[...] = more

    @pl.when(step > 0)
    def _():
        out_s[...] += more

    @pl.when(step == pl.num_programs(0) - 1)
    def _():
        for half in range(2):
            out = live_of(info, half) * out_s[half * ROWS : (half + 1) * ROWS]
            total = out + mid_ref[half]
            keep_ref[half] = jnp.where(info[0] == 0, total[:128], total[128:])
            send_ref[half] = jnp.where(info[0] == 0, out[128:], out[:128]).astype(BF)


def hidden_out(info, hidden, mid, weights):
    return pl.pallas_call(
        hidden_out_kernel,
        grid=(4,),
        out_shape=(sds((2, 128, 1024), F32), sds((2, 128, 1024), BF)),
        in_specs=[SMEM, CHUNK, FULL, DOWN],
        out_specs=(FULL, FULL),
        scratch_shapes=[pltpu.VMEM((2 * ROWS, 1024), F32)],
        compiler_params=params(BIG),
        cost_estimate=cost(2_100_000_000, 8_000_000),
        name="hidden_out",
    )(info, hidden, mid, weights)


STEPS = (("x", "c"), ("z", "a"), ("z", "b"), ("y", "a"))


def carry(ends, far, rate, block, lane, reverse, between=None):
    low, high = ends[:, :4], ends[:, 4:]
    far, rate = far[:, :4], rate[:, :4]
    first, second = (high, low) if reverse else (low, high)
    total = far * first + second
    entering = jnp.zeros_like(total)
    for k, (axis, kind) in enumerate(STEPS):
        if between is not None:
            total = between(k, total)
        other = flip(total, axis, kind)
        upper = (block >> k) & 1
        within = block & ((1 << k) - 1)
        if reverse:
            takes, gap = upper == 0, (1 << k) - 1 - within
        else:
            takes, gap = upper == 1, within
        reach = jnp.exp(-rate * (BLOCK * gap).astype(F32)) * other
        whole = jnp.exp(-rate * float(BLOCK << k))
        joined = whole * jnp.where(takes, other, total) + jnp.where(takes, total, other)
        if k >= 2:
            reach = jnp.where(lane == 1, 0.0, reach)
            joined = jnp.where(lane == 1, 0.0, joined)
        entering = entering + jnp.where(takes, reach, 0.0)
        total = joined
    inner = first + far * entering
    return jnp.concatenate([inner, entering] if reverse else [entering, inner], axis=1)


def adam(factor, w_ref, f_ref, s_ref, grad, outs, rate, decay):
    clipped = grad * factor
    first_new = BETA_ONE * f_ref[...] + (1.0 - BETA_ONE) * clipped
    second_new = BETA_TWO * s_ref[...] + (1.0 - BETA_TWO) * clipped * clipped
    fix_one = 1.0 - BETA_ONE**STEP
    fix_two = 1.0 - BETA_TWO**STEP
    direction = first_new / fix_one / (jnp.sqrt(second_new / fix_two) + ADAM_EPS)
    weight = w_ref[...]
    weight_new = weight - rate * (direction + decay * weight)
    for ref, v in zip(outs, (first_new, second_new, weight_new, weight_new.astype(BF))):
        ref[...] = v


def finish_kernel(info, mine, near, over, cross, state, gain, own_ref, give_ref, squares_ref):
    total = added(mine[...], near[...]) + added(over[...], cross[...])
    squares = jnp.sum(total * total, axis=0, keepdims=True)
    squares = jnp.sum(squares.reshape(1, 8, 128), axis=1)
    squares = jnp.sum(squares, axis=1, keepdims=True)
    for ref in (state, gain):
        piece = ref[...].reshape(-1, 16)
        piece = jnp.sum(piece * piece, axis=0, keepdims=True)
        squares = squares + 0.5 * jnp.sum(piece, axis=1, keepdims=True)
    squares_ref[...] = jnp.broadcast_to(squares, (64, 128))
    own_ref[32:] = total[64:]
    for k in range(2):
        low, high = total[32 * k : 32 * k + 16], total[32 * k + 16 : 32 * k + 32]
        own_ref[16 * k : 16 * k + 16] = jnp.where(info[0] == 0, low, high)
        give_ref[16 * k : 16 * k + 16] = jnp.where(info[0] == 0, high, low)


def finish(info, mine, near, over, cross, state, gain):
    return pl.pallas_call(
        finish_kernel,
        out_shape=(sds((64, 1024), F32), sds((32, 1024), F32), sds((64, 128), F32)),
        in_specs=[SMEM] + [FULL] * 6,
        compiler_params=params(),
        cost_estimate=cost(2_000_000, 3_000_000),
        name="finish",
    )(info, mine, near, over, cross, state, gain)


def update_kernel(info, *refs):
    ins, outs = refs[:22], refs[22:]
    weights, firsts, seconds = ins[:5], ins[5:10], ins[10:15]
    every, mine, got, mine_far, got_far, state, gain = ins[15:]
    norm = jnp.sqrt(jnp.sum(every[...], axis=0, keepdims=True)[:, :1])
    outs[20][...] = norm
    factor = jnp.minimum(1.0, CLIP_NORM / norm)
    zero = info[0] == 0
    here = info[11] == 0

    def pair(one, two):
        first, second = jnp.where(zero, one, two), jnp.where(zero, two, one)
        return first.reshape(2, 16, 1024), second.reshape(2, 16, 1024)

    down = jnp.concatenate(
        [jnp.where(here, mine[32:], mine_far[32:]), jnp.where(here, mine_far[32:], mine[32:])], axis=0
    )
    near, far = pair(mine[:32], got[...]), pair(mine_far[:32], got_far[...])
    first, second = (jnp.where(here, b, a) for a, b in zip(near, far))
    matrices = []
    for n in range(4):
        at_c = slice(HALF * (n % 2), HALF * (n % 2) + HALF)
        matrices.append(jnp.concatenate([first[n // 2, :, at_c], second[n // 2, :, at_c]], axis=1))
    attn_grad = jnp.stack(matrices)
    first, second = (jnp.where(here, a, b) for a, b in zip(near, far))
    pieces = []
    for side in range(2):
        for k in range(16):
            at_c = slice(64 * k, 64 * k + 64)
            pieces += [first[side, :, at_c], second[side, :, at_c]]
    up_grad = jnp.concatenate(pieces, axis=1)
    grads = (attn_grad, up_grad, down, state[...], gain[...])
    rates = ((RATE_MATRIX, WEIGHT_DECAY),) * 3 + ((RATE_STATE, 0.0), (RATE_GAIN, 0.0))
    for k in range(5):
        adam(factor, weights[k], firsts[k], seconds[k], grads[k], outs[4 * k : 4 * k + 4], *rates[k])


def update(info, weights, firsts, seconds, grads):
    shapes = []
    for w in weights:
        shapes += [sds(w.shape, F32)] * 3 + [sds(w.shape, BF)]
    return pl.pallas_call(
        update_kernel,
        out_shape=tuple(shapes) + (sds((1, 1), F32),),
        in_specs=[SMEM] + [FULL] * 22,
        compiler_params=pltpu.CompilerParams(vmem_limit_bytes=24 * 1024 * 1024),
        cost_estimate=cost(4_000_000, 6_000_000),
        name="update",
    )(info, *weights, *firsts, *seconds, *grads)


def body(
    tokens, cotangent, lengths, attn_weight, up_weight, down_weight, state_param, norm_gain,
    attn_first, attn_second, up_first, up_second, down_first, down_second,
    state_first, state_second, gain_first, gain_second,
):
    core = lax.axis_index("core")
    ybit = lax.axis_index("y")
    chip = (ybit * 4 + lax.axis_index("z")) * 4 + lax.axis_index("x")

    lane = chip % 2
    block = chip // 2

    def of_lane(v, which):
        return lax.dynamic_index_in_dim(v, which, 0, keepdims=False)

    def halves(mine, got):
        return jnp.stack([jnp.where(lane == 0, mine, got), jnp.where(lane == 0, got, mine)])

    x_give, dy_give = of_lane(tokens[0], 1 - lane), of_lane(cotangent[0], 1 - lane)
    x_give, dy_give, attn_weight, up_weight, down_weight, state_param, norm_gain = lax.optimization_barrier(
        (x_give, dy_give, attn_weight, up_weight, down_weight, state_param, norm_gain)
    )
    x_got, dy_got = flip(x_give, "x"), flip(dy_give, "x")

    mine = jnp.concatenate(
        [state_param.astype(BF).transpose(0, 2, 1).reshape(-1), norm_gain.astype(BF).reshape(-1)]
    )
    mine = jnp.pad(mine, (0, 1024 - mine.shape[0])).reshape(1, 8, 128)
    pair = ordered(core, mine, swap(mine), 0)
    small = lax.all_to_all(
        jnp.broadcast_to(pair[None], (32, 2, 8, 128)), CHIPS, split_axis=0, concat_axis=0, tiled=True
    ).reshape(64, 1024)
    theta = small[:, :768].reshape(64, 3, NST, 16).transpose(1, 2, 0, 3).reshape(3, NST, 1024).astype(F32)
    gains = small[:, 768:800].reshape(64, 2, 16).transpose(1, 0, 2).reshape(2, 1024).astype(F32)

    slot_blocks = SLOT // BLOCK
    live_len = lax.dynamic_index_in_dim(lengths[0], block // slot_blocks, 0, keepdims=False)
    live_rows = jnp.clip(live_len - (block % slot_blocks) * BLOCK, 0, BLOCK)
    live_rows = jnp.where(lane == 0, BLOCK, live_rows)
    group = lax.axis_index("grp")
    places = [((b + 3 * group) % 6) * 32 for b in range(6)]
    info = jnp.stack([core, live_rows, lane, ybit, chip] + places + [group]).astype(jnp.int32)

    attn_low = attn_weight.astype(BF)
    up_low = up_weight.astype(BF).reshape(16, 32, 2, 64).transpose(2, 0, 1, 3).reshape(2, 16, 2048)
    down_low = down_weight.astype(BF)
    qkv_keep = lax.dynamic_slice_in_dim(attn_low[:3], core * HALF, HALF, 2)
    qkv_give = lax.dynamic_slice_in_dim(attn_low[:3], (1 - core) * HALF, HALF, 2)
    qkv_chip = ordered(core, qkv_keep, swap(qkv_give), 1)
    out_chip = ordered(core, attn_low[3], swap(attn_low[3]), 0)
    up_keep = lax.dynamic_index_in_dim(up_low, core, 0, keepdims=False)
    up_give = lax.dynamic_index_in_dim(up_low, 1 - core, 0, keepdims=False)
    up_chip = ordered(core, up_keep, swap(up_give), 0)
    up_chip = up_chip.reshape(32, 2, 1024).transpose(1, 0, 2).reshape(64, 1024)
    qk_rows = jnp.concatenate([qkv_chip[0], qkv_chip[1]], axis=1)
    own_rows = jnp.concatenate([up_chip, down_low, qk_rows], axis=0)
    across = [(0, 3), (3, 0), (1, 2), (2, 1)]
    low = jnp.concatenate([own_rows[:96], out_chip[:, :HALF].reshape(16, 1024)], axis=0)
    high = jnp.concatenate([own_rows[96:], jnp.concatenate([qkv_chip[2], out_chip[:, HALF:]], axis=1)], axis=0)
    low, high, pair = lax.optimization_barrier((low, high, pair))
    low_got, high_got = flip(low, "y"), lax.ppermute(high, ("grp", "y"), across)
    out_got = jnp.concatenate([low_got[96:].reshape(32, HALF), high_got[64:, HALF:]], axis=1)
    out_rows = jnp.where(ybit == core, out_chip, out_got)
    own_last = jnp.concatenate([qkv_chip[2], out_rows[:, :HALF]], axis=1)
    other_last = jnp.concatenate([high_got[64:, :HALF], out_rows[:, HALF:]], axis=1)
    all_two = jnp.concatenate([own_rows, own_last, low_got[:96], high_got[:64], other_last], axis=0)
    all_two, x_got, dy_got = lax.optimization_barrier((all_two, x_got, dy_got))
    full = lax.all_gather(all_two.reshape(2, 192, 1024), ("z", "x"), axis=0)
    x_own, dy_own = (halves(of_lane(v[0], lane), got) for v, got in ((tokens, x_got), (cotangent, dy_got)))
    x = ordered(core, x_own, swap(x_own), 1)
    dy = ordered(core, dy_own, swap(dy_own), 1)

    theta_c = lax.dynamic_slice_in_dim(theta, core * HALF, HALF, 2).reshape(3, NST, 4, 128)
    theta_c = jnp.concatenate([theta_c, theta_c], axis=2)
    rate = jnp.exp(theta_c[0]) / BLOCK
    decay = jnp.exp(-rate)
    norm_scale = jnp.sqrt(-jnp.expm1(-2.0 * rate))
    cb = norm_scale * theta_c[1] * theta_c[2]
    far = jnp.exp(-rate * float(ROWS))
    gain_c = lax.dynamic_slice_in_dim(gains[0], core * HALF, HALF, 0).reshape(4, 128)
    gain_c = jnp.concatenate([gain_c, gain_c], axis=0)

    u_low, us, ended, ramp = first(info, x, gains[:1], decay)
    entering = carry(ended, far, rate, block, lane, False)
    entering, dy = lax.optimization_barrier((entering, dy))
    sb_own = state_run(us, decay, cb * gain_c, entering).reshape(2 * ROWS, HALF)
    sb_sib = swap(sb_own)

    part, q, k, v, o, p = attention(info, u_low, sb_own, sb_sib, full)
    part_sib, o_sib = lax.optimization_barrier((swap(part), swap(o)))
    middle, dz_part, hidden, ffn_grad = feed_forward(info, x, part, part_sib, gains[1:], dy, full)
    dm, gain_two_grad, dq, dk, dv, grad = attention_back(
        info, dz_part, swap(dz_part), middle, dy, gains[1:], full, q, k, v, o, p,
        o_sib, u_low, sb_own, sb_sib, ffn_grad,
    )
    grad_part = lax.psum_scatter(grad.reshape(6144, 1024), ("z", "x"), scatter_dimension=0, tiled=True)
    keep, send = inputs_back(info, dq, dk, dv, full)
    got = swap(send)
    ds, started = state_turn(keep, got, decay)
    mids = {}

    def before(k, total):
        if k == 2:
            made = state_mid(us, ds, decay, cb, entering, keep, got)
            total, *mids["first"] = lax.optimization_barrier((total,) + tuple(made))
        if k == 3:
            made = state_mid_more(us, ds, decay, cb, entering, mids["first"][0])
            total, *mids["second"] = lax.optimization_barrier((total,) + tuple(made))
        return total

    leaving = carry(started, far, rate, block, lane, True, before)
    _, qu_0, r_0, gain_q = mids["first"]
    dus, qu_1, r_1 = mids["second"]
    qu, rr = (qu_0, qu_1), (r_0, r_1)
    lanes = state_fix(
        info, leaving, decay, cb, ended, ramp, entering, far, qu, rr, gain_q, gains[:1], gain_two_grad
    )
    du_mine, du_give = state_last(info, dus, decay, cb, leaving)

    out_keep, out_send = hidden_out(info, hidden, middle, full)
    out_own = (out_keep + swap(out_send).astype(F32)).astype(BF)

    du_own = ordered(core, du_mine, swap(du_give), 2)
    x_own = x_own.astype(F32)
    grad_own = (norm_back(du_own, x_own, rms_scale(x_own), gains[0]) + dm).astype(BF)

    packed = lanes.reshape(34, 32, 16).transpose(1, 0, 2)
    small_got = lax.all_to_all(packed, CHIPS, split_axis=0, concat_axis=0, tiled=True)
    small_sum = jnp.sum(small_got, axis=0)
    small_sum = small_sum + flip(small_sum, "grp")
    hand = []
    for j in range(32):
        for c in range(2):
            hand.append((j * 2 + c, c * 32 + j))
    mine_sum = lax.ppermute(small_sum, SHARD, hand)

    t_own = state_param.astype(BF).astype(F32).transpose(0, 2, 1)
    rate_o = jnp.exp(t_own[0]) / BLOCK
    decay_o = jnp.exp(-rate_o)
    scale_o = jnp.sqrt(-jnp.expm1(-2.0 * rate_o))
    b_o = scale_o * t_own[1]
    qu_o, rr_o = mine_sum[:NST], mine_sum[NST : 2 * NST]
    gb = t_own[2] * qu_o
    log_rate_grad = rate_o * (
        -decay_o * t_own[2] * b_o * rr_o + decay_o * decay_o / scale_o * t_own[1] * gb
    )
    state_grad = jnp.stack([log_rate_grad, scale_o * gb, b_o * qu_o]).transpose(0, 2, 1)
    gain_grad = mine_sum[2 * NST :]

    mine = [of_lane(v, lane) for v in (out_own, grad_own)]
    give = jnp.stack([of_lane(v, 1 - lane) for v in (out_own, grad_own)])
    grad_part, state_grad, gain_grad, give, *mine = lax.optimization_barrier(
        (grad_part, state_grad, gain_grad, give, *mine)
    )
    traded = flip(give, "x")
    output, token_grad = (halves(a, b) for a, b in zip(mine, traded))
    here, there, give_here, give_there = (grad_part[96 * k : 96 * k + 96] for k in range(4))
    own, give, squares = finish(
        info, here, flip(give_here, "y"), flip(there, "grp"), lax.ppermute(give_there, ("grp", "y"), across),
        state_grad, gain_grad,
    )
    squares, own, got = lax.optimization_barrier((squares + swap(squares), own, swap(give)))
    every = lax.all_to_all(squares, ("grp",) + CHIPS, split_axis=0, concat_axis=0, tiled=True)
    new = update(
        info,
        (attn_weight, up_weight, down_weight, state_param, norm_gain),
        (attn_first, up_first, down_first, state_first, gain_first),
        (attn_second, up_second, down_second, state_second, gain_second),
        (every, own, got, flip(own, "grp"), flip(got, "grp"), state_grad, gain_grad),
    )
    return (output[None], token_grad[None], new[20][0, 0]) + tuple(new[:20])


def solution(mesh):
    inner = Mesh(mesh.devices.reshape(2, 2, 4, 4, 2), AXES)
    rows = P("grp", None, SHARD, None)
    attn = P(None, SHARD, None)
    flat = P(SHARD, None)
    gain = P(None, SHARD)
    in_specs = (rows, rows, P("grp", None), attn, flat, flat, attn, gain)
    in_specs += (attn, attn, flat, flat, flat, flat, attn, attn, gain, gain)
    out_specs = (rows, rows, P()) + (attn,) * 4 + (flat,) * 8 + (attn,) * 4 + (gain,) * 4
    return jax.shard_map(body, mesh=inner, in_specs=in_specs, out_specs=out_specs, check_vma=False)
```

```python
import jax
import jax.numpy as jnp
from jax import lax
from jax.experimental import pallas as pl
from jax.experimental.pallas import tpu as pltpu
from jax.sharding import Mesh
from jax.sharding import PartitionSpec as P

HEAD_DIM = 128
BLOCK = 512
STEP = 5
SLOT = 2048

EPS_NORM = 1e-05
BETA_ONE = 0.5
BETA_TWO = 0.5
ADAM_EPS = 1e-08
WEIGHT_DECAY = 0.1
CLIP_NORM = 0.5
RATE_MATRIX = 0.02
RATE_STATE = 1.0
RATE_GAIN = 0.6
MASKED = -1e30

AXES = ("grp", "y", "z", "x", "core")
CHIPS = ("y", "z", "x")
SHARD = ("y", "z", "x", "core")
BF = jnp.bfloat16
F32 = jnp.float32
NST = 16
ROWS = 256
HALF = 512


def flip(v, axis, kind="a"):
    if lax.axis_size(axis) == 2:
        pairs = [(0, 1), (1, 0)]
    elif kind == "c":
        pairs = [(0, 2), (2, 0), (1, 3), (3, 1)]
    elif kind == "a":
        pairs = [(0, 1), (1, 0), (2, 3), (3, 2)]
    else:
        pairs = [(0, 3), (3, 0), (1, 2), (2, 1)]
    return lax.ppermute(v, axis, pairs)


def swap(v):
    return flip(v, "core")


def ordered(bit, own, other, axis):
    first = jnp.where(bit == 0, own, other)
    second = jnp.where(bit == 0, other, own)
    return jnp.concatenate([first, second], axis=axis)


def rms_scale(value):
    return lax.rsqrt(jnp.mean(value * value, axis=-1, keepdims=True) + EPS_NORM)


def norm_back(grad, value, inverse, gain):
    unit = value * inverse
    scaled = grad * gain
    return inverse * (scaled - unit * jnp.mean(scaled * unit, axis=-1, keepdims=True))


def dot(left, right):
    return jnp.dot(left, right, preferred_element_type=F32)


def dot_nt(left, right):
    return lax.dot_general(left, right, (((1,), (1,)), ((), ())), preferred_element_type=F32)


def dot_tn(left, right):
    return lax.dot_general(left, right, (((0,), (0,)), ((), ())), preferred_element_type=F32)


def params(mib=16):
    return pltpu.CompilerParams(vmem_limit_bytes=mib * 1024 * 1024)


BIG = 53


def cost(flops, bytes_accessed):
    return pl.CostEstimate(flops=flops, bytes_accessed=bytes_accessed, transcendentals=0)


def sds(shape, dtype):
    return jax.ShapeDtypeStruct(shape, dtype)


SMEM = pl.BlockSpec(memory_space=pltpu.SMEM)
FULL = pl.BlockSpec(memory_space=pltpu.VMEM)


def live_of(info, half):
    return (lax.broadcasted_iota(jnp.int32, (ROWS, 1), 0) + half * ROWS < info[1]).astype(F32)


def at(ref, t):
    return ref[pl.ds(t, 8, stride=ROWS), :]


def tree(terms):
    while len(terms) > 1:
        terms = [terms[i] + terms[i + 1] for i in range(0, len(terms), 2)]
    return terms[0]


def first_kernel(info, x_ref, gain_ref, a_ref, low_ref, us_ref, e_ref, f_ref):
    for lane in range(2):
        x = x_ref[lane].astype(F32)
        unit = x * rms_scale(x)
        low_ref[lane] = (unit * gain_ref[...]).astype(BF)
        half = jnp.where(info[0] == 0, unit[:, :HALF], unit[:, HALF:])
        for g in range(4):
            us_ref[pl.ds((lane * 4 + g) * ROWS, ROWS), :] = half[:, g * 128 : (g + 1) * 128]
    half = NST // 2
    for base in (0, half):
        a = [a_ref[base + n] for n in range(half)]

        def step(t, held):
            e, f = held
            u = at(us_ref, t)
            f = tuple(a[n] * (f[n] + e[n]) for n in range(half))
            e = tuple(a[n] * e[n] + u for n in range(half))
            return e, f

        zero = tuple(jnp.zeros((8, 128), F32) for _ in range(half))
        e, f = lax.fori_loop(0, ROWS, step, (zero, zero), unroll=4)
        for n in range(half):
            e_ref[base + n] = e[n]
            f_ref[base + n] = f[n]


STATE = sds((NST, 8, 128), F32)
SPREAD = sds((9 * ROWS, 128), F32)


def first(info, x, gain, a):
    return pl.pallas_call(
        first_kernel,
        out_shape=(sds((2, ROWS, 1024), BF), SPREAD, STATE, STATE),
        in_specs=[SMEM, FULL, FULL, FULL],
        compiler_params=params(),
        cost_estimate=cost(32_000_000, 3_000_000),
        name="first",
    )(info, x, gain, a)


def run_kernel(us, a_ref, cb_ref, h_ref, s_ref, ss):
    def step(t, h):
        u = at(us, t)
        h = tuple(a_ref[n] * h[n] + u for n in range(NST))
        ss[pl.ds(t, 8, stride=ROWS), :] = tree([cb_ref[n] * h[n] for n in range(NST)])
        return h

    lax.fori_loop(0, ROWS, step, tuple(h_ref[n] for n in range(NST)), unroll=4)
    for lane in range(2):
        for g in range(4):
            s_ref[lane, :, g * 128 : (g + 1) * 128] = ss[pl.ds((lane * 4 + g) * ROWS, ROWS), :].astype(BF)


def state_run(us, a, cb, h):
    return pl.pallas_call(
        run_kernel,
        out_shape=sds((2, ROWS, HALF), BF),
        scratch_shapes=[pltpu.VMEM((9 * ROWS, 128), F32)],
        compiler_params=params(),
        cost_estimate=cost(32_000_000, 2_000_000),
        name="state_run",
    )(us, a, cb, h)


def turn_kernel(keep_ref, got_ref, a_ref, ds_ref, e_ref):
    for half in range(2):
        d = added(keep_ref[0, half], got_ref[0, half])
        for g in range(4):
            ds_ref[pl.ds((half * 4 + g) * ROWS, ROWS), :] = d[:, g * 128 : (g + 1) * 128]
    a = [a_ref[n] for n in range(NST)]

    def step(i, h):
        d = at(ds_ref, ROWS - 1 - i)
        return tuple(a[n] * h[n] + d for n in range(NST))

    h = lax.fori_loop(0, ROWS, step, tuple(jnp.zeros((8, 128), F32) for _ in range(NST)), unroll=4)
    for n in range(NST):
        e_ref[n] = h[n]


def state_turn(keep, got, a):
    return pl.pallas_call(
        turn_kernel,
        out_shape=(SPREAD, STATE),
        compiler_params=params(),
        cost_estimate=cost(16_000_000, 4_000_000),
        name="state_turn",
    )(keep, got, a)


def mid_kernel(base, us, ds, a_ref, cb_ref, h_ref, dus_in, dus, qu_ref, r_ref):
    half = NST // 2
    a = [a_ref[base + n] for n in range(half)]

    def step(i, held):
        q, v, qu, r = held
        t = ROWS - 1 - i
        u, d = at(us, t), at(ds, t)
        v = tuple(a[n] * v[n] + q[n] for n in range(half))
        q = tuple(a[n] * q[n] + d for n in range(half))
        du = tree([cb_ref[base + n] * q[n] for n in range(half)])
        dus[pl.ds(t, 8, stride=ROWS), :] = at(dus_in, t) + du
        qu = tuple(qu[n] + q[n] * u for n in range(half))
        r = tuple(r[n] + v[n] * u for n in range(half))
        return (q, v, qu, r)

    zero = tuple(jnp.zeros((8, 128), F32) for _ in range(half))
    q, v, qu, r = lax.fori_loop(0, ROWS, step, (zero,) * 4, unroll=2)
    for n in range(half):
        qu_ref[n] = qu[n]
        r_ref[n] = r[n] + h_ref[base + n] * (a[n] * v[n] + q[n])


def mid_first_kernel(us, ds, a_ref, cb_ref, h_ref, keep_ref, got_ref, dus, qu_ref, r_ref, g_ref, dq):
    for half in range(2):
        du = added(keep_ref[1, half], got_ref[1, half])
        for g in range(4):
            k = half * 4 + g
            piece = du[:, g * 128 : (g + 1) * 128]
            dq[pl.ds(k * ROWS, ROWS), :] = piece
            g_ref[k : k + 1, :] = jnp.sum(piece * us[pl.ds(k * ROWS, ROWS), :], axis=0, keepdims=True)
    mid_kernel(0, us, ds, a_ref, cb_ref, h_ref, dq, dus, qu_ref, r_ref)


def state_mid(us, ds, a, cb, h, keep, got):
    part = sds((NST // 2, 8, 128), F32)
    return pl.pallas_call(
        mid_first_kernel,
        out_shape=(SPREAD, part, part, sds((8, 128), F32)),
        scratch_shapes=[pltpu.VMEM((9 * ROWS, 128), F32)],
        compiler_params=params(),
        cost_estimate=cost(40_000_000, 4_000_000),
        name="state_mid_0",
    )(us, ds, a, cb, h, keep, got)


def state_mid_more(us, ds, a, cb, h, dus):
    part = sds((NST // 2, 8, 128), F32)
    return pl.pallas_call(
        lambda *refs: mid_kernel(NST // 2, *refs),
        out_shape=(SPREAD, part, part),
        compiler_params=params(),
        cost_estimate=cost(40_000_000, 4_000_000),
        name="state_mid_1",
    )(us, ds, a, cb, h, dus)


def fix_kernel(info, q_ref, a_ref, cb_ref, e_ref, f_ref, h_ref, far_ref, qu_0, qu_1, r_0, r_1, g_ref, gain, gain_two, out):
    half = NST // 2

    def halved(v):
        return jnp.where(info[0] == 0, v[:, :HALF], v[:, HALF:])

    def put(row, v, scale):
        both = v[:4] + v[4:]
        for g in range(4):
            at_c = slice(g * 128, (g + 1) * 128)
            value = both[g : g + 1]
            out[row : row + 1, at_c] = value * scale[:, at_c] if scale is not None else value

    gain_c = halved(gain[...])
    total = g_ref[...]
    for n in range(NST):
        q = q_ref[n]
        qu = (qu_0, qu_1)[n // half][n % half] + q * a_ref[n] * e_ref[n]
        r = (r_0, r_1)[n // half][n % half] + q * (f_ref[n] + h_ref[n] * (float(ROWS) * far_ref[n]))
        total = total + cb_ref[n] * qu
        put(n, qu, gain_c)
        put(NST + n, r, gain_c)
    put(2 * NST, total, None)
    out[2 * NST + 1 :] = halved(gain_two[...])


def state_fix(info, q, a, cb, e, f, h, far, qu, r, g, gain, gain_two):
    return pl.pallas_call(
        fix_kernel,
        out_shape=sds((2 * NST + 2, HALF), F32),
        in_specs=[SMEM] + [FULL] * 14,
        compiler_params=params(),
        cost_estimate=cost(1_000_000, 1_000_000),
        name="state_fix",
    )(info, q, a, cb, e, f, h, far, *qu, *r, g, gain, gain_two)


def last_kernel(info, dus, a_ref, cb_ref, q_ref, mine_ref, give_ref, out):
    def step(i, q):
        t = ROWS - 1 - i
        q = tuple(a_ref[n] * q[n] for n in range(NST))
        out[pl.ds(t, 8, stride=ROWS), :] = at(dus, t) + tree([cb_ref[n] * q[n] for n in range(NST)])
        return q

    lax.fori_loop(0, ROWS, step, tuple(q_ref[n] for n in range(NST)), unroll=4)
    mine = pl.multiple_of(info[0] * 128, 128)
    give = pl.multiple_of((1 - info[0]) * 128, 128)
    for lane in range(2):
        for g in range(4):
            base = (lane * 4 + g) * ROWS
            at_c = slice(g * 128, (g + 1) * 128)
            mine_ref[lane, :, at_c] = out[pl.ds(base + mine, 128), :]
            give_ref[lane, :, at_c] = out[pl.ds(base + give, 128), :]


def state_last(info, dus, a, cb, q):
    half = sds((2, 128, HALF), F32)
    return pl.pallas_call(
        last_kernel,
        out_shape=(half, half),
        in_specs=[SMEM] + [FULL] * 4,
        scratch_shapes=[pltpu.VMEM((9 * ROWS, 128), F32)],
        compiler_params=params(),
        cost_estimate=cost(32_000_000, 2_000_000),
        name="state_last",
    )(info, dus, a, cb, q)


def added(left, right):
    return left.astype(F32) + right.astype(F32)


def wide(v):
    return v.reshape(v.shape[0] * v.shape[1], v.shape[2])


class Weights:
    def __init__(self, info, full_ref, w, sems):
        self.y, self.full, self.w, self.sems = info[3], full_ref, w, sems
        self.copies = {}

    def start(self, order):
        for n in order:
            rows, cols = pl.ds(128 + 32 * (n // 2), 32), pl.ds(HALF * (n % 2), HALF)
            self.copies[n] = [
                pltpu.make_async_copy(self.full.at[:, r, rows, cols], self.w.at[n, r], self.sems.at[n, r])
                for r in range(2)
            ]
            for c in self.copies[n]:
                c.start()

    def wait(self, n):
        for c in self.copies[n]:
            c.wait()

    def half(self, n, half):
        return wide(self.w[n, half ^ self.y])

    def out(self, half):
        return wide(self.w[3, half])


WEIGHTS = [pltpu.VMEM((4, 2, 16, 32, HALF), BF), pltpu.SemaphoreType.DMA((4, 2))]
HBM = pl.BlockSpec(memory_space=pltpu.HBM)


def bring(pairs, sems):
    sems = sems if isinstance(sems, list) else [sems.at[n] for n in range(len(pairs))]
    copies = [pltpu.make_async_copy(src, dst, sem) for (src, dst), sem in zip(pairs, sems)]
    for copy in copies:
        copy.start()
    return copies


INPUTS = [pltpu.VMEM((2, ROWS, 1024), BF)] + [pltpu.VMEM((2 * ROWS, HALF), BF)] * 2 + [pltpu.SemaphoreType.DMA((6,))]


def used(p_ref, half):
    return p_ref.at[half, :, :, pl.ds(0, ROWS * (half + 1))]


def attn_kernel(
    info, u_in, own_in, sib_in, full_ref, part_ref, q_out, k_out, v_out, o_out, p_out,
    q_ref, k_ref, v_ref, o_ref, p_ref, out_sems, w_s, sems, u_ref, own, sib, in_sems,
):
    w = Weights(info, full_ref, w_s, sems)
    w.start((0,))
    arriving = bring(((u_in, u_ref), (own_in, own), (sib_in, sib)), in_sems)
    w.start((1, 2, 3))
    me, it = info[0], 1 - info[0]
    leaving = []

    def leave(src, dst, *place):
        copy = pltpu.make_async_copy(src, dst, out_sems.at[place])
        copy.start()
        leaving.append(copy)

    arriving[0].wait()
    w.wait(0)
    for half in range(2):
        u = u_ref[half]
        q_ref[half] = (dot(u[:, :HALF], w.half(0, 0)) + dot(u[:, HALF:], w.half(0, 1))).astype(BF)
    leave(q_ref, q_out, 0, 0)
    for copy in arriving[1:]:
        copy.wait()
    for n, ref, out in ((1, k_ref, k_out), (2, v_ref, v_out)):
        w.wait(n)
        ref[...] = (dot(own[...], w.half(n, me)) + dot(sib[...], w.half(n, it))).astype(BF)
        leave(ref, out, n, 0)
    w.wait(3)
    for half in range(2):
        seen = ROWS * (half + 1)
        row = lax.broadcasted_iota(jnp.int32, (ROWS, seen), 0) + half * ROWS
        allowed = lax.broadcasted_iota(jnp.int32, (ROWS, seen), 1) <= row
        for h in range(4):
            at_h = slice(h * HEAD_DIM, (h + 1) * HEAD_DIM)
            s = dot_nt(q_ref[half, :, at_h], k_ref[:seen, at_h]) * HEAD_DIM**-0.5
            s = jnp.where(allowed, s, MASKED)
            e = jnp.exp(s - jnp.max(s, axis=-1, keepdims=True))
            p = (e / jnp.sum(e, axis=-1, keepdims=True)).astype(BF)
            p_ref[half, h, :, :seen] = p
            o_ref[half, :, at_h] = dot(p, v_ref[:seen, at_h]).astype(BF)
        leave(used(p_ref, half), used(p_out, half), 3, half)
        leave(o_ref.at[half], o_out.at[half], 4, half)
        o = o_ref[half]
        for side in range(2):
            part_ref[half, :, side * HALF : (side + 1) * HALF] = dot(o, w.out(side)).astype(BF)
    for copy in leaving:
        copy.wait()


KEPT = [
    pltpu.VMEM((2, ROWS, HALF), BF), pltpu.VMEM((2 * ROWS, HALF), BF), pltpu.VMEM((2 * ROWS, HALF), BF),
    pltpu.VMEM((2, ROWS, HALF), BF), pltpu.VMEM((2, 4, ROWS, 2 * ROWS), BF), pltpu.SemaphoreType.DMA((5, 2)),
]


def attention(info, u, own, sib, full):
    return pl.pallas_call(
        attn_kernel,
        out_shape=(
            sds((2, ROWS, 1024), BF), sds((2, ROWS, HALF), BF), sds((2 * ROWS, HALF), BF),
            sds((2 * ROWS, HALF), BF), sds((2, ROWS, HALF), BF), sds((2, 4, ROWS, 2 * ROWS), BF),
        ),
        in_specs=[SMEM] + [HBM] * 4,
        out_specs=(FULL, HBM, HBM, HBM, HBM, HBM),
        scratch_shapes=KEPT + WEIGHTS + INPUTS,
        compiler_params=params(BIG),
        cost_estimate=cost(4_000_000_000, 16_000_000),
        name="attention",
    )(info, u, own, sib, full)


def attn_back_kernel(
    info, own_in, sib_in, mid_in, dy_in, gain_ref, full_ref, q_in, k_in, v_in, o_in, p_in,
    os_in, u_in, so_in, ss_in, held_ref, dm_out, g_ref, dq_out, dk_out, dv_out, grad_ref,
    q_ref, k_ref, v_ref, o_ref, p_ref, in_sems, w_s, sems, grads, out_sems,
    u_ref, s_own, s_sib, late_sems, os_ref, own_ref, sib_ref, mid_ref, dy_ref, dm_ref, first_sems,
    dq_ref, dk_ref, dv_ref, made_sems,
):
    del held_ref
    early = []
    for lane in range(2):
        pairs = ((own_in, own_ref), (sib_in, sib_ref), (mid_in, mid_ref), (dy_in, dy_ref))
        early.append(bring([(a.at[lane], b.at[lane]) for a, b in pairs], first_sems.at[lane]))
    w = Weights(info, full_ref, w_s, sems)
    w.start((3,))
    pairs = ((v_in, v_ref), (k_in, k_ref), (q_in, q_ref), (o_in, o_ref))
    pairs += tuple((used(p_in, half), used(p_ref, half)) for half in range(2))
    arriving = bring(pairs, [in_sems.at[n, 0] for n in range(5)] + [in_sems.at[0, 1]])
    me, it = info[0], 1 - info[0]
    scale = HEAD_DIM**-0.5
    gain_grad = jnp.zeros((1, 1024), F32)
    branches = []
    leaving = []

    def leave(src, dst, sem):
        copy = pltpu.make_async_copy(src, dst, sem)
        copy.start()
        leaving.append(copy)

    for lane in range(2):
        for copy in early[lane]:
            copy.wait()
        if lane == 1:
            late = bring(((u_in, u_ref), (so_in, s_own), (ss_in, s_sib), (os_in, os_ref)), late_sems)
        m = mid_ref[lane]
        dz = added(own_ref[lane], sib_ref[lane])
        inverse = rms_scale(m)
        unit = m * inverse
        gain_grad = gain_grad + jnp.sum(dz * unit, axis=0, keepdims=True)
        scaled = dz * gain_ref[...]
        dm = dy_ref[lane].astype(F32) + inverse * (
            scaled - unit * jnp.mean(scaled * unit, axis=-1, keepdims=True)
        )
        dm_ref[lane] = dm
        own_rows = pl.ds(pl.multiple_of(info[0] * 128, 128), 128)
        leave(dm_ref.at[lane, own_rows], dm_out.at[lane], made_sems.at[0, lane])
        branch = (live_of(info, lane) * dm).astype(BF)
        branches.append(branch)
    g_ref[...] = gain_grad
    w.wait(3)
    for copy in arriving:
        copy.wait()
    d_o = []
    for half in range(2):
        branch = branches[half]
        d_o.append((dot_nt(branch[:, :HALF], w.out(0)) + dot_nt(branch[:, HALF:], w.out(1))).astype(BF))
    for h in range(4):
        at_h = slice(h * HEAD_DIM, (h + 1) * HEAD_DIM)
        dk, dv = [], []
        for half in range(2):
            seen = ROWS * (half + 1)
            p_low = p_ref[half, h, :, :seen]
            p = p_low.astype(F32)
            d_o_h = d_o[half][:, at_h]
            dp = dot_nt(d_o_h, v_ref[:seen, at_h])
            total = jnp.sum(p * dp, axis=-1, keepdims=True)
            ds = (p * (dp - total)).astype(BF)
            dq_ref[half, :, at_h] = (dot(ds, k_ref[:seen, at_h]) * scale).astype(BF)
            dk.append(dot_tn(ds, q_ref[half, :, at_h]))
            dv.append(dot_tn(p_low, d_o_h))
        for ref, parts, factor in ((dk_ref, dk, scale), (dv_ref, dv, 1.0)):
            ref[:ROWS, at_h] = ((parts[0] + parts[1][:ROWS]) * factor).astype(BF)
            ref[ROWS:, at_h] = (parts[1][ROWS:] * factor).astype(BF)
    for n, (src, dst) in enumerate(((dq_ref, dq_out), (dk_ref, dk_out), (dv_ref, dv_out))):
        leave(src, dst, made_sems.at[1 + n, 0])

    def leave_grad(n):
        at_r = pl.ds(pl.multiple_of(info[8 + n // 2], 32), 32)
        at_c = pl.ds(HALF * (n % 2), HALF)
        for y in range(2):
            leave(grads.at[n, y], grad_ref.at[:, y ^ info[3], at_r, at_c], out_sems.at[n, y])

    def put(n, half, value):
        grads[n, pl.ds(half, 1)] = value.astype(BF).reshape(1, 16, 32, HALF)

    for copy in late:
        copy.wait()
    branch = jnp.concatenate(branches, axis=0)
    branch = jnp.where(info[0] == 0, branch[:, :HALF], branch[:, HALF:])
    for half, ref in ((me, o_ref), (it, os_ref)):
        put(3, half, dot_tn(wide(ref[...]), branch))
    leave_grad(3)
    for n, ref in ((1, dk_ref), (2, dv_ref)):
        for half, s_c in ((me, s_own), (it, s_sib)):
            put(n, half, dot_tn(s_c[...], ref[...]))
        leave_grad(n)
    for half in range(2):
        put(0, half, dot_tn(wide(u_ref[...])[:, half * HALF : (half + 1) * HALF], wide(dq_ref[...])))
    leave_grad(0)
    for copy in leaving:
        copy.wait()


def attention_back(info, own, sib, mid, dy, gain, full, q, k, v, o, p, o_sib, u, s_own, s_sib, held):
    return pl.pallas_call(
        attn_back_kernel,
        out_shape=(
            sds((2, 128, 1024), F32), sds((1, 1024), F32), sds((2, ROWS, HALF), BF),
            sds((2 * ROWS, HALF), BF), sds((2 * ROWS, HALF), BF), sds(held.shape, BF),
        ),
        in_specs=[SMEM] + [HBM] * 4 + [FULL] + [HBM] * 11,
        out_specs=(HBM, FULL, HBM, HBM, HBM, HBM),
        input_output_aliases={16: 5},
        scratch_shapes=KEPT + WEIGHTS + WEIGHTS + INPUTS + [
            pltpu.VMEM((2, ROWS, HALF), BF), pltpu.VMEM((2, ROWS, 1024), BF), pltpu.VMEM((2, ROWS, 1024), BF),
            pltpu.VMEM((2, ROWS, 1024), F32), pltpu.VMEM((2, ROWS, 1024), BF), pltpu.VMEM((2, ROWS, 1024), F32),
            pltpu.SemaphoreType.DMA((2, 4)),
            pltpu.VMEM((2, ROWS, HALF), BF), pltpu.VMEM((2 * ROWS, HALF), BF), pltpu.VMEM((2 * ROWS, HALF), BF),
            pltpu.SemaphoreType.DMA((4, 2)),
        ],
        compiler_params=params(BIG),
        cost_estimate=cost(6_000_000_000, 24_000_000),
        name="attention_back",
    )(info, own, sib, mid, dy, gain, full, q, k, v, o, p, o_sib, u, s_own, s_sib, held)


def inputs_back_kernel(
    info, dq_in, dk_in, dv_in, full_ref, keep_ref, send_ref, w_s, sems, dq_ref, dk_ref, dv_ref, in_sems
):
    w = Weights(info, full_ref, w_s, sems)
    w.start((1, 2))
    arriving = bring(((dk_in, dk_ref), (dv_in, dv_ref), (dq_in, dq_ref)), in_sems)
    w.start((0,))
    for copy in arriving:
        copy.wait()
    for n in (1, 2):
        w.wait(n)
    for ref, half in ((send_ref, 1 - info[0]), (keep_ref, info[0])):
        ds = dot_nt(dk_ref[...], w.half(1, half)) + dot_nt(dv_ref[...], w.half(2, half))
        ref[0] = ds.astype(BF).reshape(2, ROWS, HALF)
    w.wait(0)
    for ref, half in ((send_ref, 1 - info[0]), (keep_ref, info[0])):
        ref[1] = dot_nt(wide(dq_ref[...]), w.half(0, half)).astype(BF).reshape(2, ROWS, HALF)


def inputs_back(info, dq, dk, dv, full):
    return pl.pallas_call(
        inputs_back_kernel,
        out_shape=(sds((2, 2, ROWS, HALF), BF), sds((2, 2, ROWS, HALF), BF)),
        in_specs=[SMEM] + [HBM] * 4,
        scratch_shapes=WEIGHTS + [
            pltpu.VMEM((2, ROWS, HALF), BF), pltpu.VMEM((2 * ROWS, HALF), BF), pltpu.VMEM((2 * ROWS, HALF), BF),
            pltpu.SemaphoreType.DMA((3,)),
        ],
        compiler_params=params(BIG),
        cost_estimate=cost(2_000_000_000, 7_000_000),
        name="inputs_back",
    )(info, dq, dk, dv, full)


GELU_C = 0.7978845608028654
GELU_K = 0.044715


def ffn_kernel(
    info, x_ref, part_ref, sib_ref, gain_ref, dy_ref, up_ref, down_ref,
    mid_out, dz_ref, hidden_ref, grad_ref, z_s, d_s, dz_s, gu_s, gd_s, sems, mid_ref, mid_sems,
):
    step = pl.program_id(0)

    def mid_copy(k):
        return pltpu.make_async_copy(mid_ref.at[k], mid_out.at[k], mid_sems.at[k])

    slot = step % 2
    place, near = step % 2, step // 2
    side = near ^ info[3]

    def copies(slot, place, near):
        at_c = pl.ds(pl.multiple_of(place * HALF, HALF), HALF)
        at_r = pl.ds(pl.multiple_of(info[5 + (near ^ info[3])], 32), 32)
        at_z = pl.ds(place * 8, 8)
        made = [pltpu.make_async_copy(gu_s.at[slot], grad_ref.at[:, :, at_r, at_c], sems.at[0, slot])]
        for k in range(2):
            at_r = pl.ds(pl.multiple_of(info[7 + 3 * k], 32), 32)
            src = gd_s.at[slot, :, pl.ds(32 * k, 32), :]
            made.append(pltpu.make_async_copy(src, grad_ref.at[at_z, near, at_r, :], sems.at[1 + k, slot]))
        return made

    @pl.when(step == 0)
    def _():
        for lane in range(2):
            live = live_of(info, lane)
            m = x_ref[lane].astype(F32) + live * added(part_ref[lane], sib_ref[lane])
            mid_ref[lane] = m
            mid_copy(lane).start()
            z_s[lane * ROWS : (lane + 1) * ROWS] = (m * rms_scale(m) * gain_ref[...]).astype(BF)
            d_s[lane * ROWS : (lane + 1) * ROWS] = (live * dy_ref[lane].astype(F32)).astype(BF)
        dz_s[...] = jnp.zeros_like(dz_s)

    z, d = z_s[...], d_s[...]
    down = wide(down_ref[:, 0])
    up_0, up_1 = (up_ref[:, pl.ds(y ^ info[3], 1)].reshape(HALF, HALF) for y in range(2))
    f = dot(z[:, :HALF], up_0) + dot(z[:, HALF:], up_1)
    square = f * f
    h = 0.5 + 0.5 * jnp.tanh(GELU_C * f + (GELU_C * GELU_K) * f * square)
    hidden = (f * h).astype(BF)
    slope = h + (h - h * h) * (2.0 * GELU_C * f + (6.0 * GELU_C * GELU_K) * f * square)
    hidden_ref[...] = hidden
    back = (slope * dot_nt(d, down)).astype(BF)

    @pl.when(step >= 2)
    def _():
        for c in copies(slot, place, near):
            c.wait()

    gd_s[slot] = dot_tn(hidden, d).astype(BF).reshape(8, 64, 1024)
    gu = dot_tn(z, back).astype(BF).reshape(2, 16, 32, HALF)
    for y in range(2):
        gu_s[slot, :, pl.ds(y ^ info[3], 1)] = gu[y].reshape(16, 1, 32, HALF)
    for c in copies(slot, place, near):
        c.start()
    dz_s[:, :HALF] += dot_nt(back, up_0)
    dz_s[:, HALF:] += dot_nt(back, up_1)

    @pl.when(step == pl.num_programs(0) - 1)
    def _():
        for lane in range(2):
            dz_ref[lane] = dz_s[lane * ROWS : (lane + 1) * ROWS].astype(BF)
            mid_copy(lane).wait()
        for k in range(2):
            for c in copies(k, place, near):
                c.wait()


def feed_forward(info, x, part, sib, gain, dy, weights):
    chunk = pl.BlockSpec((2 * ROWS, HALF), lambda i, info: (0, i))
    return pl.pallas_call(
        ffn_kernel,
        grid_spec=pltpu.PrefetchScalarGridSpec(
            num_scalar_prefetch=1,
            grid=(4,),
            in_specs=[
                FULL, FULL, FULL, FULL, FULL,
                pl.BlockSpec((16, 2, 32, HALF), lambda i, info: (0, 0, (i // 2) ^ info[3], i % 2)),
                pl.BlockSpec((8, 1, 64, 1024), lambda i, info: (i % 2, i // 2, 1, 0)),
            ],
            out_specs=(HBM, FULL, chunk, HBM),
            scratch_shapes=[
                pltpu.VMEM((2 * ROWS, 1024), BF), pltpu.VMEM((2 * ROWS, 1024), BF), pltpu.VMEM((2 * ROWS, 1024), F32),
                pltpu.VMEM((2, 16, 2, 32, HALF), BF), pltpu.VMEM((2, 8, 64, 1024), BF),
                pltpu.SemaphoreType.DMA((3, 2)),
                pltpu.VMEM((2, ROWS, 1024), F32), pltpu.SemaphoreType.DMA((2,)),
            ],
        ),
        out_shape=(
            sds((2, ROWS, 1024), F32), sds((2, ROWS, 1024), BF), sds((2 * ROWS, 2048), BF),
            sds((16, 2, 192, 1024), BF),
        ),
        compiler_params=params(BIG),
        cost_estimate=cost(9_000_000_000, 28_000_000),
        name="feed_forward",
    )(info, x, part, sib, gain, dy, weights, weights)


DOWN = pl.BlockSpec((8, 1, 64, 1024), lambda i: (i % 2, i // 2, 1, 0))
CHUNK = pl.BlockSpec((2 * ROWS, HALF), lambda i: (0, i))


def hidden_out_kernel(info, hidden_ref, mid_ref, down_ref, keep_ref, send_ref, out_s):
    step = pl.program_id(0)
    more = dot(hidden_ref[...], wide(down_ref[:, 0]))

    @pl.when(step == 0)
    def _():
        out_s[...] = more

    @pl.when(step > 0)
    def _():
        out_s[...] += more

    @pl.when(step == pl.num_programs(0) - 1)
    def _():
        for half in range(2):
            out = live_of(info, half) * out_s[half * ROWS : (half + 1) * ROWS]
            total = out + mid_ref[half]
            keep_ref[half] = jnp.where(info[0] == 0, total[:128], total[128:])
            send_ref[half] = jnp.where(info[0] == 0, out[128:], out[:128]).astype(BF)


def hidden_out(info, hidden, mid, weights):
    return pl.pallas_call(
        hidden_out_kernel,
        grid=(4,),
        out_shape=(sds((2, 128, 1024), F32), sds((2, 128, 1024), BF)),
        in_specs=[SMEM, CHUNK, FULL, DOWN],
        out_specs=(FULL, FULL),
        scratch_shapes=[pltpu.VMEM((2 * ROWS, 1024), F32)],
        compiler_params=params(BIG),
        cost_estimate=cost(2_100_000_000, 8_000_000),
        name="hidden_out",
    )(info, hidden, mid, weights)


STEPS = (("x", "c"), ("z", "a"), ("z", "b"), ("y", "a"))


def carry(ends, far, rate, block, lane, reverse, between=None):
    low, high = ends[:, :4], ends[:, 4:]
    far, rate = far[:, :4], rate[:, :4]
    first, second = (high, low) if reverse else (low, high)
    total = far * first + second
    entering = jnp.zeros_like(total)
    for k, (axis, kind) in enumerate(STEPS):
        if between is not None:
            total = between(k, total)
        other = flip(total, axis, kind)
        upper = (block >> k) & 1
        within = block & ((1 << k) - 1)
        if reverse:
            takes, gap = upper == 0, (1 << k) - 1 - within
        else:
            takes, gap = upper == 1, within
        reach = jnp.exp(-rate * (BLOCK * gap).astype(F32)) * other
        whole = jnp.exp(-rate * float(BLOCK << k))
        joined = whole * jnp.where(takes, other, total) + jnp.where(takes, total, other)
        if k >= 2:
            reach = jnp.where(lane == 1, 0.0, reach)
            joined = jnp.where(lane == 1, 0.0, joined)
        entering = entering + jnp.where(takes, reach, 0.0)
        total = joined
    inner = first + far * entering
    return jnp.concatenate([inner, entering] if reverse else [entering, inner], axis=1)


def adam(factor, w_ref, f_ref, s_ref, grad, outs, rate, decay):
    clipped = grad * factor
    first_new = BETA_ONE * f_ref[...] + (1.0 - BETA_ONE) * clipped
    second_new = BETA_TWO * s_ref[...] + (1.0 - BETA_TWO) * clipped * clipped
    fix_one = 1.0 - BETA_ONE**STEP
    fix_two = 1.0 - BETA_TWO**STEP
    direction = first_new / fix_one / (jnp.sqrt(second_new / fix_two) + ADAM_EPS)
    weight = w_ref[...]
    weight_new = weight - rate * (direction + decay * weight)
    for ref, v in zip(outs, (first_new, second_new, weight_new, weight_new.astype(BF))):
        ref[...] = v


def finish_kernel(info, mine, near, over, cross, state, gain, own_ref, give_ref, squares_ref):
    total = added(mine[...], near[...]) + added(over[...], cross[...])
    squares = jnp.sum(total * total, axis=0, keepdims=True)
    squares = jnp.sum(squares.reshape(1, 8, 128), axis=1)
    squares = jnp.sum(squares, axis=1, keepdims=True)
    for ref in (state, gain):
        piece = ref[...].reshape(-1, 16)
        piece = jnp.sum(piece * piece, axis=0, keepdims=True)
        squares = squares + 0.5 * jnp.sum(piece, axis=1, keepdims=True)
    squares_ref[...] = jnp.broadcast_to(squares, (64, 128))
    own_ref[32:] = total[64:]
    for k in range(2):
        low, high = total[32 * k : 32 * k + 16], total[32 * k + 16 : 32 * k + 32]
        own_ref[16 * k : 16 * k + 16] = jnp.where(info[0] == 0, low, high)
        give_ref[16 * k : 16 * k + 16] = jnp.where(info[0] == 0, high, low)


def finish(info, mine, near, over, cross, state, gain):
    return pl.pallas_call(
        finish_kernel,
        out_shape=(sds((64, 1024), F32), sds((32, 1024), F32), sds((64, 128), F32)),
        in_specs=[SMEM] + [FULL] * 6,
        compiler_params=params(),
        cost_estimate=cost(2_000_000, 3_000_000),
        name="finish",
    )(info, mine, near, over, cross, state, gain)


def update_kernel(info, *refs):
    ins, outs = refs[:22], refs[22:]
    weights, firsts, seconds = ins[:5], ins[5:10], ins[10:15]
    every, mine, got, mine_far, got_far, state, gain = ins[15:]
    norm = jnp.sqrt(jnp.sum(every[...], axis=0, keepdims=True)[:, :1])
    outs[20][...] = norm
    factor = jnp.minimum(1.0, CLIP_NORM / norm)
    zero = info[0] == 0
    here = info[11] == 0

    def pair(one, two):
        first, second = jnp.where(zero, one, two), jnp.where(zero, two, one)
        return first.reshape(2, 16, 1024), second.reshape(2, 16, 1024)

    down = jnp.concatenate(
        [jnp.where(here, mine[32:], mine_far[32:]), jnp.where(here, mine_far[32:], mine[32:])], axis=0
    )
    near, far = pair(mine[:32], got[...]), pair(mine_far[:32], got_far[...])
    first, second = (jnp.where(here, b, a) for a, b in zip(near, far))
    matrices = []
    for n in range(4):
        at_c = slice(HALF * (n % 2), HALF * (n % 2) + HALF)
        matrices.append(jnp.concatenate([first[n // 2, :, at_c], second[n // 2, :, at_c]], axis=1))
    attn_grad = jnp.stack(matrices)
    first, second = (jnp.where(here, a, b) for a, b in zip(near, far))
    pieces = []
    for side in range(2):
        for k in range(16):
            at_c = slice(64 * k, 64 * k + 64)
            pieces += [first[side, :, at_c], second[side, :, at_c]]
    up_grad = jnp.concatenate(pieces, axis=1)
    grads = (attn_grad, up_grad, down, state[...], gain[...])
    rates = ((RATE_MATRIX, WEIGHT_DECAY),) * 3 + ((RATE_STATE, 0.0), (RATE_GAIN, 0.0))
    for k in range(5):
        adam(factor, weights[k], firsts[k], seconds[k], grads[k], outs[4 * k : 4 * k + 4], *rates[k])


def update(info, weights, firsts, seconds, grads):
    shapes = []
    for w in weights:
        shapes += [sds(w.shape, F32)] * 3 + [sds(w.shape, BF)]
    return pl.pallas_call(
        update_kernel,
        out_shape=tuple(shapes) + (sds((1, 1), F32),),
        in_specs=[SMEM] + [FULL] * 22,
        compiler_params=pltpu.CompilerParams(vmem_limit_bytes=24 * 1024 * 1024),
        cost_estimate=cost(4_000_000, 6_000_000),
        name="update",
    )(info, *weights, *firsts, *seconds, *grads)


def body(
    tokens, cotangent, lengths, attn_weight, up_weight, down_weight, state_param, norm_gain,
    attn_first, attn_second, up_first, up_second, down_first, down_second,
    state_first, state_second, gain_first, gain_second,
):
    core = lax.axis_index("core")
    ybit = lax.axis_index("y")
    chip = (ybit * 4 + lax.axis_index("z")) * 4 + lax.axis_index("x")

    lane = chip % 2
    block = chip // 2

    def of_lane(v, which):
        return lax.dynamic_index_in_dim(v, which, 0, keepdims=False)

    def halves(mine, got):
        return jnp.stack([jnp.where(lane == 0, mine, got), jnp.where(lane == 0, got, mine)])

    x_give, dy_give = of_lane(tokens[0], 1 - lane), of_lane(cotangent[0], 1 - lane)
    x_got, dy_got = flip(x_give, "x"), flip(dy_give, "x")

    mine = jnp.concatenate(
        [state_param.astype(BF).transpose(0, 2, 1).reshape(-1), norm_gain.astype(BF).reshape(-1)]
    )
    mine = jnp.pad(mine, (0, 1024 - mine.shape[0])).reshape(1, 8, 128)
    pair = ordered(core, mine, swap(mine), 0)
    small = lax.all_to_all(
        jnp.broadcast_to(pair[None], (32, 2, 8, 128)), CHIPS, split_axis=0, concat_axis=0, tiled=True
    ).reshape(64, 1024)
    theta = small[:, :768].reshape(64, 3, NST, 16).transpose(1, 2, 0, 3).reshape(3, NST, 1024).astype(F32)
    gains = small[:, 768:800].reshape(64, 2, 16).transpose(1, 0, 2).reshape(2, 1024).astype(F32)

    slot_blocks = SLOT // BLOCK
    live_len = lax.dynamic_index_in_dim(lengths[0], block // slot_blocks, 0, keepdims=False)
    live_rows = jnp.clip(live_len - (block % slot_blocks) * BLOCK, 0, BLOCK)
    live_rows = jnp.where(lane == 0, BLOCK, live_rows)
    group = lax.axis_index("grp")
    places = [((b + 3 * group) % 6) * 32 for b in range(6)]
    info = jnp.stack([core, live_rows, lane, ybit, chip] + places + [group]).astype(jnp.int32)

    attn_low = attn_weight.astype(BF)
    up_low = up_weight.astype(BF).reshape(16, 32, 2, 64).transpose(2, 0, 1, 3).reshape(2, 16, 2048)
    down_low = down_weight.astype(BF)
    qkv_keep = lax.dynamic_slice_in_dim(attn_low[:3], core * HALF, HALF, 2)
    qkv_give = lax.dynamic_slice_in_dim(attn_low[:3], (1 - core) * HALF, HALF, 2)
    qkv_chip = ordered(core, qkv_keep, swap(qkv_give), 1)
    out_chip = ordered(core, attn_low[3], swap(attn_low[3]), 0)
    up_keep = lax.dynamic_index_in_dim(up_low, core, 0, keepdims=False)
    up_give = lax.dynamic_index_in_dim(up_low, 1 - core, 0, keepdims=False)
    up_chip = ordered(core, up_keep, swap(up_give), 0)
    up_chip = up_chip.reshape(32, 2, 1024).transpose(1, 0, 2).reshape(64, 1024)
    qk_rows = jnp.concatenate([qkv_chip[0], qkv_chip[1]], axis=1)
    own_rows = jnp.concatenate([up_chip, down_low, qk_rows], axis=0)
    across = [(0, 3), (3, 0), (1, 2), (2, 1)]
    low = jnp.concatenate([own_rows[:96], out_chip[:, :HALF].reshape(16, 1024)], axis=0)
    high = jnp.concatenate([own_rows[96:], jnp.concatenate([qkv_chip[2], out_chip[:, HALF:]], axis=1)], axis=0)
    low, high, pair = lax.optimization_barrier((low, high, pair))
    low_got, high_got = flip(low, "y"), lax.ppermute(high, ("grp", "y"), across)
    out_got = jnp.concatenate([low_got[96:].reshape(32, HALF), high_got[64:, HALF:]], axis=1)
    out_rows = jnp.where(ybit == core, out_chip, out_got)
    own_last = jnp.concatenate([qkv_chip[2], out_rows[:, :HALF]], axis=1)
    other_last = jnp.concatenate([high_got[64:, :HALF], out_rows[:, HALF:]], axis=1)
    all_two = jnp.concatenate([own_rows, own_last, low_got[:96], high_got[:64], other_last], axis=0)
    all_two, x_got, dy_got = lax.optimization_barrier((all_two, x_got, dy_got))
    full = lax.all_gather(all_two.reshape(2, 192, 1024), ("z", "x"), axis=0)
    x_own, dy_own = (halves(of_lane(v[0], lane), got) for v, got in ((tokens, x_got), (cotangent, dy_got)))
    x = ordered(core, x_own, swap(x_own), 1)
    dy = ordered(core, dy_own, swap(dy_own), 1)

    theta_c = lax.dynamic_slice_in_dim(theta, core * HALF, HALF, 2).reshape(3, NST, 4, 128)
    theta_c = jnp.concatenate([theta_c, theta_c], axis=2)
    rate = jnp.exp(theta_c[0]) / BLOCK
    decay = jnp.exp(-rate)
    norm_scale = jnp.sqrt(-jnp.expm1(-2.0 * rate))
    cb = norm_scale * theta_c[1] * theta_c[2]
    far = jnp.exp(-rate * float(ROWS))
    gain_c = lax.dynamic_slice_in_dim(gains[0], core * HALF, HALF, 0).reshape(4, 128)
    gain_c = jnp.concatenate([gain_c, gain_c], axis=0)

    u_low, us, ended, ramp = first(info, x, gains[:1], decay)
    entering = carry(ended, far, rate, block, lane, False)
    entering, dy = lax.optimization_barrier((entering, dy))
    sb_own = state_run(us, decay, cb * gain_c, entering).reshape(2 * ROWS, HALF)
    sb_sib = swap(sb_own)

    part, q, k, v, o, p = attention(info, u_low, sb_own, sb_sib, full)
    part_sib, o_sib = lax.optimization_barrier((swap(part), swap(o)))
    middle, dz_part, hidden, ffn_grad = feed_forward(info, x, part, part_sib, gains[1:], dy, full)
    dm, gain_two_grad, dq, dk, dv, grad = attention_back(
        info, dz_part, swap(dz_part), middle, dy, gains[1:], full, q, k, v, o, p,
        o_sib, u_low, sb_own, sb_sib, ffn_grad,
    )
    grad_part = lax.psum_scatter(grad.reshape(6144, 1024), ("z", "x"), scatter_dimension=0, tiled=True)
    keep, send = inputs_back(info, dq, dk, dv, full)
    got = swap(send)
    ds, started = state_turn(keep, got, decay)
    mids = {}

    def before(k, total):
        if k == 2:
            made = state_mid(us, ds, decay, cb, entering, keep, got)
            total, *mids["first"] = lax.optimization_barrier((total,) + tuple(made))
        if k == 3:
            made = state_mid_more(us, ds, decay, cb, entering, mids["first"][0])
            total, *mids["second"] = lax.optimization_barrier((total,) + tuple(made))
        return total

    leaving = carry(started, far, rate, block, lane, True, before)
    _, qu_0, r_0, gain_q = mids["first"]
    dus, qu_1, r_1 = mids["second"]
    qu, rr = (qu_0, qu_1), (r_0, r_1)
    lanes = state_fix(
        info, leaving, decay, cb, ended, ramp, entering, far, qu, rr, gain_q, gains[:1], gain_two_grad
    )
    du_mine, du_give = state_last(info, dus, decay, cb, leaving)

    out_keep, out_send = hidden_out(info, hidden, middle, full)
    out_own = (out_keep + swap(out_send).astype(F32)).astype(BF)

    du_own = ordered(core, du_mine, swap(du_give), 2)
    x_own = x_own.astype(F32)
    grad_own = (norm_back(du_own, x_own, rms_scale(x_own), gains[0]) + dm).astype(BF)

    packed = lanes.reshape(34, 32, 16).transpose(1, 0, 2)
    small_got = lax.all_to_all(packed, CHIPS, split_axis=0, concat_axis=0, tiled=True)
    small_sum = jnp.sum(small_got, axis=0)
    small_sum = small_sum + flip(small_sum, "grp")
    hand = []
    for j in range(32):
        for c in range(2):
            hand.append((j * 2 + c, c * 32 + j))
    mine_sum = lax.ppermute(small_sum, SHARD, hand)

    t_own = state_param.astype(BF).astype(F32).transpose(0, 2, 1)
    rate_o = jnp.exp(t_own[0]) / BLOCK
    decay_o = jnp.exp(-rate_o)
    scale_o = jnp.sqrt(-jnp.expm1(-2.0 * rate_o))
    b_o = scale_o * t_own[1]
    qu_o, rr_o = mine_sum[:NST], mine_sum[NST : 2 * NST]
    gb = t_own[2] * qu_o
    log_rate_grad = rate_o * (
        -decay_o * t_own[2] * b_o * rr_o + decay_o * decay_o / scale_o * t_own[1] * gb
    )
    state_grad = jnp.stack([log_rate_grad, scale_o * gb, b_o * qu_o]).transpose(0, 2, 1)
    gain_grad = mine_sum[2 * NST :]

    mine = [of_lane(v, lane) for v in (out_own, grad_own)]
    give = jnp.stack([of_lane(v, 1 - lane) for v in (out_own, grad_own)])
    grad_part, state_grad, gain_grad, give, *mine = lax.optimization_barrier(
        (grad_part, state_grad, gain_grad, give, *mine)
    )
    traded = flip(give, "x")
    output, token_grad = (halves(a, b) for a, b in zip(mine, traded))
    here, there, give_here, give_there = (grad_part[96 * k : 96 * k + 96] for k in range(4))
    own, give, squares = finish(
        info, here, flip(give_here, "y"), flip(there, "grp"), lax.ppermute(give_there, ("grp", "y"), across),
        state_grad, gain_grad,
    )
    squares, own, got = lax.optimization_barrier((squares + swap(squares), own, swap(give)))
    every = lax.all_to_all(squares, ("grp",) + CHIPS, split_axis=0, concat_axis=0, tiled=True)
    new = update(
        info,
        (attn_weight, up_weight, down_weight, state_param, norm_gain),
        (attn_first, up_first, down_first, state_first, gain_first),
        (attn_second, up_second, down_second, state_second, gain_second),
        (every, own, got, flip(own, "grp"), flip(got, "grp"), state_grad, gain_grad),
    )
    return (output[None], token_grad[None], new[20][0, 0]) + tuple(new[:20])


def solution(mesh):
    inner = Mesh(mesh.devices.reshape(2, 2, 4, 4, 2), AXES)
    rows = P("grp", None, SHARD, None)
    attn = P(None, SHARD, None)
    flat = P(SHARD, None)
    gain = P(None, SHARD)
    in_specs = (rows, rows, P("grp", None), attn, flat, flat, attn, gain)
    in_specs += (attn, attn, flat, flat, flat, flat, attn, attn, gain, gain)
    out_specs = (rows, rows, P()) + (attn,) * 4 + (flat,) * 8 + (attn,) * 4 + (gain,) * 4
    return jax.shard_map(body, mesh=inner, in_specs=in_specs, out_specs=out_specs, check_vma=False)
```

```python
import jax
import jax.numpy as jnp
from jax import lax
from jax.experimental import pallas as pl
from jax.experimental.pallas import tpu as pltpu
from jax.sharding import Mesh
from jax.sharding import PartitionSpec as P

HEAD_DIM = 128
BLOCK = 512
STEP = 5
SLOT = 2048

EPS_NORM = 1e-05
BETA_ONE = 0.5
BETA_TWO = 0.5
ADAM_EPS = 1e-08
WEIGHT_DECAY = 0.1
CLIP_NORM = 0.5
RATE_MATRIX = 0.02
RATE_STATE = 1.0
RATE_GAIN = 0.6
MASKED = -1e30

AXES = ("grp", "y", "z", "x", "core")
CHIPS = ("y", "z", "x")
SHARD = ("y", "z", "x", "core")
BF = jnp.bfloat16
F32 = jnp.float32
NST = 16
ROWS = 256
HALF = 512


def flip(v, axis, kind="a"):
    if lax.axis_size(axis) == 2:
        pairs = [(0, 1), (1, 0)]
    elif kind == "c":
        pairs = [(0, 2), (2, 0), (1, 3), (3, 1)]
    elif kind == "a":
        pairs = [(0, 1), (1, 0), (2, 3), (3, 2)]
    else:
        pairs = [(0, 3), (3, 0), (1, 2), (2, 1)]
    return lax.ppermute(v, axis, pairs)


def swap(v):
    return flip(v, "core")


def ordered(bit, own, other, axis):
    first = jnp.where(bit == 0, own, other)
    second = jnp.where(bit == 0, other, own)
    return jnp.concatenate([first, second], axis=axis)


def rms_scale(value):
    return lax.rsqrt(jnp.mean(value * value, axis=-1, keepdims=True) + EPS_NORM)


def norm_back(grad, value, inverse, gain):
    unit = value * inverse
    scaled = grad * gain
    return inverse * (scaled - unit * jnp.mean(scaled * unit, axis=-1, keepdims=True))


def dot(left, right):
    return jnp.dot(left, right, preferred_element_type=F32)


def dot_nt(left, right):
    return lax.dot_general(left, right, (((1,), (1,)), ((), ())), preferred_element_type=F32)


def dot_tn(left, right):
    return lax.dot_general(left, right, (((0,), (0,)), ((), ())), preferred_element_type=F32)


def params(mib=16):
    return pltpu.CompilerParams(vmem_limit_bytes=mib * 1024 * 1024)


BIG = 53


def cost(flops, bytes_accessed):
    return pl.CostEstimate(flops=flops, bytes_accessed=bytes_accessed, transcendentals=0)


def sds(shape, dtype):
    return jax.ShapeDtypeStruct(shape, dtype)


SMEM = pl.BlockSpec(memory_space=pltpu.SMEM)
FULL = pl.BlockSpec(memory_space=pltpu.VMEM)


def live_of(info, half):
    return (lax.broadcasted_iota(jnp.int32, (ROWS, 1), 0) + half * ROWS < info[1]).astype(F32)


def at(ref, t):
    return ref[pl.ds(t, 8, stride=ROWS), :]


def tree(terms):
    while len(terms) > 1:
        terms = [terms[i] + terms[i + 1] for i in range(0, len(terms), 2)]
    return terms[0]


def first_kernel(info, x_ref, gain_ref, a_ref, low_ref, us_ref, e_ref, f_ref):
    for lane in range(2):
        x = x_ref[lane].astype(F32)
        unit = x * rms_scale(x)
        low_ref[lane] = (unit * gain_ref[...]).astype(BF)
        half = jnp.where(info[0] == 0, unit[:, :HALF], unit[:, HALF:])
        for g in range(4):
            us_ref[pl.ds((lane * 4 + g) * ROWS, ROWS), :] = half[:, g * 128 : (g + 1) * 128]
    half = NST // 2
    for base in (0, half):
        a = [a_ref[base + n] for n in range(half)]

        def step(t, held):
            e, f = held
            u = at(us_ref, t)
            f = tuple(a[n] * (f[n] + e[n]) for n in range(half))
            e = tuple(a[n] * e[n] + u for n in range(half))
            return e, f

        zero = tuple(jnp.zeros((8, 128), F32) for _ in range(half))
        e, f = lax.fori_loop(0, ROWS, step, (zero, zero), unroll=4)
        for n in range(half):
            e_ref[base + n] = e[n]
            f_ref[base + n] = f[n]


STATE = sds((NST, 8, 128), F32)
SPREAD = sds((9 * ROWS, 128), F32)


def first(info, x, gain, a):
    return pl.pallas_call(
        first_kernel,
        out_shape=(sds((2, ROWS, 1024), BF), SPREAD, STATE, STATE),
        in_specs=[SMEM, FULL, FULL, FULL],
        compiler_params=params(),
        cost_estimate=cost(32_000_000, 3_000_000),
        name="first",
    )(info, x, gain, a)


def run_kernel(us, a_ref, cb_ref, h_ref, s_ref, ss):
    def step(t, h):
        u = at(us, t)
        h = tuple(a_ref[n] * h[n] + u for n in range(NST))
        ss[pl.ds(t, 8, stride=ROWS), :] = tree([cb_ref[n] * h[n] for n in range(NST)])
        return h

    lax.fori_loop(0, ROWS, step, tuple(h_ref[n] for n in range(NST)), unroll=4)
    for lane in range(2):
        for g in range(4):
            s_ref[lane, :, g * 128 : (g + 1) * 128] = ss[pl.ds((lane * 4 + g) * ROWS, ROWS), :].astype(BF)


def state_run(us, a, cb, h):
    return pl.pallas_call(
        run_kernel,
        out_shape=sds((2, ROWS, HALF), BF),
        scratch_shapes=[pltpu.VMEM((9 * ROWS, 128), F32)],
        compiler_params=params(),
        cost_estimate=cost(32_000_000, 2_000_000),
        name="state_run",
    )(us, a, cb, h)


def turn_kernel(keep_ref, got_ref, a_ref, ds_ref, e_ref):
    for half in range(2):
        d = added(keep_ref[0, half], got_ref[0, half])
        for g in range(4):
            ds_ref[pl.ds((half * 4 + g) * ROWS, ROWS), :] = d[:, g * 128 : (g + 1) * 128]
    a = [a_ref[n] for n in range(NST)]

    def step(i, h):
        d = at(ds_ref, ROWS - 1 - i)
        return tuple(a[n] * h[n] + d for n in range(NST))

    h = lax.fori_loop(0, ROWS, step, tuple(jnp.zeros((8, 128), F32) for _ in range(NST)), unroll=4)
    for n in range(NST):
        e_ref[n] = h[n]


def state_turn(keep, got, a):
    return pl.pallas_call(
        turn_kernel,
        out_shape=(SPREAD, STATE),
        compiler_params=params(),
        cost_estimate=cost(16_000_000, 4_000_000),
        name="state_turn",
    )(keep, got, a)


def mid_kernel(base, us, ds, a_ref, cb_ref, h_ref, dus_in, dus, qu_ref, r_ref):
    half = NST // 2
    a = [a_ref[base + n] for n in range(half)]

    def step(i, held):
        q, v, qu, r = held
        t = ROWS - 1 - i
        u, d = at(us, t), at(ds, t)
        v = tuple(a[n] * v[n] + q[n] for n in range(half))
        q = tuple(a[n] * q[n] + d for n in range(half))
        du = tree([cb_ref[base + n] * q[n] for n in range(half)])
        dus[pl.ds(t, 8, stride=ROWS), :] = at(dus_in, t) + du
        qu = tuple(qu[n] + q[n] * u for n in range(half))
        r = tuple(r[n] + v[n] * u for n in range(half))
        return (q, v, qu, r)

    zero = tuple(jnp.zeros((8, 128), F32) for _ in range(half))
    q, v, qu, r = lax.fori_loop(0, ROWS, step, (zero,) * 4, unroll=2)
    for n in range(half):
        qu_ref[n] = qu[n]
        r_ref[n] = r[n] + h_ref[base + n] * (a[n] * v[n] + q[n])


def mid_first_kernel(us, ds, a_ref, cb_ref, h_ref, keep_ref, got_ref, dus, qu_ref, r_ref, g_ref, dq):
    for half in range(2):
        du = added(keep_ref[1, half], got_ref[1, half])
        for g in range(4):
            k = half * 4 + g
            piece = du[:, g * 128 : (g + 1) * 128]
            dq[pl.ds(k * ROWS, ROWS), :] = piece
            g_ref[k : k + 1, :] = jnp.sum(piece * us[pl.ds(k * ROWS, ROWS), :], axis=0, keepdims=True)
    mid_kernel(0, us, ds, a_ref, cb_ref, h_ref, dq, dus, qu_ref, r_ref)


def state_mid(us, ds, a, cb, h, keep, got):
    part = sds((NST // 2, 8, 128), F32)
    return pl.pallas_call(
        mid_first_kernel,
        out_shape=(SPREAD, part, part, sds((8, 128), F32)),
        scratch_shapes=[pltpu.VMEM((9 * ROWS, 128), F32)],
        compiler_params=params(),
        cost_estimate=cost(40_000_000, 4_000_000),
        name="state_mid_0",
    )(us, ds, a, cb, h, keep, got)


def state_mid_more(us, ds, a, cb, h, dus):
    part = sds((NST // 2, 8, 128), F32)
    return pl.pallas_call(
        lambda *refs: mid_kernel(NST // 2, *refs),
        out_shape=(SPREAD, part, part),
        compiler_params=params(),
        cost_estimate=cost(40_000_000, 4_000_000),
        name="state_mid_1",
    )(us, ds, a, cb, h, dus)


def fix_kernel(info, q_ref, a_ref, cb_ref, e_ref, f_ref, h_ref, far_ref, qu_0, qu_1, r_0, r_1, g_ref, gain, gain_two, out):
    half = NST // 2

    def halved(v):
        return jnp.where(info[0] == 0, v[:, :HALF], v[:, HALF:])

    def put(row, v, scale):
        both = v[:4] + v[4:]
        for g in range(4):
            at_c = slice(g * 128, (g + 1) * 128)
            value = both[g : g + 1]
            out[row : row + 1, at_c] = value * scale[:, at_c] if scale is not None else value

    gain_c = halved(gain[...])
    total = g_ref[...]
    for n in range(NST):
        q = q_ref[n]
        qu = (qu_0, qu_1)[n // half][n % half] + q * a_ref[n] * e_ref[n]
        r = (r_0, r_1)[n // half][n % half] + q * (f_ref[n] + h_ref[n] * (float(ROWS) * far_ref[n]))
        total = total + cb_ref[n] * qu
        put(n, qu, gain_c)
        put(NST + n, r, gain_c)
    put(2 * NST, total, None)
    out[2 * NST + 1 :] = halved(gain_two[...])


def state_fix(info, q, a, cb, e, f, h, far, qu, r, g, gain, gain_two):
    return pl.pallas_call(
        fix_kernel,
        out_shape=sds((2 * NST + 2, HALF), F32),
        in_specs=[SMEM] + [FULL] * 14,
        compiler_params=params(),
        cost_estimate=cost(1_000_000, 1_000_000),
        name="state_fix",
    )(info, q, a, cb, e, f, h, far, *qu, *r, g, gain, gain_two)


def last_kernel(info, dus, a_ref, cb_ref, q_ref, mine_ref, give_ref, out):
    def step(i, q):
        t = ROWS - 1 - i
        q = tuple(a_ref[n] * q[n] for n in range(NST))
        out[pl.ds(t, 8, stride=ROWS), :] = at(dus, t) + tree([cb_ref[n] * q[n] for n in range(NST)])
        return q

    lax.fori_loop(0, ROWS, step, tuple(q_ref[n] for n in range(NST)), unroll=4)
    mine = pl.multiple_of(info[0] * 128, 128)
    give = pl.multiple_of((1 - info[0]) * 128, 128)
    for lane in range(2):
        for g in range(4):
            base = (lane * 4 + g) * ROWS
            at_c = slice(g * 128, (g + 1) * 128)
            mine_ref[lane, :, at_c] = out[pl.ds(base + mine, 128), :]
            give_ref[lane, :, at_c] = out[pl.ds(base + give, 128), :]


def state_last(info, dus, a, cb, q):
    half = sds((2, 128, HALF), F32)
    return pl.pallas_call(
        last_kernel,
        out_shape=(half, half),
        in_specs=[SMEM] + [FULL] * 4,
        scratch_shapes=[pltpu.VMEM((9 * ROWS, 128), F32)],
        compiler_params=params(),
        cost_estimate=cost(32_000_000, 2_000_000),
        name="state_last",
    )(info, dus, a, cb, q)


def added(left, right):
    return left.astype(F32) + right.astype(F32)


def wide(v):
    return v.reshape(v.shape[0] * v.shape[1], v.shape[2])


class Weights:
    def __init__(self, info, full_ref, w, sems):
        self.y, self.full, self.w, self.sems = info[3], full_ref, w, sems
        self.copies = {}

    def start(self, order):
        for n in order:
            rows, cols = pl.ds(128 + 32 * (n // 2), 32), pl.ds(HALF * (n % 2), HALF)
            self.copies[n] = [
                pltpu.make_async_copy(self.full.at[:, r, rows, cols], self.w.at[n, r], self.sems.at[n, r])
                for r in range(2)
            ]
            for c in self.copies[n]:
                c.start()

    def wait(self, n):
        for c in self.copies[n]:
            c.wait()

    def half(self, n, half):
        return wide(self.w[n, half ^ self.y])

    def out(self, half):
        return wide(self.w[3, half])


WEIGHTS = [pltpu.VMEM((4, 2, 16, 32, HALF), BF), pltpu.SemaphoreType.DMA((4, 2))]
HBM = pl.BlockSpec(memory_space=pltpu.HBM)


def bring(pairs, sems):
    sems = sems if isinstance(sems, list) else [sems.at[n] for n in range(len(pairs))]
    copies = [pltpu.make_async_copy(src, dst, sem) for (src, dst), sem in zip(pairs, sems)]
    for copy in copies:
        copy.start()
    return copies


INPUTS = [pltpu.VMEM((2, ROWS, 1024), BF)] + [pltpu.VMEM((2 * ROWS, HALF), BF)] * 2 + [pltpu.SemaphoreType.DMA((6,))]


def used(p_ref, half):
    return p_ref.at[half, :, :, pl.ds(0, ROWS * (half + 1))]


def attn_kernel(
    info, u_in, own_in, sib_in, full_ref, part_ref, q_out, k_out, v_out, o_out, p_out,
    q_ref, k_ref, v_ref, o_ref, p_ref, out_sems, w_s, sems, u_ref, own, sib, in_sems,
):
    w = Weights(info, full_ref, w_s, sems)
    w.start((0,))
    arriving = bring(((u_in, u_ref), (own_in, own), (sib_in, sib)), in_sems)
    w.start((1, 2, 3))
    me, it = info[0], 1 - info[0]
    leaving = []

    def leave(src, dst, *place):
        copy = pltpu.make_async_copy(src, dst, out_sems.at[place])
        copy.start()
        leaving.append(copy)

    arriving[0].wait()
    w.wait(0)
    for half in range(2):
        u = u_ref[half]
        q_ref[half] = (dot(u[:, :HALF], w.half(0, 0)) + dot(u[:, HALF:], w.half(0, 1))).astype(BF)
    leave(q_ref, q_out, 0, 0)
    for copy in arriving[1:]:
        copy.wait()
    for n, ref, out in ((1, k_ref, k_out), (2, v_ref, v_out)):
        w.wait(n)
        ref[...] = (dot(own[...], w.half(n, me)) + dot(sib[...], w.half(n, it))).astype(BF)
        leave(ref, out, n, 0)
    w.wait(3)
    for half in range(2):
        seen = ROWS * (half + 1)
        row = lax.broadcasted_iota(jnp.int32, (ROWS, seen), 0) + half * ROWS
        allowed = lax.broadcasted_iota(jnp.int32, (ROWS, seen), 1) <= row
        for h in range(4):
            at_h = slice(h * HEAD_DIM, (h + 1) * HEAD_DIM)
            s = dot_nt(q_ref[half, :, at_h], k_ref[:seen, at_h]) * HEAD_DIM**-0.5
            s = jnp.where(allowed, s, MASKED)
            e = jnp.exp(s - jnp.max(s, axis=-1, keepdims=True))
            p = (e / jnp.sum(e, axis=-1, keepdims=True)).astype(BF)
            p_ref[half, h, :, :seen] = p
            o_ref[half, :, at_h] = dot(p, v_ref[:seen, at_h]).astype(BF)
        leave(used(p_ref, half), used(p_out, half), 3, half)
        leave(o_ref.at[half], o_out.at[half], 4, half)
        o = o_ref[half]
        for side in range(2):
            part_ref[half, :, side * HALF : (side + 1) * HALF] = dot(o, w.out(side)).astype(BF)
    for copy in leaving:
        copy.wait()


KEPT = [
    pltpu.VMEM((2, ROWS, HALF), BF), pltpu.VMEM((2 * ROWS, HALF), BF), pltpu.VMEM((2 * ROWS, HALF), BF),
    pltpu.VMEM((2, ROWS, HALF), BF), pltpu.VMEM((2, 4, ROWS, 2 * ROWS), BF), pltpu.SemaphoreType.DMA((5, 2)),
]


def attention(info, u, own, sib, full):
    return pl.pallas_call(
        attn_kernel,
        out_shape=(
            sds((2, ROWS, 1024), BF), sds((2, ROWS, HALF), BF), sds((2 * ROWS, HALF), BF),
            sds((2 * ROWS, HALF), BF), sds((2, ROWS, HALF), BF), sds((2, 4, ROWS, 2 * ROWS), BF),
        ),
        in_specs=[SMEM] + [HBM] * 4,
        out_specs=(FULL, HBM, HBM, HBM, HBM, HBM),
        scratch_shapes=KEPT + WEIGHTS + INPUTS,
        compiler_params=params(BIG),
        cost_estimate=cost(4_000_000_000, 16_000_000),
        name="attention",
    )(info, u, own, sib, full)


def attn_back_kernel(
    info, own_in, sib_in, mid_in, dy_in, gain_ref, full_ref, q_in, k_in, v_in, o_in, p_in,
    os_in, u_in, so_in, ss_in, held_ref, dm_out, g_ref, dq_out, dk_out, dv_out, grad_ref,
    q_ref, k_ref, v_ref, o_ref, p_ref, in_sems, w_s, sems, grads, out_sems,
    u_ref, s_own, s_sib, late_sems, os_ref, own_ref, sib_ref, mid_ref, dy_ref, dm_ref, first_sems,
    dq_ref, dk_ref, dv_ref, made_sems,
):
    del held_ref
    early = []
    for lane in range(2):
        pairs = ((own_in, own_ref), (sib_in, sib_ref), (mid_in, mid_ref), (dy_in, dy_ref))
        early.append(bring([(a.at[lane], b.at[lane]) for a, b in pairs], first_sems.at[lane]))
    w = Weights(info, full_ref, w_s, sems)
    w.start((3,))
    pairs = ((v_in, v_ref), (k_in, k_ref), (q_in, q_ref), (o_in, o_ref))
    pairs += tuple((used(p_in, half), used(p_ref, half)) for half in range(2))
    arriving = bring(pairs, [in_sems.at[n, 0] for n in range(5)] + [in_sems.at[0, 1]])
    me, it = info[0], 1 - info[0]
    scale = HEAD_DIM**-0.5
    gain_grad = jnp.zeros((1, 1024), F32)
    branches = []
    leaving = []

    def leave(src, dst, sem):
        copy = pltpu.make_async_copy(src, dst, sem)
        copy.start()
        leaving.append(copy)

    for lane in range(2):
        for copy in early[lane]:
            copy.wait()
        if lane == 1:
            late = bring(((u_in, u_ref), (so_in, s_own), (ss_in, s_sib), (os_in, os_ref)), late_sems)
        m = mid_ref[lane]
        dz = added(own_ref[lane], sib_ref[lane])
        inverse = rms_scale(m)
        unit = m * inverse
        gain_grad = gain_grad + jnp.sum(dz * unit, axis=0, keepdims=True)
        scaled = dz * gain_ref[...]
        dm = dy_ref[lane].astype(F32) + inverse * (
            scaled - unit * jnp.mean(scaled * unit, axis=-1, keepdims=True)
        )
        dm_ref[lane] = dm
        own_rows = pl.ds(pl.multiple_of(info[0] * 128, 128), 128)
        leave(dm_ref.at[lane, own_rows], dm_out.at[lane], made_sems.at[0, lane])
        branch = (live_of(info, lane) * dm).astype(BF)
        branches.append(branch)
    g_ref[...] = gain_grad
    w.wait(3)
    for copy in arriving:
        copy.wait()
    d_o = []
    for half in range(2):
        branch = branches[half]
        d_o.append((dot_nt(branch[:, :HALF], w.out(0)) + dot_nt(branch[:, HALF:], w.out(1))).astype(BF))
    for h in range(4):
        at_h = slice(h * HEAD_DIM, (h + 1) * HEAD_DIM)
        dk, dv = [], []
        for half in range(2):
            seen = ROWS * (half + 1)
            p_low = p_ref[half, h, :, :seen]
            p = p_low.astype(F32)
            d_o_h = d_o[half][:, at_h]
            dp = dot_nt(d_o_h, v_ref[:seen, at_h])
            total = jnp.sum(p * dp, axis=-1, keepdims=True)
            ds = (p * (dp - total)).astype(BF)
            dq_ref[half, :, at_h] = (dot(ds, k_ref[:seen, at_h]) * scale).astype(BF)
            dk.append(dot_tn(ds, q_ref[half, :, at_h]))
            dv.append(dot_tn(p_low, d_o_h))
        for ref, parts, factor in ((dk_ref, dk, scale), (dv_ref, dv, 1.0)):
            ref[:ROWS, at_h] = ((parts[0] + parts[1][:ROWS]) * factor).astype(BF)
            ref[ROWS:, at_h] = (parts[1][ROWS:] * factor).astype(BF)
    for n, (src, dst) in enumerate(((dq_ref, dq_out), (dk_ref, dk_out), (dv_ref, dv_out))):
        leave(src, dst, made_sems.at[1 + n, 0])

    def leave_grad(n):
        at_r = pl.ds(pl.multiple_of(info[8 + n // 2], 32), 32)
        at_c = pl.ds(HALF * (n % 2), HALF)
        for y in range(2):
            leave(grads.at[n, y], grad_ref.at[:, y ^ info[3], at_r, at_c], out_sems.at[n, y])

    def put(n, half, value):
        grads[n, pl.ds(half, 1)] = value.astype(BF).reshape(1, 16, 32, HALF)

    for copy in late:
        copy.wait()
    branch = jnp.concatenate(branches, axis=0)
    branch = jnp.where(info[0] == 0, branch[:, :HALF], branch[:, HALF:])
    for half, ref in ((me, o_ref), (it, os_ref)):
        put(3, half, dot_tn(wide(ref[...]), branch))
    leave_grad(3)
    for n, ref in ((1, dk_ref), (2, dv_ref)):
        for half, s_c in ((me, s_own), (it, s_sib)):
            put(n, half, dot_tn(s_c[...], ref[...]))
        leave_grad(n)
    for half in range(2):
        put(0, half, dot_tn(wide(u_ref[...])[:, half * HALF : (half + 1) * HALF], wide(dq_ref[...])))
    leave_grad(0)
    for copy in leaving:
        copy.wait()


def attention_back(info, own, sib, mid, dy, gain, full, q, k, v, o, p, o_sib, u, s_own, s_sib, held):
    return pl.pallas_call(
        attn_back_kernel,
        out_shape=(
            sds((2, 128, 1024), F32), sds((1, 1024), F32), sds((2, ROWS, HALF), BF),
            sds((2 * ROWS, HALF), BF), sds((2 * ROWS, HALF), BF), sds(held.shape, BF),
        ),
        in_specs=[SMEM] + [HBM] * 4 + [FULL] + [HBM] * 11,
        out_specs=(HBM, FULL, HBM, HBM, HBM, HBM),
        input_output_aliases={16: 5},
        scratch_shapes=KEPT + WEIGHTS + WEIGHTS + INPUTS + [
            pltpu.VMEM((2, ROWS, HALF), BF), pltpu.VMEM((2, ROWS, 1024), BF), pltpu.VMEM((2, ROWS, 1024), BF),
            pltpu.VMEM((2, ROWS, 1024), F32), pltpu.VMEM((2, ROWS, 1024), BF), pltpu.VMEM((2, ROWS, 1024), F32),
            pltpu.SemaphoreType.DMA((2, 4)),
            pltpu.VMEM((2, ROWS, HALF), BF), pltpu.VMEM((2 * ROWS, HALF), BF), pltpu.VMEM((2 * ROWS, HALF), BF),
            pltpu.SemaphoreType.DMA((4, 2)),
        ],
        compiler_params=params(BIG),
        cost_estimate=cost(6_000_000_000, 24_000_000),
        name="attention_back",
    )(info, own, sib, mid, dy, gain, full, q, k, v, o, p, o_sib, u, s_own, s_sib, held)


def inputs_back_kernel(
    info, dq_in, dk_in, dv_in, full_ref, keep_ref, send_ref, w_s, sems, dq_ref, dk_ref, dv_ref, in_sems
):
    w = Weights(info, full_ref, w_s, sems)
    w.start((1, 2))
    arriving = bring(((dk_in, dk_ref), (dv_in, dv_ref), (dq_in, dq_ref)), in_sems)
    w.start((0,))
    for copy in arriving:
        copy.wait()
    for n in (1, 2):
        w.wait(n)
    for ref, half in ((send_ref, 1 - info[0]), (keep_ref, info[0])):
        ds = dot_nt(dk_ref[...], w.half(1, half)) + dot_nt(dv_ref[...], w.half(2, half))
        ref[0] = ds.astype(BF).reshape(2, ROWS, HALF)
    w.wait(0)
    for ref, half in ((send_ref, 1 - info[0]), (keep_ref, info[0])):
        ref[1] = dot_nt(wide(dq_ref[...]), w.half(0, half)).astype(BF).reshape(2, ROWS, HALF)


def inputs_back(info, dq, dk, dv, full):
    return pl.pallas_call(
        inputs_back_kernel,
        out_shape=(sds((2, 2, ROWS, HALF), BF), sds((2, 2, ROWS, HALF), BF)),
        in_specs=[SMEM] + [HBM] * 4,
        scratch_shapes=WEIGHTS + [
            pltpu.VMEM((2, ROWS, HALF), BF), pltpu.VMEM((2 * ROWS, HALF), BF), pltpu.VMEM((2 * ROWS, HALF), BF),
            pltpu.SemaphoreType.DMA((3,)),
        ],
        compiler_params=params(BIG),
        cost_estimate=cost(2_000_000_000, 7_000_000),
        name="inputs_back",
    )(info, dq, dk, dv, full)


GELU_C = 0.7978845608028654
GELU_K = 0.044715


def ffn_kernel(
    info, x_ref, part_ref, sib_ref, gain_ref, d_ref, up_ref, down_ref,
    mid_out, dz_ref, hidden_ref, grad_ref, z_s, dz_s, gu_s, gd_s, sems, mid_ref, mid_sems,
):
    step = pl.program_id(0)

    def mid_copy(k):
        return pltpu.make_async_copy(mid_ref.at[k], mid_out.at[k], mid_sems.at[k])

    slot = step % 2
    place, near = step % 2, step // 2
    side = near ^ info[3]

    def copies(slot, place, near):
        at_c = pl.ds(pl.multiple_of(place * HALF, HALF), HALF)
        at_r = pl.ds(pl.multiple_of(info[5 + (near ^ info[3])], 32), 32)
        at_z = pl.ds(place * 8, 8)
        made = [pltpu.make_async_copy(gu_s.at[slot], grad_ref.at[:, :, at_r, at_c], sems.at[0, slot])]
        for k in range(2):
            at_r = pl.ds(pl.multiple_of(info[7 + 3 * k], 32), 32)
            src = gd_s.at[slot, :, pl.ds(32 * k, 32), :]
            made.append(pltpu.make_async_copy(src, grad_ref.at[at_z, near, at_r, :], sems.at[1 + k, slot]))
        return made

    @pl.when(step == 0)
    def _():
        for lane in range(2):
            live = live_of(info, lane)
            m = x_ref[lane].astype(F32) + live * added(part_ref[lane], sib_ref[lane])
            mid_ref[lane] = m
            mid_copy(lane).start()
            z_s[lane * ROWS : (lane + 1) * ROWS] = (m * rms_scale(m) * gain_ref[...]).astype(BF)
        dz_s[...] = jnp.zeros_like(dz_s)

    z, d = z_s[...], d_ref[...]
    down = wide(down_ref[:, 0])
    up_0, up_1 = (up_ref[:, pl.ds(y ^ info[3], 1)].reshape(HALF, HALF) for y in range(2))
    f = dot(z[:, :HALF], up_0) + dot(z[:, HALF:], up_1)
    square = f * f
    h = 0.5 + 0.5 * jnp.tanh(GELU_C * f + (GELU_C * GELU_K) * f * square)
    hidden = (f * h).astype(BF)
    slope = h + (h - h * h) * (2.0 * GELU_C * f + (6.0 * GELU_C * GELU_K) * f * square)
    hidden_ref[...] = hidden
    back = (slope * dot_nt(d, down)).astype(BF)

    @pl.when(step >= 2)
    def _():
        for c in copies(slot, place, near):
            c.wait()

    gd_s[slot] = dot_tn(hidden, d).astype(BF).reshape(8, 64, 1024)
    gu = dot_tn(z, back).astype(BF).reshape(2, 16, 32, HALF)
    for y in range(2):
        gu_s[slot, :, pl.ds(y ^ info[3], 1)] = gu[y].reshape(16, 1, 32, HALF)
    for c in copies(slot, place, near):
        c.start()
    dz_s[:, :HALF] += dot_nt(back, up_0)
    dz_s[:, HALF:] += dot_nt(back, up_1)

    @pl.when(step == pl.num_programs(0) - 1)
    def _():
        for lane in range(2):
            dz_ref[lane] = dz_s[lane * ROWS : (lane + 1) * ROWS].astype(BF)
            mid_copy(lane).wait()
        for k in range(2):
            for c in copies(k, place, near):
                c.wait()


def feed_forward(info, x, part, sib, gain, d, weights):
    chunk = pl.BlockSpec((2 * ROWS, HALF), lambda i, info: (0, i))
    return pl.pallas_call(
        ffn_kernel,
        grid_spec=pltpu.PrefetchScalarGridSpec(
            num_scalar_prefetch=1,
            grid=(4,),
            in_specs=[
                FULL, FULL, FULL, FULL, FULL,
                pl.BlockSpec((16, 2, 32, HALF), lambda i, info: (0, 0, (i // 2) ^ info[3], i % 2)),
                pl.BlockSpec((8, 1, 64, 1024), lambda i, info: (i % 2, i // 2, 1, 0)),
            ],
            out_specs=(HBM, FULL, chunk, HBM),
            scratch_shapes=[
                pltpu.VMEM((2 * ROWS, 1024), BF), pltpu.VMEM((2 * ROWS, 1024), F32),
                pltpu.VMEM((2, 16, 2, 32, HALF), BF), pltpu.VMEM((2, 8, 64, 1024), BF),
                pltpu.SemaphoreType.DMA((3, 2)),
                pltpu.VMEM((2, ROWS, 1024), F32), pltpu.SemaphoreType.DMA((2,)),
            ],
        ),
        out_shape=(
            sds((2, ROWS, 1024), F32), sds((2, ROWS, 1024), BF), sds((2 * ROWS, 2048), BF),
            sds((16, 2, 192, 1024), BF),
        ),
        compiler_params=params(BIG),
        cost_estimate=cost(9_000_000_000, 28_000_000),
        name="feed_forward",
    )(info, x, part, sib, gain, d, weights, weights)


DOWN = pl.BlockSpec((8, 1, 64, 1024), lambda i: (i % 2, i // 2, 1, 0))
CHUNK = pl.BlockSpec((2 * ROWS, HALF), lambda i: (0, i))


def hidden_out_kernel(info, hidden_ref, mid_ref, down_ref, keep_ref, send_ref, out_s):
    step = pl.program_id(0)
    more = dot(hidden_ref[...], wide(down_ref[:, 0]))

    @pl.when(step == 0)
    def _():
        out_s[...] = more

    @pl.when(step > 0)
    def _():
        out_s[...] += more

    @pl.when(step == pl.num_programs(0) - 1)
    def _():
        for half in range(2):
            out = live_of(info, half) * out_s[half * ROWS : (half + 1) * ROWS]
            total = out + mid_ref[half]
            keep_ref[half] = jnp.where(info[0] == 0, total[:128], total[128:])
            send_ref[half] = jnp.where(info[0] == 0, out[128:], out[:128]).astype(BF)


def hidden_out(info, hidden, mid, weights):
    return pl.pallas_call(
        hidden_out_kernel,
        grid=(4,),
        out_shape=(sds((2, 128, 1024), F32), sds((2, 128, 1024), BF)),
        in_specs=[SMEM, CHUNK, FULL, DOWN],
        out_specs=(FULL, FULL),
        scratch_shapes=[pltpu.VMEM((2 * ROWS, 1024), F32)],
        compiler_params=params(BIG),
        cost_estimate=cost(2_100_000_000, 8_000_000),
        name="hidden_out",
    )(info, hidden, mid, weights)


STEPS = (("x", "c"), ("z", "a"), ("z", "b"), ("y", "a"))


def carry(ends, far, rate, block, lane, reverse, between=None):
    low, high = ends[:, :4], ends[:, 4:]
    far, rate = far[:, :4], rate[:, :4]
    first, second = (high, low) if reverse else (low, high)
    total = far * first + second
    entering = jnp.zeros_like(total)
    for k, (axis, kind) in enumerate(STEPS):
        if between is not None:
            total = between(k, total)
        other = flip(total, axis, kind)
        upper = (block >> k) & 1
        within = block & ((1 << k) - 1)
        if reverse:
            takes, gap = upper == 0, (1 << k) - 1 - within
        else:
            takes, gap = upper == 1, within
        reach = jnp.exp(-rate * (BLOCK * gap).astype(F32)) * other
        whole = jnp.exp(-rate * float(BLOCK << k))
        joined = whole * jnp.where(takes, other, total) + jnp.where(takes, total, other)
        if k >= 2:
            reach = jnp.where(lane == 1, 0.0, reach)
            joined = jnp.where(lane == 1, 0.0, joined)
        entering = entering + jnp.where(takes, reach, 0.0)
        total = joined
    inner = first + far * entering
    return jnp.concatenate([inner, entering] if reverse else [entering, inner], axis=1)


def adam(factor, w_ref, f_ref, s_ref, grad, outs, rate, decay):
    clipped = grad * factor
    first_new = BETA_ONE * f_ref[...] + (1.0 - BETA_ONE) * clipped
    second_new = BETA_TWO * s_ref[...] + (1.0 - BETA_TWO) * clipped * clipped
    fix_one = 1.0 - BETA_ONE**STEP
    fix_two = 1.0 - BETA_TWO**STEP
    direction = first_new / fix_one / (jnp.sqrt(second_new / fix_two) + ADAM_EPS)
    weight = w_ref[...]
    weight_new = weight - rate * (direction + decay * weight)
    for ref, v in zip(outs, (first_new, second_new, weight_new, weight_new.astype(BF))):
        ref[...] = v


def finish_kernel(info, mine, near, over, cross, state, gain, own_ref, give_ref, squares_ref):
    total = added(mine[...], near[...]) + added(over[...], cross[...])
    squares = jnp.sum(total * total, axis=0, keepdims=True)
    squares = jnp.sum(squares.reshape(1, 8, 128), axis=1)
    squares = jnp.sum(squares, axis=1, keepdims=True)
    for ref in (state, gain):
        piece = ref[...].reshape(-1, 16)
        piece = jnp.sum(piece * piece, axis=0, keepdims=True)
        squares = squares + 0.5 * jnp.sum(piece, axis=1, keepdims=True)
    squares_ref[...] = jnp.broadcast_to(squares, (64, 128))
    own_ref[32:] = total[64:]
    for k in range(2):
        low, high = total[32 * k : 32 * k + 16], total[32 * k + 16 : 32 * k + 32]
        own_ref[16 * k : 16 * k + 16] = jnp.where(info[0] == 0, low, high)
        give_ref[16 * k : 16 * k + 16] = jnp.where(info[0] == 0, high, low)


def finish(info, mine, near, over, cross, state, gain):
    return pl.pallas_call(
        finish_kernel,
        out_shape=(sds((64, 1024), F32), sds((32, 1024), F32), sds((64, 128), F32)),
        in_specs=[SMEM] + [FULL] * 6,
        compiler_params=params(),
        cost_estimate=cost(2_000_000, 3_000_000),
        name="finish",
    )(info, mine, near, over, cross, state, gain)


def update_kernel(info, *refs):
    ins, outs = refs[:22], refs[22:]
    weights, firsts, seconds = ins[:5], ins[5:10], ins[10:15]
    every, mine, got, mine_far, got_far, state, gain = ins[15:]
    norm = jnp.sqrt(jnp.sum(every[...], axis=0, keepdims=True)[:, :1])
    outs[20][...] = norm
    factor = jnp.minimum(1.0, CLIP_NORM / norm)
    zero = info[0] == 0
    here = info[11] == 0

    def pair(one, two):
        first, second = jnp.where(zero, one, two), jnp.where(zero, two, one)
        return first.reshape(2, 16, 1024), second.reshape(2, 16, 1024)

    down = jnp.concatenate(
        [jnp.where(here, mine[32:], mine_far[32:]), jnp.where(here, mine_far[32:], mine[32:])], axis=0
    )
    near, far = pair(mine[:32], got[...]), pair(mine_far[:32], got_far[...])
    first, second = (jnp.where(here, b, a) for a, b in zip(near, far))
    matrices = []
    for n in range(4):
        at_c = slice(HALF * (n % 2), HALF * (n % 2) + HALF)
        matrices.append(jnp.concatenate([first[n // 2, :, at_c], second[n // 2, :, at_c]], axis=1))
    attn_grad = jnp.stack(matrices)
    first, second = (jnp.where(here, a, b) for a, b in zip(near, far))
    pieces = []
    for side in range(2):
        for k in range(16):
            at_c = slice(64 * k, 64 * k + 64)
            pieces += [first[side, :, at_c], second[side, :, at_c]]
    up_grad = jnp.concatenate(pieces, axis=1)
    grads = (attn_grad, up_grad, down, state[...], gain[...])
    rates = ((RATE_MATRIX, WEIGHT_DECAY),) * 3 + ((RATE_STATE, 0.0), (RATE_GAIN, 0.0))
    for k in range(5):
        adam(factor, weights[k], firsts[k], seconds[k], grads[k], outs[4 * k : 4 * k + 4], *rates[k])


def update(info, weights, firsts, seconds, grads):
    shapes = []
    for w in weights:
        shapes += [sds(w.shape, F32)] * 3 + [sds(w.shape, BF)]
    return pl.pallas_call(
        update_kernel,
        out_shape=tuple(shapes) + (sds((1, 1), F32),),
        in_specs=[SMEM] + [FULL] * 22,
        compiler_params=pltpu.CompilerParams(vmem_limit_bytes=24 * 1024 * 1024),
        cost_estimate=cost(4_000_000, 6_000_000),
        name="update",
    )(info, *weights, *firsts, *seconds, *grads)


def body(
    tokens, cotangent, lengths, attn_weight, up_weight, down_weight, state_param, norm_gain,
    attn_first, attn_second, up_first, up_second, down_first, down_second,
    state_first, state_second, gain_first, gain_second,
):
    core = lax.axis_index("core")
    ybit = lax.axis_index("y")
    chip = (ybit * 4 + lax.axis_index("z")) * 4 + lax.axis_index("x")

    lane = chip % 2
    block = chip // 2

    def of_lane(v, which):
        return lax.dynamic_index_in_dim(v, which, 0, keepdims=False)

    def halves(mine, got):
        return jnp.stack([jnp.where(lane == 0, mine, got), jnp.where(lane == 0, got, mine)])

    x_give, dy_give = of_lane(tokens[0], 1 - lane), of_lane(cotangent[0], 1 - lane)
    x_got, dy_got = flip(x_give, "x"), flip(dy_give, "x")

    mine = jnp.concatenate(
        [state_param.astype(BF).transpose(0, 2, 1).reshape(-1), norm_gain.astype(BF).reshape(-1)]
    )
    mine = jnp.pad(mine, (0, 1024 - mine.shape[0])).reshape(1, 8, 128)
    pair = ordered(core, mine, swap(mine), 0)
    small = lax.all_to_all(
        jnp.broadcast_to(pair[None], (32, 2, 8, 128)), CHIPS, split_axis=0, concat_axis=0, tiled=True
    ).reshape(64, 1024)
    theta = small[:, :768].reshape(64, 3, NST, 16).transpose(1, 2, 0, 3).reshape(3, NST, 1024).astype(F32)
    gains = small[:, 768:800].reshape(64, 2, 16).transpose(1, 0, 2).reshape(2, 1024).astype(F32)

    slot_blocks = SLOT // BLOCK
    live_len = lax.dynamic_index_in_dim(lengths[0], block // slot_blocks, 0, keepdims=False)
    live_rows = jnp.clip(live_len - (block % slot_blocks) * BLOCK, 0, BLOCK)
    live_rows = jnp.where(lane == 0, BLOCK, live_rows)
    group = lax.axis_index("grp")
    places = [((b + 3 * group) % 6) * 32 for b in range(6)]
    info = jnp.stack([core, live_rows, lane, ybit, chip] + places + [group]).astype(jnp.int32)

    attn_low = attn_weight.astype(BF)
    up_low = up_weight.astype(BF).reshape(16, 32, 2, 64).transpose(2, 0, 1, 3).reshape(2, 16, 2048)
    down_low = down_weight.astype(BF)
    qkv_keep = lax.dynamic_slice_in_dim(attn_low[:3], core * HALF, HALF, 2)
    qkv_give = lax.dynamic_slice_in_dim(attn_low[:3], (1 - core) * HALF, HALF, 2)
    qkv_chip = ordered(core, qkv_keep, swap(qkv_give), 1)
    out_chip = ordered(core, attn_low[3], swap(attn_low[3]), 0)
    up_keep = lax.dynamic_index_in_dim(up_low, core, 0, keepdims=False)
    up_give = lax.dynamic_index_in_dim(up_low, 1 - core, 0, keepdims=False)
    up_chip = ordered(core, up_keep, swap(up_give), 0)
    up_chip = up_chip.reshape(32, 2, 1024).transpose(1, 0, 2).reshape(64, 1024)
    qk_rows = jnp.concatenate([qkv_chip[0], qkv_chip[1]], axis=1)
    own_rows = jnp.concatenate([up_chip, down_low, qk_rows], axis=0)
    across = [(0, 3), (3, 0), (1, 2), (2, 1)]
    low = jnp.concatenate([own_rows[:96], out_chip[:, :HALF].reshape(16, 1024)], axis=0)
    high = jnp.concatenate([own_rows[96:], jnp.concatenate([qkv_chip[2], out_chip[:, HALF:]], axis=1)], axis=0)
    low, high, pair = lax.optimization_barrier((low, high, pair))
    low_got, high_got = flip(low, "y"), lax.ppermute(high, ("grp", "y"), across)
    out_got = jnp.concatenate([low_got[96:].reshape(32, HALF), high_got[64:, HALF:]], axis=1)
    out_rows = jnp.where(ybit == core, out_chip, out_got)
    own_last = jnp.concatenate([qkv_chip[2], out_rows[:, :HALF]], axis=1)
    other_last = jnp.concatenate([high_got[64:, :HALF], out_rows[:, HALF:]], axis=1)
    all_two = jnp.concatenate([own_rows, own_last, low_got[:96], high_got[:64], other_last], axis=0)
    all_two, x_got, dy_got = lax.optimization_barrier((all_two, x_got, dy_got))
    full = lax.all_gather(all_two.reshape(2, 192, 1024), ("z", "x"), axis=0)
    x_own, dy_own = (halves(of_lane(v[0], lane), got) for v, got in ((tokens, x_got), (cotangent, dy_got)))
    x = ordered(core, x_own, swap(x_own), 1)
    dy = ordered(core, dy_own, swap(dy_own), 1)

    theta_c = lax.dynamic_slice_in_dim(theta, core * HALF, HALF, 2).reshape(3, NST, 4, 128)
    theta_c = jnp.concatenate([theta_c, theta_c], axis=2)
    rate = jnp.exp(theta_c[0]) / BLOCK
    decay = jnp.exp(-rate)
    norm_scale = jnp.sqrt(-jnp.expm1(-2.0 * rate))
    cb = norm_scale * theta_c[1] * theta_c[2]
    far = jnp.exp(-rate * float(ROWS))
    gain_c = lax.dynamic_slice_in_dim(gains[0], core * HALF, HALF, 0).reshape(4, 128)
    gain_c = jnp.concatenate([gain_c, gain_c], axis=0)

    u_low, us, ended, ramp = first(info, x, gains[:1], decay)
    entering = carry(ended, far, rate, block, lane, False)
    d_low = jnp.where((lax.iota(jnp.int32, BLOCK) < live_rows).reshape(2, ROWS, 1), dy, jnp.zeros((), BF))
    entering, dy, d_low = lax.optimization_barrier((entering, dy, d_low.reshape(2 * ROWS, 1024)))
    sb_own = state_run(us, decay, cb * gain_c, entering).reshape(2 * ROWS, HALF)
    sb_sib = swap(sb_own)

    part, q, k, v, o, p = attention(info, u_low, sb_own, sb_sib, full)
    part_sib, o_sib = lax.optimization_barrier((swap(part), swap(o)))
    middle, dz_part, hidden, ffn_grad = feed_forward(info, x, part, part_sib, gains[1:], d_low, full)
    dm, gain_two_grad, dq, dk, dv, grad = attention_back(
        info, dz_part, swap(dz_part), middle, dy, gains[1:], full, q, k, v, o, p,
        o_sib, u_low, sb_own, sb_sib, ffn_grad,
    )
    grad_part = lax.psum_scatter(grad.reshape(6144, 1024), ("z", "x"), scatter_dimension=0, tiled=True)
    keep, send = inputs_back(info, dq, dk, dv, full)
    got = swap(send)
    ds, started = state_turn(keep, got, decay)
    mids = {}

    def before(k, total):
        if k == 2:
            made = state_mid(us, ds, decay, cb, entering, keep, got)
            total, *mids["first"] = lax.optimization_barrier((total,) + tuple(made))
        if k == 3:
            made = state_mid_more(us, ds, decay, cb, entering, mids["first"][0])
            total, *mids["second"] = lax.optimization_barrier((total,) + tuple(made))
        return total

    leaving = carry(started, far, rate, block, lane, True, before)
    _, qu_0, r_0, gain_q = mids["first"]
    dus, qu_1, r_1 = mids["second"]
    qu, rr = (qu_0, qu_1), (r_0, r_1)
    lanes = state_fix(
        info, leaving, decay, cb, ended, ramp, entering, far, qu, rr, gain_q, gains[:1], gain_two_grad
    )
    du_mine, du_give = state_last(info, dus, decay, cb, leaving)

    out_keep, out_send = hidden_out(info, hidden, middle, full)
    out_own = (out_keep + swap(out_send).astype(F32)).astype(BF)

    du_own = ordered(core, du_mine, swap(du_give), 2)
    x_own = x_own.astype(F32)
    grad_own = (norm_back(du_own, x_own, rms_scale(x_own), gains[0]) + dm).astype(BF)

    packed = lanes.reshape(34, 32, 16).transpose(1, 0, 2)
    small_got = lax.all_to_all(packed, CHIPS, split_axis=0, concat_axis=0, tiled=True)
    small_sum = jnp.sum(small_got, axis=0)
    small_sum = small_sum + flip(small_sum, "grp")
    hand = []
    for j in range(32):
        for c in range(2):
            hand.append((j * 2 + c, c * 32 + j))
    mine_sum = lax.ppermute(small_sum, SHARD, hand)

    t_own = state_param.astype(BF).astype(F32).transpose(0, 2, 1)
    rate_o = jnp.exp(t_own[0]) / BLOCK
    decay_o = jnp.exp(-rate_o)
    scale_o = jnp.sqrt(-jnp.expm1(-2.0 * rate_o))
    b_o = scale_o * t_own[1]
    qu_o, rr_o = mine_sum[:NST], mine_sum[NST : 2 * NST]
    gb = t_own[2] * qu_o
    log_rate_grad = rate_o * (
        -decay_o * t_own[2] * b_o * rr_o + decay_o * decay_o / scale_o * t_own[1] * gb
    )
    state_grad = jnp.stack([log_rate_grad, scale_o * gb, b_o * qu_o]).transpose(0, 2, 1)
    gain_grad = mine_sum[2 * NST :]

    mine = [of_lane(v, lane) for v in (out_own, grad_own)]
    give = jnp.stack([of_lane(v, 1 - lane) for v in (out_own, grad_own)])
    grad_part, state_grad, gain_grad, give, *mine = lax.optimization_barrier(
        (grad_part, state_grad, gain_grad, give, *mine)
    )
    traded = flip(give, "x")
    output, token_grad = (halves(a, b) for a, b in zip(mine, traded))
    here, there, give_here, give_there = (grad_part[96 * k : 96 * k + 96] for k in range(4))
    own, give, squares = finish(
        info, here, flip(give_here, "y"), flip(there, "grp"), lax.ppermute(give_there, ("grp", "y"), across),
        state_grad, gain_grad,
    )
    squares, own, got = lax.optimization_barrier((squares + swap(squares), own, swap(give)))
    every = lax.all_to_all(squares, ("grp",) + CHIPS, split_axis=0, concat_axis=0, tiled=True)
    new = update(
        info,
        (attn_weight, up_weight, down_weight, state_param, norm_gain),
        (attn_first, up_first, down_first, state_first, gain_first),
        (attn_second, up_second, down_second, state_second, gain_second),
        (every, own, got, flip(own, "grp"), flip(got, "grp"), state_grad, gain_grad),
    )
    return (output[None], token_grad[None], new[20][0, 0]) + tuple(new[:20])


def solution(mesh):
    inner = Mesh(mesh.devices.reshape(2, 2, 4, 4, 2), AXES)
    rows = P("grp", None, SHARD, None)
    attn = P(None, SHARD, None)
    flat = P(SHARD, None)
    gain = P(None, SHARD)
    in_specs = (rows, rows, P("grp", None), attn, flat, flat, attn, gain)
    in_specs += (attn, attn, flat, flat, flat, flat, attn, attn, gain, gain)
    out_specs = (rows, rows, P()) + (attn,) * 4 + (flat,) * 8 + (attn,) * 4 + (gain,) * 4
    return jax.shard_map(body, mesh=inner, in_specs=in_specs, out_specs=out_specs, check_vma=False)
```

```python
import jax
import jax.numpy as jnp
from jax import lax
from jax.experimental import pallas as pl
from jax.experimental.pallas import tpu as pltpu
from jax.sharding import Mesh
from jax.sharding import PartitionSpec as P

HEAD_DIM = 128
BLOCK = 512
STEP = 5
SLOT = 2048

EPS_NORM = 1e-05
BETA_ONE = 0.5
BETA_TWO = 0.5
ADAM_EPS = 1e-08
WEIGHT_DECAY = 0.1
CLIP_NORM = 0.5
RATE_MATRIX = 0.02
RATE_STATE = 1.0
RATE_GAIN = 0.6
MASKED = -1e30

AXES = ("grp", "y", "z", "x", "core")
CHIPS = ("y", "z", "x")
SHARD = ("y", "z", "x", "core")
BF = jnp.bfloat16
F32 = jnp.float32
NST = 16
ROWS = 256
HALF = 512


def flip(v, axis, kind="a"):
    if lax.axis_size(axis) == 2:
        pairs = [(0, 1), (1, 0)]
    elif kind == "c":
        pairs = [(0, 2), (2, 0), (1, 3), (3, 1)]
    elif kind == "a":
        pairs = [(0, 1), (1, 0), (2, 3), (3, 2)]
    else:
        pairs = [(0, 3), (3, 0), (1, 2), (2, 1)]
    return lax.ppermute(v, axis, pairs)


def swap(v):
    return flip(v, "core")


def ordered(bit, own, other, axis):
    first = jnp.where(bit == 0, own, other)
    second = jnp.where(bit == 0, other, own)
    return jnp.concatenate([first, second], axis=axis)


def rms_scale(value):
    return lax.rsqrt(jnp.mean(value * value, axis=-1, keepdims=True) + EPS_NORM)


def norm_back(grad, value, inverse, gain):
    unit = value * inverse
    scaled = grad * gain
    return inverse * (scaled - unit * jnp.mean(scaled * unit, axis=-1, keepdims=True))


def dot(left, right):
    return jnp.dot(left, right, preferred_element_type=F32)


def dot_nt(left, right):
    return lax.dot_general(left, right, (((1,), (1,)), ((), ())), preferred_element_type=F32)


def dot_tn(left, right):
    return lax.dot_general(left, right, (((0,), (0,)), ((), ())), preferred_element_type=F32)


def params(mib=16):
    return pltpu.CompilerParams(vmem_limit_bytes=mib * 1024 * 1024)


BIG = 53


def cost(flops, bytes_accessed):
    return pl.CostEstimate(flops=flops, bytes_accessed=bytes_accessed, transcendentals=0)


def sds(shape, dtype):
    return jax.ShapeDtypeStruct(shape, dtype)


SMEM = pl.BlockSpec(memory_space=pltpu.SMEM)
FULL = pl.BlockSpec(memory_space=pltpu.VMEM)


def live_of(info, half):
    return (lax.broadcasted_iota(jnp.int32, (ROWS, 1), 0) + half * ROWS < info[1]).astype(F32)


def at(ref, t):
    return ref[pl.ds(t, 8, stride=ROWS), :]


def tree(terms):
    while len(terms) > 1:
        terms = [terms[i] + terms[i + 1] for i in range(0, len(terms), 2)]
    return terms[0]


def first_kernel(info, x_ref, gain_ref, a_ref, low_ref, us_ref, e_ref, f_ref):
    for lane in range(2):
        x = x_ref[lane].astype(F32)
        unit = x * rms_scale(x)
        low_ref[lane] = (unit * gain_ref[...]).astype(BF)
        half = jnp.where(info[0] == 0, unit[:, :HALF], unit[:, HALF:])
        for g in range(4):
            us_ref[pl.ds((lane * 4 + g) * ROWS, ROWS), :] = half[:, g * 128 : (g + 1) * 128]
    half = NST // 2
    for base in (0, half):
        a = [a_ref[base + n] for n in range(half)]

        def step(t, held):
            e, f = held
            u = at(us_ref, t)
            f = tuple(a[n] * (f[n] + e[n]) for n in range(half))
            e = tuple(a[n] * e[n] + u for n in range(half))
            return e, f

        zero = tuple(jnp.zeros((8, 128), F32) for _ in range(half))
        e, f = lax.fori_loop(0, ROWS, step, (zero, zero), unroll=4)
        for n in range(half):
            e_ref[base + n] = e[n]
            f_ref[base + n] = f[n]


STATE = sds((NST, 8, 128), F32)
SPREAD = sds((9 * ROWS, 128), F32)


def first(info, x, gain, a):
    return pl.pallas_call(
        first_kernel,
        out_shape=(sds((2, ROWS, 1024), BF), SPREAD, STATE, STATE),
        in_specs=[SMEM, FULL, FULL, FULL],
        compiler_params=params(),
        cost_estimate=cost(32_000_000, 3_000_000),
        name="first",
    )(info, x, gain, a)


def run_kernel(us, a_ref, cb_ref, h_ref, s_ref, ss):
    def step(t, h):
        u = at(us, t)
        h = tuple(a_ref[n] * h[n] + u for n in range(NST))
        ss[pl.ds(t, 8, stride=ROWS), :] = tree([cb_ref[n] * h[n] for n in range(NST)])
        return h

    lax.fori_loop(0, ROWS, step, tuple(h_ref[n] for n in range(NST)), unroll=4)
    for lane in range(2):
        for g in range(4):
            s_ref[lane, :, g * 128 : (g + 1) * 128] = ss[pl.ds((lane * 4 + g) * ROWS, ROWS), :].astype(BF)


def state_run(us, a, cb, h):
    return pl.pallas_call(
        run_kernel,
        out_shape=sds((2, ROWS, HALF), BF),
        scratch_shapes=[pltpu.VMEM((9 * ROWS, 128), F32)],
        compiler_params=params(),
        cost_estimate=cost(32_000_000, 2_000_000),
        name="state_run",
    )(us, a, cb, h)


def turn_kernel(keep_ref, got_ref, a_ref, ds_ref, e_ref):
    for half in range(2):
        d = added(keep_ref[0, half], got_ref[0, half])
        for g in range(4):
            ds_ref[pl.ds((half * 4 + g) * ROWS, ROWS), :] = d[:, g * 128 : (g + 1) * 128]
    a = [a_ref[n] for n in range(NST)]

    def step(i, h):
        d = at(ds_ref, ROWS - 1 - i)
        return tuple(a[n] * h[n] + d for n in range(NST))

    h = lax.fori_loop(0, ROWS, step, tuple(jnp.zeros((8, 128), F32) for _ in range(NST)), unroll=4)
    for n in range(NST):
        e_ref[n] = h[n]


def state_turn(keep, got, a):
    return pl.pallas_call(
        turn_kernel,
        out_shape=(SPREAD, STATE),
        compiler_params=params(),
        cost_estimate=cost(16_000_000, 4_000_000),
        name="state_turn",
    )(keep, got, a)


def mid_kernel(base, us, ds, a_ref, cb_ref, h_ref, dus_in, dus, qu_ref, r_ref):
    half = NST // 2
    a = [a_ref[base + n] for n in range(half)]

    def step(i, held):
        q, v, qu, r = held
        t = ROWS - 1 - i
        u, d = at(us, t), at(ds, t)
        v = tuple(a[n] * v[n] + q[n] for n in range(half))
        q = tuple(a[n] * q[n] + d for n in range(half))
        du = tree([cb_ref[base + n] * q[n] for n in range(half)])
        dus[pl.ds(t, 8, stride=ROWS), :] = at(dus_in, t) + du
        qu = tuple(qu[n] + q[n] * u for n in range(half))
        r = tuple(r[n] + v[n] * u for n in range(half))
        return (q, v, qu, r)

    zero = tuple(jnp.zeros((8, 128), F32) for _ in range(half))
    q, v, qu, r = lax.fori_loop(0, ROWS, step, (zero,) * 4, unroll=2)
    for n in range(half):
        qu_ref[n] = qu[n]
        r_ref[n] = r[n] + h_ref[base + n] * (a[n] * v[n] + q[n])


def mid_first_kernel(us, ds, a_ref, cb_ref, h_ref, keep_ref, got_ref, dus, qu_ref, r_ref, g_ref, dq):
    for half in range(2):
        du = added(keep_ref[1, half], got_ref[1, half])
        for g in range(4):
            k = half * 4 + g
            piece = du[:, g * 128 : (g + 1) * 128]
            dq[pl.ds(k * ROWS, ROWS), :] = piece
            g_ref[k : k + 1, :] = jnp.sum(piece * us[pl.ds(k * ROWS, ROWS), :], axis=0, keepdims=True)
    mid_kernel(0, us, ds, a_ref, cb_ref, h_ref, dq, dus, qu_ref, r_ref)


def state_mid(us, ds, a, cb, h, keep, got):
    part = sds((NST // 2, 8, 128), F32)
    return pl.pallas_call(
        mid_first_kernel,
        out_shape=(SPREAD, part, part, sds((8, 128), F32)),
        scratch_shapes=[pltpu.VMEM((9 * ROWS, 128), F32)],
        compiler_params=params(),
        cost_estimate=cost(40_000_000, 4_000_000),
        name="state_mid_0",
    )(us, ds, a, cb, h, keep, got)


def state_mid_more(us, ds, a, cb, h, dus):
    part = sds((NST // 2, 8, 128), F32)
    return pl.pallas_call(
        lambda *refs: mid_kernel(NST // 2, *refs),
        out_shape=(SPREAD, part, part),
        compiler_params=params(),
        cost_estimate=cost(40_000_000, 4_000_000),
        name="state_mid_1",
    )(us, ds, a, cb, h, dus)


def fix_kernel(info, q_ref, a_ref, cb_ref, e_ref, f_ref, h_ref, far_ref, qu_0, qu_1, r_0, r_1, g_ref, gain, gain_two, out):
    half = NST // 2

    def halved(v):
        return jnp.where(info[0] == 0, v[:, :HALF], v[:, HALF:])

    def put(row, v, scale):
        both = v[:4] + v[4:]
        for g in range(4):
            at_c = slice(g * 128, (g + 1) * 128)
            value = both[g : g + 1]
            out[row : row + 1, at_c] = value * scale[:, at_c] if scale is not None else value

    gain_c = halved(gain[...])
    total = g_ref[...]
    for n in range(NST):
        q = q_ref[n]
        qu = (qu_0, qu_1)[n // half][n % half] + q * a_ref[n] * e_ref[n]
        r = (r_0, r_1)[n // half][n % half] + q * (f_ref[n] + h_ref[n] * (float(ROWS) * far_ref[n]))
        total = total + cb_ref[n] * qu
        put(n, qu, gain_c)
        put(NST + n, r, gain_c)
    put(2 * NST, total, None)
    out[2 * NST + 1 :] = halved(gain_two[...])


def state_fix(info, q, a, cb, e, f, h, far, qu, r, g, gain, gain_two):
    return pl.pallas_call(
        fix_kernel,
        out_shape=sds((2 * NST + 2, HALF), F32),
        in_specs=[SMEM] + [FULL] * 14,
        compiler_params=params(),
        cost_estimate=cost(1_000_000, 1_000_000),
        name="state_fix",
    )(info, q, a, cb, e, f, h, far, *qu, *r, g, gain, gain_two)


def last_kernel(info, dus, a_ref, cb_ref, q_ref, mine_ref, give_ref, out):
    def step(i, q):
        t = ROWS - 1 - i
        q = tuple(a_ref[n] * q[n] for n in range(NST))
        out[pl.ds(t, 8, stride=ROWS), :] = at(dus, t) + tree([cb_ref[n] * q[n] for n in range(NST)])
        return q

    lax.fori_loop(0, ROWS, step, tuple(q_ref[n] for n in range(NST)), unroll=4)
    mine = pl.multiple_of(info[0] * 128, 128)
    give = pl.multiple_of((1 - info[0]) * 128, 128)
    for lane in range(2):
        for g in range(4):
            base = (lane * 4 + g) * ROWS
            at_c = slice(g * 128, (g + 1) * 128)
            mine_ref[lane, :, at_c] = out[pl.ds(base + mine, 128), :]
            give_ref[lane, :, at_c] = out[pl.ds(base + give, 128), :]


def state_last(info, dus, a, cb, q):
    half = sds((2, 128, HALF), F32)
    return pl.pallas_call(
        last_kernel,
        out_shape=(half, half),
        in_specs=[SMEM] + [FULL] * 4,
        scratch_shapes=[pltpu.VMEM((9 * ROWS, 128), F32)],
        compiler_params=params(),
        cost_estimate=cost(32_000_000, 2_000_000),
        name="state_last",
    )(info, dus, a, cb, q)


def added(left, right):
    return left.astype(F32) + right.astype(F32)


def wide(v):
    return v.reshape(v.shape[0] * v.shape[1], v.shape[2])


class Weights:
    def __init__(self, info, full_ref, w, sems):
        self.y, self.full, self.w, self.sems = info[3], full_ref, w, sems
        self.copies = {}

    def start(self, order):
        for n in order:
            rows, cols = pl.ds(128 + 32 * (n // 2), 32), pl.ds(HALF * (n % 2), HALF)
            self.copies[n] = [
                pltpu.make_async_copy(self.full.at[:, r, rows, cols], self.w.at[n, r], self.sems.at[n, r])
                for r in range(2)
            ]
            for c in self.copies[n]:
                c.start()

    def wait(self, n):
        for c in self.copies[n]:
            c.wait()

    def half(self, n, half):
        return wide(self.w[n, half ^ self.y])

    def out(self, half):
        return wide(self.w[3, half])


WEIGHTS = [pltpu.VMEM((4, 2, 16, 32, HALF), BF), pltpu.SemaphoreType.DMA((4, 2))]
HBM = pl.BlockSpec(memory_space=pltpu.HBM)


def bring(pairs, sems):
    sems = sems if isinstance(sems, list) else [sems.at[n] for n in range(len(pairs))]
    copies = [pltpu.make_async_copy(src, dst, sem) for (src, dst), sem in zip(pairs, sems)]
    for copy in copies:
        copy.start()
    return copies


INPUTS = [pltpu.VMEM((2, ROWS, 1024), BF)] + [pltpu.VMEM((2 * ROWS, HALF), BF)] * 2 + [pltpu.SemaphoreType.DMA((6,))]


def used(p_ref, half):
    return p_ref.at[half, :, :, pl.ds(0, ROWS * (half + 1))]


def attn_kernel(
    info, u_in, own_in, sib_in, full_ref, part_ref, q_out, k_out, v_out, o_out, p_out,
    q_ref, k_ref, v_ref, o_ref, p_ref, out_sems, w_s, sems, u_ref, own, sib, in_sems,
):
    w = Weights(info, full_ref, w_s, sems)
    w.start((0,))
    arriving = bring(((u_in, u_ref), (own_in, own), (sib_in, sib)), in_sems)
    w.start((1, 2, 3))
    me, it = info[0], 1 - info[0]
    leaving = []

    def leave(src, dst, *place):
        copy = pltpu.make_async_copy(src, dst, out_sems.at[place])
        copy.start()
        leaving.append(copy)

    arriving[0].wait()
    w.wait(0)
    for half in range(2):
        u = u_ref[half]
        q_ref[half] = (dot(u[:, :HALF], w.half(0, 0)) + dot(u[:, HALF:], w.half(0, 1))).astype(BF)
    leave(q_ref, q_out, 0, 0)
    for copy in arriving[1:]:
        copy.wait()
    for n, ref, out in ((1, k_ref, k_out), (2, v_ref, v_out)):
        w.wait(n)
        ref[...] = (dot(own[...], w.half(n, me)) + dot(sib[...], w.half(n, it))).astype(BF)
        leave(ref, out, n, 0)
    w.wait(3)
    for half in range(2):
        seen = ROWS * (half + 1)
        row = lax.broadcasted_iota(jnp.int32, (ROWS, seen), 0) + half * ROWS
        allowed = lax.broadcasted_iota(jnp.int32, (ROWS, seen), 1) <= row
        for h in range(4):
            at_h = slice(h * HEAD_DIM, (h + 1) * HEAD_DIM)
            s = dot_nt(q_ref[half, :, at_h], k_ref[:seen, at_h]) * HEAD_DIM**-0.5
            s = jnp.where(allowed, s, MASKED)
            e = jnp.exp(s - jnp.max(s, axis=-1, keepdims=True))
            p = (e / jnp.sum(e, axis=-1, keepdims=True)).astype(BF)
            p_ref[half, h, :, :seen] = p
            o_ref[half, :, at_h] = dot(p, v_ref[:seen, at_h]).astype(BF)
        leave(used(p_ref, half), used(p_out, half), 3, half)
        leave(o_ref.at[half], o_out.at[half], 4, half)
        o = o_ref[half]
        for side in range(2):
            part_ref[half, :, side * HALF : (side + 1) * HALF] = dot(o, w.out(side)).astype(BF)
    for copy in leaving:
        copy.wait()


KEPT = [
    pltpu.VMEM((2, ROWS, HALF), BF), pltpu.VMEM((2 * ROWS, HALF), BF), pltpu.VMEM((2 * ROWS, HALF), BF),
    pltpu.VMEM((2, ROWS, HALF), BF), pltpu.VMEM((2, 4, ROWS, 2 * ROWS), BF), pltpu.SemaphoreType.DMA((5, 2)),
]


def attention(info, u, own, sib, full):
    return pl.pallas_call(
        attn_kernel,
        out_shape=(
            sds((2, ROWS, 1024), BF), sds((2, ROWS, HALF), BF), sds((2 * ROWS, HALF), BF),
            sds((2 * ROWS, HALF), BF), sds((2, ROWS, HALF), BF), sds((2, 4, ROWS, 2 * ROWS), BF),
        ),
        in_specs=[SMEM] + [HBM] * 4,
        out_specs=(FULL, HBM, HBM, HBM, HBM, HBM),
        scratch_shapes=KEPT + WEIGHTS + INPUTS,
        compiler_params=params(BIG),
        cost_estimate=cost(4_000_000_000, 16_000_000),
        name="attention",
    )(info, u, own, sib, full)


def attn_back_kernel(
    info, own_in, sib_in, mid_in, dy_in, gain_ref, full_ref, q_in, k_in, v_in, o_in, p_in,
    os_in, u_in, so_in, ss_in, held_ref, dm_out, g_ref, dq_out, dk_out, dv_out, grad_ref,
    q_ref, k_ref, v_ref, o_ref, p_ref, in_sems, w_s, sems, grads, out_sems,
    u_ref, s_own, s_sib, late_sems, os_ref, own_ref, sib_ref, mid_ref, dy_ref, dm_ref, first_sems,
    dq_ref, dk_ref, dv_ref, made_sems,
):
    del held_ref
    early = []
    for lane in range(2):
        pairs = ((own_in, own_ref), (sib_in, sib_ref), (mid_in, mid_ref), (dy_in, dy_ref))
        early.append(bring([(a.at[lane], b.at[lane]) for a, b in pairs], first_sems.at[lane]))
    w = Weights(info, full_ref, w_s, sems)
    w.start((3,))
    pairs = ((v_in, v_ref), (k_in, k_ref), (q_in, q_ref), (o_in, o_ref))
    pairs += tuple((used(p_in, half), used(p_ref, half)) for half in range(2))
    arriving = bring(pairs, [in_sems.at[n, 0] for n in range(5)] + [in_sems.at[0, 1]])
    me, it = info[0], 1 - info[0]
    scale = HEAD_DIM**-0.5
    gain_grad = jnp.zeros((1, 1024), F32)
    branches = []
    leaving = []

    def leave(src, dst, sem):
        copy = pltpu.make_async_copy(src, dst, sem)
        copy.start()
        leaving.append(copy)

    for lane in range(2):
        for copy in early[lane]:
            copy.wait()
        if lane == 1:
            late = bring(((u_in, u_ref), (so_in, s_own), (ss_in, s_sib), (os_in, os_ref)), late_sems)
        m = mid_ref[lane]
        dz = added(own_ref[lane], sib_ref[lane])
        inverse = rms_scale(m)
        unit = m * inverse
        gain_grad = gain_grad + jnp.sum(dz * unit, axis=0, keepdims=True)
        scaled = dz * gain_ref[...]
        dm = dy_ref[lane].astype(F32) + inverse * (
            scaled - unit * jnp.mean(scaled * unit, axis=-1, keepdims=True)
        )
        dm_ref[lane] = dm
        own_rows = pl.ds(pl.multiple_of(info[0] * 128, 128), 128)
        leave(dm_ref.at[lane, own_rows], dm_out.at[lane], made_sems.at[0, lane])
        branch = (live_of(info, lane) * dm).astype(BF)
        branches.append(branch)
    g_ref[...] = gain_grad
    w.wait(3)
    for copy in arriving:
        copy.wait()
    d_o = []
    for half in range(2):
        branch = branches[half]
        d_o.append((dot_nt(branch[:, :HALF], w.out(0)) + dot_nt(branch[:, HALF:], w.out(1))).astype(BF))
    for h in range(4):
        at_h = slice(h * HEAD_DIM, (h + 1) * HEAD_DIM)
        dk, dv = [], []
        for half in range(2):
            seen = ROWS * (half + 1)
            p_low = p_ref[half, h, :, :seen]
            p = p_low.astype(F32)
            d_o_h = d_o[half][:, at_h]
            dp = dot_nt(d_o_h, v_ref[:seen, at_h])
            total = jnp.sum(p * dp, axis=-1, keepdims=True)
            ds = (p * (dp - total)).astype(BF)
            dq_ref[half, :, at_h] = (dot(ds, k_ref[:seen, at_h]) * scale).astype(BF)
            dk.append(dot_tn(ds, q_ref[half, :, at_h]))
            dv.append(dot_tn(p_low, d_o_h))
        for ref, parts, factor in ((dk_ref, dk, scale), (dv_ref, dv, 1.0)):
            ref[:ROWS, at_h] = ((parts[0] + parts[1][:ROWS]) * factor).astype(BF)
            ref[ROWS:, at_h] = (parts[1][ROWS:] * factor).astype(BF)
    for n, (src, dst) in enumerate(((dq_ref, dq_out), (dk_ref, dk_out), (dv_ref, dv_out))):
        leave(src, dst, made_sems.at[1 + n, 0])

    def leave_grad(n):
        at_r = pl.ds(pl.multiple_of(info[8 + n // 2], 32), 32)
        at_c = pl.ds(HALF * (n % 2), HALF)
        for y in range(2):
            leave(grads.at[n, y], grad_ref.at[:, y ^ info[3], at_r, at_c], out_sems.at[n, y])

    def put(n, half, value):
        grads[n, pl.ds(half, 1)] = value.astype(BF).reshape(1, 16, 32, HALF)

    for copy in late:
        copy.wait()
    branch = jnp.concatenate(branches, axis=0)
    branch = jnp.where(info[0] == 0, branch[:, :HALF], branch[:, HALF:])
    for half, ref in ((me, o_ref), (it, os_ref)):
        put(3, half, dot_tn(wide(ref[...]), branch))
    leave_grad(3)
    for n, ref in ((1, dk_ref), (2, dv_ref)):
        for half, s_c in ((me, s_own), (it, s_sib)):
            put(n, half, dot_tn(s_c[...], ref[...]))
        leave_grad(n)
    for half in range(2):
        put(0, half, dot_tn(wide(u_ref[...])[:, half * HALF : (half + 1) * HALF], wide(dq_ref[...])))
    leave_grad(0)
    for copy in leaving:
        copy.wait()


def attention_back(info, own, sib, mid, dy, gain, full, q, k, v, o, p, o_sib, u, s_own, s_sib, held):
    return pl.pallas_call(
        attn_back_kernel,
        out_shape=(
            sds((2, 128, 1024), F32), sds((1, 1024), F32), sds((2, ROWS, HALF), BF),
            sds((2 * ROWS, HALF), BF), sds((2 * ROWS, HALF), BF), sds(held.shape, BF),
        ),
        in_specs=[SMEM] + [HBM] * 4 + [FULL] + [HBM] * 11,
        out_specs=(HBM, FULL, HBM, HBM, HBM, HBM),
        input_output_aliases={16: 5},
        scratch_shapes=KEPT + WEIGHTS + WEIGHTS + INPUTS + [
            pltpu.VMEM((2, ROWS, HALF), BF), pltpu.VMEM((2, ROWS, 1024), BF), pltpu.VMEM((2, ROWS, 1024), BF),
            pltpu.VMEM((2, ROWS, 1024), F32), pltpu.VMEM((2, ROWS, 1024), BF), pltpu.VMEM((2, ROWS, 1024), F32),
            pltpu.SemaphoreType.DMA((2, 4)),
            pltpu.VMEM((2, ROWS, HALF), BF), pltpu.VMEM((2 * ROWS, HALF), BF), pltpu.VMEM((2 * ROWS, HALF), BF),
            pltpu.SemaphoreType.DMA((4, 2)),
        ],
        compiler_params=params(BIG),
        cost_estimate=cost(6_000_000_000, 24_000_000),
        name="attention_back",
    )(info, own, sib, mid, dy, gain, full, q, k, v, o, p, o_sib, u, s_own, s_sib, held)


def inputs_back_kernel(
    info, dq_in, dk_in, dv_in, full_ref, keep_ref, send_ref, w_s, sems, dq_ref, dk_ref, dv_ref, in_sems
):
    w = Weights(info, full_ref, w_s, sems)
    w.start((1, 2))
    arriving = bring(((dk_in, dk_ref), (dv_in, dv_ref), (dq_in, dq_ref)), in_sems)
    w.start((0,))
    for copy in arriving:
        copy.wait()
    for n in (1, 2):
        w.wait(n)
    for ref, half in ((send_ref, 1 - info[0]), (keep_ref, info[0])):
        ds = dot_nt(dk_ref[...], w.half(1, half)) + dot_nt(dv_ref[...], w.half(2, half))
        ref[0] = ds.astype(BF).reshape(2, ROWS, HALF)
    w.wait(0)
    for ref, half in ((send_ref, 1 - info[0]), (keep_ref, info[0])):
        ref[1] = dot_nt(wide(dq_ref[...]), w.half(0, half)).astype(BF).reshape(2, ROWS, HALF)


def inputs_back(info, dq, dk, dv, full):
    return pl.pallas_call(
        inputs_back_kernel,
        out_shape=(sds((2, 2, ROWS, HALF), BF), sds((2, 2, ROWS, HALF), BF)),
        in_specs=[SMEM] + [HBM] * 4,
        scratch_shapes=WEIGHTS + [
            pltpu.VMEM((2, ROWS, HALF), BF), pltpu.VMEM((2 * ROWS, HALF), BF), pltpu.VMEM((2 * ROWS, HALF), BF),
            pltpu.SemaphoreType.DMA((3,)),
        ],
        compiler_params=params(BIG),
        cost_estimate=cost(2_000_000_000, 7_000_000),
        name="inputs_back",
    )(info, dq, dk, dv, full)


GELU_C = 0.7978845608028654
GELU_K = 0.044715


def ffn_kernel(
    info, x_ref, part_ref, sib_ref, gain_ref, d_ref, up_ref, down_ref,
    mid_out, dz_ref, hidden_ref, grad_ref, z_s, dz_s, gu_s, gd_s, sems, mid_ref, mid_sems,
):
    step = pl.program_id(0)

    def mid_copy(k):
        return pltpu.make_async_copy(mid_ref.at[k], mid_out.at[k], mid_sems.at[k])

    slot = step % 2
    place, near = step % 2, step // 2
    side = near ^ info[3]

    def copies(slot, place, near):
        at_c = pl.ds(pl.multiple_of(place * HALF, HALF), HALF)
        at_r = pl.ds(pl.multiple_of(info[5 + (near ^ info[3])], 32), 32)
        at_z = pl.ds(place * 8, 8)
        made = [pltpu.make_async_copy(gu_s.at[slot], grad_ref.at[:, :, at_r, at_c], sems.at[0, slot])]
        for k in range(2):
            at_r = pl.ds(pl.multiple_of(info[7 + 3 * k], 32), 32)
            src = gd_s.at[slot, :, pl.ds(32 * k, 32), :]
            made.append(pltpu.make_async_copy(src, grad_ref.at[at_z, near, at_r, :], sems.at[1 + k, slot]))
        return made

    @pl.when(step == 0)
    def _():
        for lane in range(2):
            live = live_of(info, lane)
            m = x_ref[lane].astype(F32) + live * added(part_ref[lane], sib_ref[lane])
            mid_ref[lane] = m
            mid_copy(lane).start()
            z_s[lane * ROWS : (lane + 1) * ROWS] = (m * rms_scale(m) * gain_ref[...]).astype(BF)
        dz_s[...] = jnp.zeros_like(dz_s)

    z, d = z_s[...], d_ref[...]
    down = wide(down_ref[:, 0])
    up_0, up_1 = (up_ref[:, pl.ds(y ^ info[3], 1)].reshape(HALF, HALF) for y in range(2))
    f = dot(z[:, :HALF], up_0) + dot(z[:, HALF:], up_1)
    square = f * f
    h = 0.5 + 0.5 * jnp.tanh(GELU_C * f + (GELU_C * GELU_K) * f * square)
    hidden = (f * h).astype(BF)
    slope = h + (h - h * h) * (2.0 * GELU_C * f + (6.0 * GELU_C * GELU_K) * f * square)
    hidden_ref[...] = hidden
    back = (slope * dot_nt(d, down)).astype(BF)

    @pl.when(step >= 2)
    def _():
        for c in copies(slot, place, near):
            c.wait()

    gd_s[slot] = dot_tn(hidden, d).astype(BF).reshape(8, 64, 1024)
    gu = dot_tn(z, back).astype(BF).reshape(2, 16, 32, HALF)
    for y in range(2):
        gu_s[slot, :, pl.ds(y ^ info[3], 1)] = gu[y].reshape(16, 1, 32, HALF)
    for c in copies(slot, place, near):
        c.start()
    dz_s[:, :HALF] += dot_nt(back, up_0)
    dz_s[:, HALF:] += dot_nt(back, up_1)

    @pl.when(step == pl.num_programs(0) - 1)
    def _():
        for lane in range(2):
            dz_ref[lane] = dz_s[lane * ROWS : (lane + 1) * ROWS].astype(BF)
            mid_copy(lane).wait()
        for k in range(2):
            for c in copies(k, place, near):
                c.wait()


def feed_forward(info, x, part, sib, gain, d, weights):
    chunk = pl.BlockSpec((2 * ROWS, HALF), lambda i, info: (0, i))
    return pl.pallas_call(
        ffn_kernel,
        grid_spec=pltpu.PrefetchScalarGridSpec(
            num_scalar_prefetch=1,
            grid=(4,),
            in_specs=[
                FULL, FULL, FULL, FULL, FULL,
                pl.BlockSpec((16, 2, 32, HALF), lambda i, info: (0, 0, (i // 2) ^ info[3], i % 2)),
                pl.BlockSpec((8, 1, 64, 1024), lambda i, info: (i % 2, i // 2, 1, 0)),
            ],
            out_specs=(HBM, FULL, chunk, HBM),
            scratch_shapes=[
                pltpu.VMEM((2 * ROWS, 1024), BF), pltpu.VMEM((2 * ROWS, 1024), F32),
                pltpu.VMEM((2, 16, 2, 32, HALF), BF), pltpu.VMEM((2, 8, 64, 1024), BF),
                pltpu.SemaphoreType.DMA((3, 2)),
                pltpu.VMEM((2, ROWS, 1024), F32), pltpu.SemaphoreType.DMA((2,)),
            ],
        ),
        out_shape=(
            sds((2, ROWS, 1024), F32), sds((2, ROWS, 1024), BF), sds((2 * ROWS, 2048), BF),
            sds((16, 2, 192, 1024), BF),
        ),
        compiler_params=params(BIG),
        cost_estimate=cost(9_000_000_000, 28_000_000),
        name="feed_forward",
    )(info, x, part, sib, gain, d, weights, weights)


DOWN = pl.BlockSpec((8, 1, 64, 1024), lambda i: (i % 2, i // 2, 1, 0))
CHUNK = pl.BlockSpec((2 * ROWS, HALF), lambda i: (0, i))


def hidden_out_kernel(info, hidden_ref, mid_ref, down_ref, keep_ref, send_ref, out_s):
    step = pl.program_id(0)
    more = dot(hidden_ref[...], wide(down_ref[:, 0]))

    @pl.when(step == 0)
    def _():
        out_s[...] = more

    @pl.when(step > 0)
    def _():
        out_s[...] += more

    @pl.when(step == pl.num_programs(0) - 1)
    def _():
        for half in range(2):
            out = live_of(info, half) * out_s[half * ROWS : (half + 1) * ROWS]
            total = out + mid_ref[half]
            keep_ref[half] = jnp.where(info[0] == 0, total[:128], total[128:])
            send_ref[half] = jnp.where(info[0] == 0, out[128:], out[:128]).astype(BF)


def hidden_out(info, hidden, mid, weights):
    return pl.pallas_call(
        hidden_out_kernel,
        grid=(4,),
        out_shape=(sds((2, 128, 1024), F32), sds((2, 128, 1024), BF)),
        in_specs=[SMEM, CHUNK, FULL, DOWN],
        out_specs=(FULL, FULL),
        scratch_shapes=[pltpu.VMEM((2 * ROWS, 1024), F32)],
        compiler_params=params(BIG),
        cost_estimate=cost(2_100_000_000, 8_000_000),
        name="hidden_out",
    )(info, hidden, mid, weights)


STEPS = (("x", "c"), ("z", "a"), ("z", "b"), ("y", "a"))


def carry(ends, far, rate, block, lane, reverse, between=None):
    low, high = ends[:, :4], ends[:, 4:]
    far, rate = far[:, :4], rate[:, :4]
    first, second = (high, low) if reverse else (low, high)
    total = far * first + second
    entering = jnp.zeros_like(total)
    for k, (axis, kind) in enumerate(STEPS):
        if between is not None:
            total = between(k, total)
        other = flip(total, axis, kind)
        upper = (block >> k) & 1
        within = block & ((1 << k) - 1)
        if reverse:
            takes, gap = upper == 0, (1 << k) - 1 - within
        else:
            takes, gap = upper == 1, within
        reach = jnp.exp(-rate * (BLOCK * gap).astype(F32)) * other
        whole = jnp.exp(-rate * float(BLOCK << k))
        joined = whole * jnp.where(takes, other, total) + jnp.where(takes, total, other)
        if k >= 2:
            reach = jnp.where(lane == 1, 0.0, reach)
            joined = jnp.where(lane == 1, 0.0, joined)
        entering = entering + jnp.where(takes, reach, 0.0)
        total = joined
    inner = first + far * entering
    return jnp.concatenate([inner, entering] if reverse else [entering, inner], axis=1)


def adam(factor, w_ref, f_ref, s_ref, grad, outs, rate, decay):
    clipped = grad * factor
    first_new = BETA_ONE * f_ref[...] + (1.0 - BETA_ONE) * clipped
    second_new = BETA_TWO * s_ref[...] + (1.0 - BETA_TWO) * clipped * clipped
    fix_one = 1.0 - BETA_ONE**STEP
    fix_two = 1.0 - BETA_TWO**STEP
    direction = first_new / fix_one / (jnp.sqrt(second_new / fix_two) + ADAM_EPS)
    weight = w_ref[...]
    weight_new = weight - rate * (direction + decay * weight)
    for ref, v in zip(outs, (first_new, second_new, weight_new, weight_new.astype(BF))):
        ref[...] = v


def finish_kernel(info, mine, near, over, cross, state, gain, own_ref, give_ref, squares_ref):
    total = added(mine[...], near[...]) + added(over[...], cross[...])
    squares = jnp.sum(total * total, axis=0, keepdims=True)
    squares = jnp.sum(squares.reshape(1, 8, 128), axis=1)
    squares = jnp.sum(squares, axis=1, keepdims=True)
    for ref in (state, gain):
        piece = ref[...].reshape(-1, 16)
        piece = jnp.sum(piece * piece, axis=0, keepdims=True)
        squares = squares + 0.5 * jnp.sum(piece, axis=1, keepdims=True)
    squares_ref[...] = jnp.broadcast_to(squares, (64, 128))
    own_ref[32:] = total[64:]
    for k in range(2):
        low, high = total[32 * k : 32 * k + 16], total[32 * k + 16 : 32 * k + 32]
        own_ref[16 * k : 16 * k + 16] = jnp.where(info[0] == 0, low, high)
        give_ref[16 * k : 16 * k + 16] = jnp.where(info[0] == 0, high, low)


def finish(info, mine, near, over, cross, state, gain):
    return pl.pallas_call(
        finish_kernel,
        out_shape=(sds((64, 1024), F32), sds((32, 1024), F32), sds((64, 128), F32)),
        in_specs=[SMEM] + [FULL] * 6,
        compiler_params=params(),
        cost_estimate=cost(2_000_000, 3_000_000),
        name="finish",
    )(info, mine, near, over, cross, state, gain)


def update_kernel(info, *refs):
    ins, outs = refs[:22], refs[22:]
    weights, firsts, seconds = ins[:5], ins[5:10], ins[10:15]
    every, mine, got, mine_far, got_far, state, gain = ins[15:]
    norm = jnp.sqrt(jnp.sum(every[...], axis=0, keepdims=True)[:, :1])
    outs[20][...] = norm
    factor = jnp.minimum(1.0, CLIP_NORM / norm)
    zero = info[0] == 0
    here = info[11] == 0

    def pair(one, two):
        first, second = jnp.where(zero, one, two), jnp.where(zero, two, one)
        return first.reshape(2, 16, 1024), second.reshape(2, 16, 1024)

    down = jnp.concatenate(
        [jnp.where(here, mine[32:], mine_far[32:]), jnp.where(here, mine_far[32:], mine[32:])], axis=0
    )
    near, far = pair(mine[:32], got[...]), pair(mine_far[:32], got_far[...])
    first, second = (jnp.where(here, b, a) for a, b in zip(near, far))
    matrices = []
    for n in range(4):
        at_c = slice(HALF * (n % 2), HALF * (n % 2) + HALF)
        matrices.append(jnp.concatenate([first[n // 2, :, at_c], second[n // 2, :, at_c]], axis=1))
    attn_grad = jnp.stack(matrices)
    first, second = (jnp.where(here, a, b) for a, b in zip(near, far))
    pieces = []
    for side in range(2):
        for k in range(16):
            at_c = slice(64 * k, 64 * k + 64)
            pieces += [first[side, :, at_c], second[side, :, at_c]]
    up_grad = jnp.concatenate(pieces, axis=1)
    grads = (attn_grad, up_grad, down, state[...], gain[...])
    rates = ((RATE_MATRIX, WEIGHT_DECAY),) * 3 + ((RATE_STATE, 0.0), (RATE_GAIN, 0.0))
    for k in range(5):
        adam(factor, weights[k], firsts[k], seconds[k], grads[k], outs[4 * k : 4 * k + 4], *rates[k])


def update(info, weights, firsts, seconds, grads):
    shapes = []
    for w in weights:
        shapes += [sds(w.shape, F32)] * 3 + [sds(w.shape, BF)]
    return pl.pallas_call(
        update_kernel,
        out_shape=tuple(shapes) + (sds((1, 1), F32),),
        in_specs=[SMEM] + [FULL] * 22,
        compiler_params=pltpu.CompilerParams(vmem_limit_bytes=24 * 1024 * 1024),
        cost_estimate=cost(4_000_000, 6_000_000),
        name="update",
    )(info, *weights, *firsts, *seconds, *grads)


def body(
    tokens, cotangent, lengths, attn_weight, up_weight, down_weight, state_param, norm_gain,
    attn_first, attn_second, up_first, up_second, down_first, down_second,
    state_first, state_second, gain_first, gain_second,
):
    core = lax.axis_index("core")
    ybit = lax.axis_index("y")
    chip = (ybit * 4 + lax.axis_index("z")) * 4 + lax.axis_index("x")

    lane = chip % 2
    block = chip // 2

    def of_lane(v, which):
        return lax.dynamic_index_in_dim(v, which, 0, keepdims=False)

    def halves(mine, got):
        return jnp.stack([jnp.where(lane == 0, mine, got), jnp.where(lane == 0, got, mine)])

    x_give, dy_give = of_lane(tokens[0], 1 - lane), of_lane(cotangent[0], 1 - lane)
    x_got, dy_got = flip(x_give, "x"), flip(dy_give, "x")

    mine = jnp.concatenate(
        [state_param.astype(BF).transpose(0, 2, 1).reshape(-1), norm_gain.astype(BF).reshape(-1)]
    )
    mine = jnp.pad(mine, (0, 1024 - mine.shape[0])).reshape(1, 8, 128)
    pair = ordered(core, mine, swap(mine), 0)
    small = lax.all_to_all(
        jnp.broadcast_to(pair[None], (32, 2, 8, 128)), CHIPS, split_axis=0, concat_axis=0, tiled=True
    ).reshape(64, 1024)
    theta = small[:, :768].reshape(64, 3, NST, 16).transpose(1, 2, 0, 3).reshape(3, NST, 1024).astype(F32)
    gains = small[:, 768:800].reshape(64, 2, 16).transpose(1, 0, 2).reshape(2, 1024).astype(F32)

    slot_blocks = SLOT // BLOCK
    live_len = lax.dynamic_index_in_dim(lengths[0], block // slot_blocks, 0, keepdims=False)
    live_rows = jnp.clip(live_len - (block % slot_blocks) * BLOCK, 0, BLOCK)
    live_rows = jnp.where(lane == 0, BLOCK, live_rows)
    group = lax.axis_index("grp")
    places = [((b + 3 * group) % 6) * 32 for b in range(6)]
    info = jnp.stack([core, live_rows, lane, ybit, chip] + places + [group]).astype(jnp.int32)

    attn_low = attn_weight.astype(BF)
    up_low = up_weight.astype(BF).reshape(16, 32, 2, 64).transpose(2, 0, 1, 3).reshape(2, 16, 2048)
    down_low = down_weight.astype(BF)
    qkv_keep = lax.dynamic_slice_in_dim(attn_low[:3], core * HALF, HALF, 2)
    qkv_give = lax.dynamic_slice_in_dim(attn_low[:3], (1 - core) * HALF, HALF, 2)
    qkv_chip = ordered(core, qkv_keep, swap(qkv_give), 1)
    out_chip = ordered(core, attn_low[3], swap(attn_low[3]), 0)
    up_keep = lax.dynamic_index_in_dim(up_low, core, 0, keepdims=False)
    up_give = lax.dynamic_index_in_dim(up_low, 1 - core, 0, keepdims=False)
    up_chip = ordered(core, up_keep, swap(up_give), 0)
    up_chip = up_chip.reshape(32, 2, 1024).transpose(1, 0, 2).reshape(64, 1024)
    qk_rows = jnp.concatenate([qkv_chip[0], qkv_chip[1]], axis=1)
    own_rows = jnp.concatenate([up_chip, down_low, qk_rows], axis=0)
    across = [(0, 3), (3, 0), (1, 2), (2, 1)]
    low = jnp.concatenate([own_rows[:96], out_chip[:, :HALF].reshape(16, 1024)], axis=0)
    high = jnp.concatenate([own_rows[96:], jnp.concatenate([qkv_chip[2], out_chip[:, HALF:]], axis=1)], axis=0)
    low, high, pair = lax.optimization_barrier((low, high, pair))
    low_got, high_got = flip(low, "y"), lax.ppermute(high, ("grp", "y"), across)
    out_got = jnp.concatenate([low_got[96:].reshape(32, HALF), high_got[64:, HALF:]], axis=1)
    out_rows = jnp.where(ybit == core, out_chip, out_got)
    own_last = jnp.concatenate([qkv_chip[2], out_rows[:, :HALF]], axis=1)
    other_last = jnp.concatenate([high_got[64:, :HALF], out_rows[:, HALF:]], axis=1)
    all_two = jnp.concatenate([own_rows, own_last, low_got[:96], high_got[:64], other_last], axis=0)
    all_two, x_got, dy_got = lax.optimization_barrier((all_two, x_got, dy_got))
    full = lax.all_gather(all_two.reshape(2, 192, 1024), ("z", "x"), axis=0)
    x_own, dy_own = (halves(of_lane(v[0], lane), got) for v, got in ((tokens, x_got), (cotangent, dy_got)))
    x = ordered(core, x_own, swap(x_own), 1)
    dy = ordered(core, dy_own, swap(dy_own), 1)

    theta_c = lax.dynamic_slice_in_dim(theta, core * HALF, HALF, 2).reshape(3, NST, 4, 128)
    theta_c = jnp.concatenate([theta_c, theta_c], axis=2)
    rate = jnp.exp(theta_c[0]) / BLOCK
    decay = jnp.exp(-rate)
    norm_scale = jnp.sqrt(-jnp.expm1(-2.0 * rate))
    cb = norm_scale * theta_c[1] * theta_c[2]
    far = jnp.exp(-rate * float(ROWS))
    gain_c = lax.dynamic_slice_in_dim(gains[0], core * HALF, HALF, 0).reshape(4, 128)
    gain_c = jnp.concatenate([gain_c, gain_c], axis=0)

    u_low, us, ended, ramp = first(info, x, gains[:1], decay)
    entering = carry(ended, far, rate, block, lane, False)
    d_low = jnp.where((lax.iota(jnp.int32, BLOCK) < live_rows).reshape(2, ROWS, 1), dy, jnp.zeros((), BF))
    entering, dy, d_low = lax.optimization_barrier((entering, dy, d_low.reshape(2 * ROWS, 1024)))
    sb_own = state_run(us, decay, cb * gain_c, entering).reshape(2 * ROWS, HALF)
    sb_sib = swap(sb_own)

    part, q, k, v, o, p = attention(info, u_low, sb_own, sb_sib, full)
    part_sib, o_sib = swap(part), swap(o)
    middle, dz_part, hidden, ffn_grad = feed_forward(info, x, part, part_sib, gains[1:], d_low, full)
    dz_part, o_sib = lax.optimization_barrier((dz_part, o_sib))
    dm, gain_two_grad, dq, dk, dv, grad = attention_back(
        info, dz_part, swap(dz_part), middle, dy, gains[1:], full, q, k, v, o, p,
        o_sib, u_low, sb_own, sb_sib, ffn_grad,
    )
    grad_part = lax.psum_scatter(grad.reshape(6144, 1024), ("z", "x"), scatter_dimension=0, tiled=True)
    keep, send = inputs_back(info, dq, dk, dv, full)
    got = swap(send)
    ds, started = state_turn(keep, got, decay)
    mids = {}

    def before(k, total):
        if k == 2:
            made = state_mid(us, ds, decay, cb, entering, keep, got)
            total, *mids["first"] = lax.optimization_barrier((total,) + tuple(made))
        if k == 3:
            made = state_mid_more(us, ds, decay, cb, entering, mids["first"][0])
            total, *mids["second"] = lax.optimization_barrier((total,) + tuple(made))
        return total

    leaving = carry(started, far, rate, block, lane, True, before)
    _, qu_0, r_0, gain_q = mids["first"]
    dus, qu_1, r_1 = mids["second"]
    qu, rr = (qu_0, qu_1), (r_0, r_1)
    lanes = state_fix(
        info, leaving, decay, cb, ended, ramp, entering, far, qu, rr, gain_q, gains[:1], gain_two_grad
    )
    du_mine, du_give = state_last(info, dus, decay, cb, leaving)

    out_keep, out_send = hidden_out(info, hidden, middle, full)
    out_own = (out_keep + swap(out_send).astype(F32)).astype(BF)

    du_own = ordered(core, du_mine, swap(du_give), 2)
    x_own = x_own.astype(F32)
    grad_own = (norm_back(du_own, x_own, rms_scale(x_own), gains[0]) + dm).astype(BF)

    packed = lanes.reshape(34, 32, 16).transpose(1, 0, 2)
    small_got = lax.all_to_all(packed, CHIPS, split_axis=0, concat_axis=0, tiled=True)
    small_sum = jnp.sum(small_got, axis=0)
    small_sum = small_sum + flip(small_sum, "grp")
    hand = []
    for j in range(32):
        for c in range(2):
            hand.append((j * 2 + c, c * 32 + j))
    mine_sum = lax.ppermute(small_sum, SHARD, hand)

    t_own = state_param.astype(BF).astype(F32).transpose(0, 2, 1)
    rate_o = jnp.exp(t_own[0]) / BLOCK
    decay_o = jnp.exp(-rate_o)
    scale_o = jnp.sqrt(-jnp.expm1(-2.0 * rate_o))
    b_o = scale_o * t_own[1]
    qu_o, rr_o = mine_sum[:NST], mine_sum[NST : 2 * NST]
    gb = t_own[2] * qu_o
    log_rate_grad = rate_o * (
        -decay_o * t_own[2] * b_o * rr_o + decay_o * decay_o / scale_o * t_own[1] * gb
    )
    state_grad = jnp.stack([log_rate_grad, scale_o * gb, b_o * qu_o]).transpose(0, 2, 1)
    gain_grad = mine_sum[2 * NST :]

    mine = [of_lane(v, lane) for v in (out_own, grad_own)]
    give = jnp.stack([of_lane(v, 1 - lane) for v in (out_own, grad_own)])
    grad_part, state_grad, gain_grad, give, *mine = lax.optimization_barrier(
        (grad_part, state_grad, gain_grad, give, *mine)
    )
    traded = flip(give, "x")
    output, token_grad = (halves(a, b) for a, b in zip(mine, traded))
    here, there, give_here, give_there = (grad_part[96 * k : 96 * k + 96] for k in range(4))
    own, give, squares = finish(
        info, here, flip(give_here, "y"), flip(there, "grp"), lax.ppermute(give_there, ("grp", "y"), across),
        state_grad, gain_grad,
    )
    squares, own, got = lax.optimization_barrier((squares + swap(squares), own, swap(give)))
    every = lax.all_to_all(squares, ("grp",) + CHIPS, split_axis=0, concat_axis=0, tiled=True)
    new = update(
        info,
        (attn_weight, up_weight, down_weight, state_param, norm_gain),
        (attn_first, up_first, down_first, state_first, gain_first),
        (attn_second, up_second, down_second, state_second, gain_second),
        (every, own, got, flip(own, "grp"), flip(got, "grp"), state_grad, gain_grad),
    )
    return (output[None], token_grad[None], new[20][0, 0]) + tuple(new[:20])


def solution(mesh):
    inner = Mesh(mesh.devices.reshape(2, 2, 4, 4, 2), AXES)
    rows = P("grp", None, SHARD, None)
    attn = P(None, SHARD, None)
    flat = P(SHARD, None)
    gain = P(None, SHARD)
    in_specs = (rows, rows, P("grp", None), attn, flat, flat, attn, gain)
    in_specs += (attn, attn, flat, flat, flat, flat, attn, attn, gain, gain)
    out_specs = (rows, rows, P()) + (attn,) * 4 + (flat,) * 8 + (attn,) * 4 + (gain,) * 4
    return jax.shard_map(body, mesh=inner, in_specs=in_specs, out_specs=out_specs, check_vma=False)
```
